128 devices in a mesh: row: 16 (over y_hi, x, core), col: 8 (over y_lo, z).
Axes of the slice: x: 4, y: 4 (y_hi: 2, y_lo: 2; y = y_hi * 2 + y_lo), z: 4, core: 2. Of those that a mesh axis runs over, the one named last changes fastest.
Arguments:
- tokens: bfloat16 [16384, 2048], P('row', 'col'), may hold values from -6 to 6
- cotangent: bfloat16 [16384, 2048], P('row', 'col'), may hold values from -6 to 6
- routes: int32 [16384, 8], P('row'), may hold values from 0 to 15, all different within a row; in each aligned block of 1024 rows (0 to 1023, 1024 to 2047, ...) at most 544 rows name the same one
- adapter_set: int32 [16], P('row'), may hold values from 0 to 7
- attn_gain: float32 [2048], replicated, may hold values from 0.5 to 1.5
- mixer_gain: float32 [2048], replicated, may hold values from 0.5 to 1.5
- query_gain: float32 [2048], P('col'), may hold values from 0.5 to 1.5
- key_gain: float32 [2048], P('col'), may hold values from 0.5 to 1.5
- qkv_weight: bfloat16 [3, 2048, 2048], P(None, 'row', 'col'), may hold values from -0.125 to 0.125
- qkv_down: bfloat16 [3, 2048, 128], P(None, 'row'), may hold values from -0.125 to 0.125
- qkv_up: bfloat16 [3, 128, 2048], P(None, None, 'col'), may hold values from -0.5 to 0.5
- out_weight: bfloat16 [2048, 2048], P('col', 'row'), may hold values from -0.375 to 0.375
- out_down: bfloat16 [2048, 128], P('col'), may hold values from -0.375 to 0.375
- out_up: bfloat16 [128, 2048], P(None, 'col'), may hold values from -0.5 to 0.5
- router_weight: bfloat16 [2048, 16], P('row'), may hold values from -0.0625 to 0.0625
- router_down: bfloat16 [2048, 128], P('row'), may hold values from -0.125 to 0.125
- router_up: bfloat16 [128, 16], replicated, may hold values from -0.25 to 0.25
- expert_in: bfloat16 [16, 2, 2048, 1024], P('col', None, 'row'), may hold values from -0.125 to 0.125
- expert_in_down: bfloat16 [16, 2, 2048, 128], P('col', None, 'row'), may hold values from -0.125 to 0.125
- expert_in_up: bfloat16 [16, 2, 128, 1024], P('col'), may hold values from -0.5 to 0.5
- expert_out: bfloat16 [16, 1024, 2048], P('col', None, 'row'), may hold values from -0.75 to 0.75
- expert_out_down: bfloat16 [16, 1024, 128], P('col'), may hold values from -0.1875 to 0.1875
- expert_out_up: bfloat16 [16, 128, 2048], P('col', None, 'row'), may hold values from -2 to 2
Outputs:
- mixed: bfloat16 [16384, 2048], P('row', 'col')
- tokens_grad: float32 [16384, 2048], P('row', 'col')
- qkv_down_grad: float32 [3, 2048, 128], P(None, 'row')
- qkv_up_grad: float32 [3, 128, 2048], P(None, None, 'col')
- out_down_grad: float32 [2048, 128], P('col')
- out_up_grad: float32 [128, 2048], P(None, 'col')
- router_down_grad: float32 [2048, 128], P('row')
- router_up_grad: float32 [128, 16], replicated
- expert_in_down_grad: float32 [16, 2, 2048, 128], P('col', None, 'row')
- expert_in_up_grad: float32 [16, 2, 128, 1024], P('col')
- expert_out_down_grad: float32 [16, 1024, 128], P('col')
- expert_out_up_grad: float32 [16, 128, 2048], P('col', None, 'row')
The draws below stay inside these ranges and needn't reach their ends.
Inputs may be any that keep to these rules, and one draw needn't show every extreme that they name: `routes`: each row names 8 different experts; within the rows of one sequence (aligned blocks of 1024 rows) no expert is named by more than 544 rows, and in every draw some expert of some sequence is named by exactly 544.
All inputs are finite; a program needn't handle non-finite values.
Results may differ from the reference program's by a relative error of at most 0.024.
Values may be sent and summed in bfloat16 or wider, within the bound.
A program may use at most 448 MiB of HBM per device.

```python
import math
import jax
import jax.numpy as jnp
import numpy as np
from jax import lax

MODEL_WIDTH = 2048
HEADS = 16
HEAD_DIM = 128
FF = 1024
EXPERTS = 16
TOP = 8
RANK = 16
SETS = 8
LENGTH = 1024
SEQS = 16
TOKENS = 16384
CAP = 544


def with_ends(values, key, least, largest):
    longest = values.shape.index(max(values.shape))
    spots = []
    for shift in (0, 1):
        where = [jax.random.randint(jax.random.fold_in(key, axis), (), 0, length) for axis, length in enumerate(values.shape)]
        where[longest] = (where[longest] + shift) % values.shape[longest]
        spots.append(tuple(where))
    return values.at[spots[0]].set(least).at[spots[1]].set(largest)


def level_of(key, dims, cuts, least, largest):
    factor_of = 1.0
    for position, parts in cuts:
        draws = jax.random.uniform(jax.random.fold_in(jax.random.fold_in(key, 6), position), (parts,), jnp.float32, least / len(cuts), largest / len(cuts))
        factor_of = factor_of * jnp.repeat(jnp.exp(draws), dims[position] // parts).reshape((-1,) + (1,) * (len(dims) - 1 - position))
    return factor_of


def deal_out(rng, own, number, rows, number_of, top, bound, slope):
    ranking = jax.random.permutation(rng, number_of)
    crowded, usual = load_shares(number_of, rows * top, bound, slope, True), load_shares(number_of, rows * top, bound, slope, False)
    places = jnp.arange(number_of)

    def named(tallies, offset_by):
        used = int((tallies > 0).sum())
        fixed = max(1, used // 4)
        passed = fixed + (places - fixed + offset_by * (used - fixed)) % max(1, number_of - fixed)
        return jnp.zeros((number_of,), jnp.int32).at[ranking[jnp.where(places < fixed, places, passed)]].set(jnp.asarray(tallies, jnp.int32))

    tallies = jnp.where(number % 4 == 0, named(crowded, number // 4), named(usual, number - number // 4 - 1))
    mixed = jax.random.permutation(jax.random.fold_in(own, 3), number_of)
    source_of, sink = mixed[0:number_of // 2 * 2:2], mixed[1:number_of // 2 * 2:2]
    margin = jnp.minimum(tallies[source_of] - 1, bound - tallies[sink]) // 2
    margin = jnp.where((source_of == ranking[0]) | (sink == ranking[0]) | (tallies[sink] == 0), 0, jnp.maximum(margin, 0))
    passed = jax.random.randint(jax.random.fold_in(own, 4), (number_of // 2,), 0, 1 << 20) % (margin + 1)
    tallies = tallies.at[source_of].add(-passed).at[sink].add(passed)
    labels = jnp.searchsorted(jnp.cumsum(tallies), jnp.arange(rows * top), side="right").astype(jnp.int32)
    listing = labels.reshape(top, rows).T
    listing = listing[jax.random.permutation(jax.random.fold_in(own, 1), rows)]
    offset_by = jax.random.randint(jax.random.fold_in(own, 2), (rows, 1), 0, top)
    return jnp.take_along_axis(listing, (jnp.arange(top)[None, :] + offset_by) % top, axis=1)


def load_shares(number_of, total, bound, lean, full):
    weights = [(1 << 20) // math.isqrt(rank ** lean) + 1 for rank in range(1, number_of + 1)]
    largest = bound if full else min(bound, max(-(-total // number_of), total * weights[0] // sum(weights)))
    least = 1 if total - largest >= number_of - 1 else 0
    holding, surplus = [largest] + [least] * (number_of - 1), total - largest - least * (number_of - 1)
    while surplus > 0:
        movable = [i for i in range(1, number_of) if holding[i] < largest] or [i for i in range(1, number_of) if holding[i] < bound]
        mass, budget = sum([weights[i] for i in movable]), surplus
        for i in movable:
            extra = min(bound - holding[i], max(1, budget * weights[i] // mass), surplus)
            holding[i] = holding[i] + extra
            surplus = surplus - extra
    return np.array(holding)


def normal_values(own_key, dims, deviation, limit, shards=(), kind=jnp.bfloat16):
    factor_of = level_of(own_key, dims, shards, -0.22, 0.18) if shards else 1.0
    drawn = jax.random.normal(own_key, dims, jnp.float32) * deviation * factor_of
    return jnp.minimum(jnp.maximum(drawn, -limit), limit).astype(kind)


def setup_inputs(seed: int = 0) -> dict:
    splits = jax.random.split(jax.random.key(seed), 24)
    tokens = normal_values(splits[0], (TOKENS, MODEL_WIDTH), 1.0, 6.0, ((0, 16), (1, 8)))
    cotangent = normal_values(splits[1], (TOKENS, MODEL_WIDTH), 1.0, 6.0, ((0, 16), (1, 8)))
    routes_keys = jax.random.split(jax.random.fold_in(splits[2], 1), TOKENS // LENGTH)
    routes_turns = jax.random.permutation(jax.random.fold_in(splits[2], 3), TOKENS // LENGTH)
    routes = jax.vmap(lambda own, number: deal_out(jax.random.fold_in(splits[2], 2), own, number, LENGTH, EXPERTS, TOP, CAP, 0))(routes_keys, routes_turns).reshape((TOKENS, TOP))
    adapter_set = with_ends(jax.random.randint(splits[3], (SEQS,), 0, SETS), jax.random.fold_in(splits[3], 1), 0, SETS - 1).astype(jnp.int32)
    attn_gain = jnp.clip(1.0 + 0.1 * jax.random.normal(splits[4], (MODEL_WIDTH,), jnp.float32), 0.5, 1.5)
    mixer_gain = jnp.clip(1.0 + 0.1 * jax.random.normal(splits[5], (MODEL_WIDTH,), jnp.float32), 0.5, 1.5)
    query_gain = jnp.clip(1.0 + 0.1 * jax.random.normal(splits[6], (MODEL_WIDTH,), jnp.float32), 0.5, 1.5)
    key_gain = jnp.clip(1.0 + 0.1 * jax.random.normal(splits[7], (MODEL_WIDTH,), jnp.float32), 0.5, 1.5)
    qkv_weight = normal_values(splits[8], (3, MODEL_WIDTH, MODEL_WIDTH), MODEL_WIDTH ** -0.5, 0.125, ((1, 16), (2, 8)))
    qkv_down = normal_values(splits[9], (3, MODEL_WIDTH, SETS * RANK), MODEL_WIDTH ** -0.5, 0.125, ((1, 16),))
    qkv_up = normal_values(splits[10], (3, SETS * RANK, MODEL_WIDTH), (SETS * RANK) ** -0.5, 0.5, ((2, 8),))
    out_weight = normal_values(splits[11], (MODEL_WIDTH, MODEL_WIDTH), (MODEL_WIDTH // 8) ** -0.5, 0.375, ((0, 8), (1, 16)))
    out_down = normal_values(splits[12], (MODEL_WIDTH, SETS * RANK), (MODEL_WIDTH // 8) ** -0.5, 0.375, ((0, 8),))
    out_up = normal_values(splits[13], (SETS * RANK, MODEL_WIDTH), (SETS * RANK) ** -0.5, 0.5, ((1, 8),))
    router_weight = normal_values(splits[14], (MODEL_WIDTH, EXPERTS), (4 * MODEL_WIDTH) ** -0.5, 0.0625, ((0, 16),))
    router_down = normal_values(splits[15], (MODEL_WIDTH, SETS * RANK), MODEL_WIDTH ** -0.5, 0.125, ((0, 16),))
    router_up = normal_values(splits[16], (SETS * RANK, EXPERTS), (4 * SETS * RANK) ** -0.5, 0.25)
    expert_in = normal_values(splits[17], (EXPERTS, 2, MODEL_WIDTH, FF), MODEL_WIDTH ** -0.5, 0.125, ((0, 8), (2, 16)))
    expert_in_down = normal_values(splits[18], (EXPERTS, 2, MODEL_WIDTH, SETS * RANK), MODEL_WIDTH ** -0.5, 0.125, ((0, 8), (2, 16)))
    expert_in_up = normal_values(splits[19], (EXPERTS, 2, SETS * RANK, FF), (SETS * RANK) ** -0.5, 0.5, ((0, 8),))
    expert_out = normal_values(splits[20], (EXPERTS, FF, MODEL_WIDTH), (FF // 16) ** -0.5, 0.75, ((0, 8), (2, 16)))
    expert_out_down = normal_values(splits[21], (EXPERTS, FF, SETS * RANK), FF ** -0.5, 0.1875, ((0, 8),))
    expert_out_up = normal_values(splits[22], (EXPERTS, SETS * RANK, MODEL_WIDTH), (SETS * RANK // 16) ** -0.5, 2.0, ((0, 8), (2, 16)))
    return dict(tokens=tokens, cotangent=cotangent, routes=routes, adapter_set=adapter_set, attn_gain=attn_gain, mixer_gain=mixer_gain, query_gain=query_gain, key_gain=key_gain, qkv_weight=qkv_weight, qkv_down=qkv_down, qkv_up=qkv_up, out_weight=out_weight, out_down=out_down, out_up=out_up, router_weight=router_weight, router_down=router_down, router_up=router_up, expert_in=expert_in, expert_in_down=expert_in_down, expert_in_up=expert_in_up, expert_out=expert_out, expert_out_down=expert_out_down, expert_out_up=expert_out_up)


EPS = 1e-05
THETA = 10000.0
HIGH = lax.Precision.HIGHEST

@jax.custom_vjp
def low(v):
    return lax.optimization_barrier(v.astype(jnp.bfloat16)).astype(jnp.float32)

@jax.custom_vjp
def low_back(v):
    return v

def low_keep(v):
    return (low(v), None)

def low_pass(kept, grad):
    return (grad,)

def back_keep(v):
    return (v, None)

def back_low(kept, grad):
    return (low(grad),)
low.defvjp(low_keep, low_pass)
low_back.defvjp(back_keep, back_low)

def matmul(spec, left, right):
    return jnp.einsum(spec, left, right, precision=HIGH)

def inverse_rms(values):
    return lax.rsqrt(lax.optimization_barrier(jnp.mean(values * values, axis=-1, keepdims=True)) + EPS)

def rope_tables():
    half = HEAD_DIM // 2
    frequency = THETA ** (-(jnp.arange(half, dtype=jnp.float32) * 2.0) / HEAD_DIM)
    angle = jnp.arange(LENGTH, dtype=jnp.float32)[:, None] * frequency[None, :]
    cosine = jnp.concatenate([jnp.cos(angle), jnp.cos(angle)], axis=1)
    sine = jnp.concatenate([jnp.sin(angle), jnp.sin(angle)], axis=1)
    return (cosine, sine)

def rotate(values):
    half = values.shape[-1] // 2
    return jnp.concatenate([-values[..., half:], values[..., :half]], axis=-1)

def apply_rope(values, cosine, sine):
    return values * cosine[:, None, :] + rotate(values) * sine[:, None, :]

def slot_rows(member):
    order = jnp.cumsum(member).astype(jnp.int32) - 1
    target = jnp.where(member > 0, order, CAP)
    rows = jnp.zeros((CAP + 1,), jnp.int32).at[target].set(jnp.arange(member.shape[0], dtype=jnp.int32))
    filled = jnp.sum(member).astype(jnp.int32)
    valid = jnp.arange(CAP, dtype=jnp.int32) < filled
    return (rows[:CAP], valid)

def one_head(item):
    query_rows, key_rows, value_rows = item
    scores = low_back(matmul('qe,ke->qk', query_rows, key_rows) * HEAD_DIM ** (-0.5))
    allowed = jnp.arange(LENGTH)[None, :] <= jnp.arange(LENGTH)[:, None]
    scores = jnp.where(allowed, scores, -jnp.inf)
    weights = jnp.exp(scores - lax.optimization_barrier(jnp.max(scores, axis=1, keepdims=True)))
    attend = weights / lax.optimization_barrier(jnp.sum(weights, axis=1, keepdims=True))
    return matmul('qk,ke->qe', low(attend), value_rows)

def layer(resid, route_rows, chosen, frozen, train):
    attn_gain, mixer_gain, query_gain, key_gain, qkv_weight, out_weight, router_weight, expert_in, expert_out = frozen
    qkv_down, qkv_up, out_down, out_up, router_down, router_up, in_down, in_up, down_down, down_up = train
    start = (chosen * RANK).astype(jnp.int32)

    def pick(array, axis):
        return lax.dynamic_slice_in_dim(array, start, RANK, axis)
    normed = low(resid * inverse_rms(resid) * attn_gain)
    hidden_code = low(matmul('td,kdr->ktr', normed, pick(qkv_down, 2)))
    projected = low_back(matmul('td,kdn->ktn', normed, qkv_weight) + matmul('ktr,krn->ktn', hidden_code, pick(qkv_up, 1)))
    queries = projected[0] * inverse_rms(projected[0]) * query_gain
    keys = projected[1] * inverse_rms(projected[1]) * key_gain
    value_rows = low(projected[2]).reshape(LENGTH, HEADS, HEAD_DIM)
    cosine, sine = rope_tables()
    queries = low(apply_rope(queries.reshape(LENGTH, HEADS, HEAD_DIM), cosine, sine))
    keys = low(apply_rope(keys.reshape(LENGTH, HEADS, HEAD_DIM), cosine, sine))
    heads_out = lax.map(jax.checkpoint(one_head), (queries.transpose(1, 0, 2), keys.transpose(1, 0, 2), value_rows.transpose(1, 0, 2)))
    attention = low(low_back(heads_out.transpose(1, 0, 2).reshape(LENGTH, MODEL_WIDTH)))
    output_hidden_code = matmul('td,dr->tr', attention, pick(out_down, 1))
    branch = low_back(matmul('td,de->te', attention, out_weight) + matmul('tr,re->te', output_hidden_code, pick(out_up, 0)))
    state = resid + branch
    mixer_in = low(state * inverse_rms(state) * mixer_gain)
    router_hidden_code = low(low_back(matmul('td,dr->tr', mixer_in, pick(router_down, 1))))
    logits = low_back(matmul('td,de->te', mixer_in, router_weight) + matmul('tr,re->te', router_hidden_code, pick(router_up, 0)))
    shifted = jnp.exp(logits - lax.optimization_barrier(jnp.max(logits, axis=1, keepdims=True)))
    probability = shifted / lax.optimization_barrier(jnp.sum(shifted, axis=1, keepdims=True))
    gate_all = jnp.take_along_axis(probability, route_rows, axis=1)

    def expert_step(total, item):
        ident, weight_in, adapt_in, lift_in, weight_down, adapt_down, lift_down = item
        hits = route_rows == ident
        member = jnp.any(hits, axis=1).astype(jnp.int32)
        expert_gate = lax.optimization_barrier(jnp.sum(jnp.where(hits, gate_all, 0.0), axis=1))
        rows, valid = slot_rows(member)
        routed = mixer_in[rows]
        in_latent = low(low_back(matmul('td,kdr->ktr', routed, pick(adapt_in, 2))))
        gate_up = low_back(matmul('td,kdf->ktf', routed, weight_in) + matmul('ktr,krf->ktf', in_latent, pick(lift_in, 1)))
        hidden = low(jax.nn.silu(gate_up[0]) * gate_up[1])
        down_latent = low(low_back(matmul('tf,fr->tr', hidden, pick(adapt_down, 1))))
        expert_value = low_back(matmul('tf,fd->td', hidden, weight_down) + matmul('tr,rd->td', down_latent, pick(lift_down, 0)))
        factor = expert_gate[rows] * valid.astype(expert_gate.dtype)
        return (total.at[rows].add(expert_value * factor[:, None]), None)
    items = (jnp.arange(EXPERTS, dtype=jnp.int32), expert_in, in_down, in_up, expert_out, down_down, down_up)
    mixture, unused = lax.scan(jax.checkpoint(expert_step), jnp.zeros_like(resid), items)
    return state + mixture

def reference(tokens, cotangent, routes, adapter_set, attn_gain, mixer_gain, query_gain, key_gain, qkv_weight, qkv_down, qkv_up, out_weight, out_down, out_up, router_weight, router_down, router_up, expert_in, expert_in_down, expert_in_up, expert_out, expert_out_down, expert_out_up):

    def wide(array):
        return array.astype(jnp.float32)
    frozen = (wide(attn_gain), wide(mixer_gain), wide(query_gain), wide(key_gain), wide(qkv_weight), wide(out_weight), wide(router_weight), wide(expert_in), wide(expert_out))
    train = (wide(qkv_down), wide(qkv_up), wide(out_down), wide(out_up), wide(router_down), wide(router_up), wide(expert_in_down), wide(expert_in_up), wide(expert_out_down), wide(expert_out_up))

    def forward(inputs, params):

        def one(item):
            resid, route_rows, chosen = item
            return layer(resid, route_rows, chosen, frozen, params)
        outputs = lax.map(jax.checkpoint(one), (inputs.reshape(SEQS, LENGTH, MODEL_WIDTH), routes.reshape(SEQS, LENGTH, TOP), adapter_set))
        return outputs.reshape(TOKENS, MODEL_WIDTH)
    result, pullback = jax.vjp(forward, wide(tokens), train)
    input_grad, grads = pullback(wide(cotangent))
    return (result.astype(jnp.bfloat16), input_grad, grads[0], grads[1], grads[2], grads[3], grads[4], grads[5], grads[6], grads[7], grads[8], grads[9])
```

```python
import functools

import jax
import jax.numpy as jnp
import numpy as np
from jax import lax
from jax.experimental import pallas as pl
from jax.experimental.pallas import tpu as pltpu
from jax.sharding import PartitionSpec as P

D = 2048
HEAD = 128
FF = 1024
RANK = 16
SETS = 8
S = 1024
W = 256
T = 128
PEERS = 8
PAD = 128
EPS = 1e-05
FACTOR = HEAD ** (-0.5)
F32 = jnp.float32
BF = jnp.bfloat16
MESH = pl.DeviceIdType.MESH
VMEM = pl.BlockSpec(memory_space=pltpu.VMEM)
ANY = pl.BlockSpec(memory_space=pl.ANY)

NN = (((1,), (0,)), ((), ()))
NT = (((1,), (1,)), ((), ()))
TN = (((0,), (0,)), ((), ()))


def nn(a, b):
    return lax.dot_general(a, b, NN, preferred_element_type=F32)


def nt(a, b):
    return lax.dot_general(a, b, NT, preferred_element_type=F32)


def tn(a, b):
    return lax.dot_general(a, b, TN, preferred_element_type=F32)


def lanes(rows):
    return lax.broadcasted_iota(jnp.int32, (rows, PAD), 1)


def span(start, size):
    return pl.ds(pl.multiple_of(start, size), size)


def params(collective=None, limit=62):
    return pltpu.CompilerParams(
        collective_id=collective,
        has_side_effects=collective is not None,
        vmem_limit_bytes=limit * 2**20,
    )


def greet():
    c = lax.axis_index("col")
    barrier = pltpu.get_barrier_semaphore()
    for k in range(1, PEERS):
        pl.semaphore_signal(
            barrier, inc=1, device_id={"col": lax.rem(c + k, PEERS)}, device_id_type=MESH
        )
    return barrier


def to_peer(src, dst, send, recv, peer):
    return pltpu.make_async_remote_copy(
        src_ref=src,
        dst_ref=dst,
        send_sem=send,
        recv_sem=recv,
        device_id={"col": peer},
        device_id_type=MESH,
    )


def peer_of(k):
    return lax.rem(lax.axis_index("col") + k, PEERS)


def source_of(k):
    return lax.rem(lax.axis_index("col") + PEERS - k, PEERS)


ORDER = (4, 1, 7, 5, 3, 2, 6)


def tokens_kernel(pay, gain, normed, rinv, resid, extra, buf, send, recv):
    c = lax.axis_index("col")
    barrier = greet()
    buf[c] = pay[...]
    pl.semaphore_wait(barrier, PEERS - 1)
    for k in ORDER:
        to_peer(pay, buf.at[c], send.at[k], recv.at[k], peer_of(k)).start()
    for k in ORDER:
        to_peer(pay, buf.at[source_of(k)], send.at[k], recv.at[k], peer_of(k)).wait_recv()
    extra[...] = jnp.zeros_like(extra)
    for p in range(PEERS):
        resid[p] = buf[p, span(c * T, T), :]
        extra[p, 0 : 2 * RANK, :] = buf[p, S : S + 2 * RANK, :]

    @pl.loop(0, S // 64)
    def _(i):
        rows = span(i * 64, 64)
        total = jnp.zeros((64, 1), F32)
        for p in range(PEERS):
            x = buf[p, rows, :].astype(F32)
            total += jnp.sum(x * x, axis=1, keepdims=True)
        r = lax.rsqrt(total / D + EPS)
        for p in range(PEERS):
            x = buf[p, rows, :].astype(F32)
            normed[rows, W * p : W * p + W] = (x * r * gain[:, W * p : W * p + W]).astype(BF)
        rinv[rows, :] = jnp.broadcast_to(r, (64, PAD))

    for k in ORDER:
        to_peer(pay, buf.at[source_of(k)], send.at[k], recv.at[k], peer_of(k)).wait_send()


def gather_tokens(pay, gain):
    rows = pay.shape[0]
    return pl.pallas_call(
        tokens_kernel,
        out_shape=(
            jax.ShapeDtypeStruct((S, D), BF),
            jax.ShapeDtypeStruct((S, PAD), F32),
            jax.ShapeDtypeStruct((PEERS, T, W), BF),
            jax.ShapeDtypeStruct((PEERS, PAD, W), BF),
        ),
        in_specs=[VMEM, VMEM],
        out_specs=(VMEM, VMEM, VMEM, VMEM),
        scratch_shapes=[
            pltpu.VMEM((PEERS, rows, W), BF),
            pltpu.SemaphoreType.DMA((PEERS,)),
            pltpu.SemaphoreType.DMA((PEERS,)),
        ],
        compiler_params=params(1, 32),
        cost_estimate=pl.CostEstimate(flops=5 * 10**10, bytes_accessed=10**7, transcendentals=0),
        name="tokens",
    )(pay, gain)


def columns_to_rows(first, second):
    lane = lanes(first.shape[0])
    tile = jnp.where(lane == 0, first, jnp.where(lane == 1, second, 0.0))
    return jnp.transpose(tile)[0:8, :]


def rows_to_columns(rows):
    padded = jnp.concatenate([rows, jnp.zeros((PAD - 8, rows.shape[1]), F32)], axis=0)
    return jnp.transpose(padded)


def swap_start(stat, inbox, send, recv):
    c = lax.axis_index("col")
    for k in ORDER:
        to_peer(stat, inbox.at[c], send.at[k], recv.at[k], peer_of(k)).start()


def swap_finish(stat, inbox, send, recv):
    for k in ORDER:
        to_peer(stat, inbox.at[source_of(k)], send.at[k], recv.at[k], peer_of(k)).wait()
    total = stat[...]
    for k in range(1, PEERS):
        total += inbox[source_of(k)]
    return total


def attention_kernel(
    normed, wq, bank, up, qgain, kgain, cosine, sine,
    att_t, att, qo, ko, vo, qraw, kraw, cols, lat,
    w, wsem, stat, inbox, ssem, rsem, asend, arecv,
):
    c = lax.axis_index("col")
    barrier = greet()
    loads = [
        pltpu.make_async_copy(wq.at[:, T * k : T * k + T, :], w.at[k], wsem.at[k]) for k in range(3)
    ]
    for load in loads:
        load.start()
    for load in loads:
        load.wait()
    blocks = 4
    rows_of = S // blocks
    lane = lanes(rows_of)
    for i in range(blocks):
        rows = slice(i * rows_of, (i + 1) * rows_of)
        x = normed[rows, :]
        code = jnp.where(lane < 3 * RANK, nn(x, bank[:, 0:PAD]), 0.0).astype(BF)
        lat[rows, :] = code
        parts = [
            nn(x, w[k].reshape(D, W)) + nn(code, up[:, W * k : W * k + W]) for k in range(3)
        ]
        qraw[rows, :] = parts[0]
        kraw[rows, :] = parts[1]
        vo[rows, :] = parts[2].astype(BF)
        stat[:, rows] = columns_to_rows(
            jnp.sum(parts[0] * parts[0], axis=1, keepdims=True),
            jnp.sum(parts[1] * parts[1], axis=1, keepdims=True),
        )
    pl.semaphore_wait(barrier, PEERS - 1)
    swap_start(stat, inbox, ssem, rsem)
    total = swap_finish(stat, inbox, ssem, rsem)
    scale = lax.rsqrt(total / D + EPS)
    for i in range(blocks):
        rows = slice(i * rows_of, (i + 1) * rows_of)
        column = rows_to_columns(scale[:, rows])
        cols[rows, :] = column
        for index, (raw, gain, out) in enumerate(((qraw, qgain, qo), (kraw, kgain, ko))):
            for h in range(2):
                feats = slice(HEAD * h, HEAD * h + HEAD)
                x = raw[rows, feats] * column[:, index : index + 1] * gain[:, feats]
                y = x * cosine[rows, :] + pltpu.roll(x, HEAD // 2, 1) * sine[rows, :]
                out[rows, feats] = y.astype(BF)
    for i in range(blocks):
        rows = slice(i * rows_of, (i + 1) * rows_of)
        seen = (i + 1) * rows_of
        allowed = lax.broadcasted_iota(jnp.int32, (rows_of, seen), 1) <= (
            lax.broadcasted_iota(jnp.int32, (rows_of, seen), 0) + i * rows_of
        )
        logs = []
        for h in range(2):
            feats = slice(HEAD * h, HEAD * h + HEAD)
            score = nt(qo[rows, feats], ko[0:seen, feats]) * FACTOR
            score = jnp.where(allowed, score, -1e30)
            top = jnp.max(score, axis=1, keepdims=True)
            weight = jnp.exp(score - top)
            norm = jnp.sum(weight, axis=1, keepdims=True)
            attend = (weight * (1.0 / norm)).astype(BF)
            att[rows, feats] = nn(attend, vo[0:seen, feats]).astype(BF)
            logs.append(top + jnp.log(norm))
        cols[rows, :] = jnp.where(
            lane == 2, logs[0], jnp.where(lane == 3, logs[1], cols[rows, :])
        )
        for p in (2 * i, 2 * i + 1):
            mine = slice(T * p, T * p + T)

            @pl.when(c != p)
            def _():
                to_peer(att.at[mine], att_t.at[c], asend.at[p], arecv.at[c], p).start()

            @pl.when(c == p)
            def _():
                att_t[p] = att[mine, :]

    for p in range(PEERS):

        @pl.when(c != p)
        def _():
            to_peer(
                att.at[T * p : T * p + T], att_t.at[p], asend.at[p], arecv.at[p], p
            ).wait()


def attention(normed, wq, bank, up, qgain, kgain, cosine, sine):
    full = jax.ShapeDtypeStruct((S, W), BF)
    wide = jax.ShapeDtypeStruct((S, W), F32)
    return pl.pallas_call(
        attention_kernel,
        out_shape=(
            jax.ShapeDtypeStruct((PEERS, T, W), BF),
            full, full, full, full, wide, wide,
            jax.ShapeDtypeStruct((S, PAD), F32),
            jax.ShapeDtypeStruct((S, PAD), BF),
        ),
        in_specs=[VMEM, ANY, VMEM, VMEM, VMEM, VMEM, VMEM, VMEM],
        out_specs=(VMEM,) * 9,
        scratch_shapes=[
            pltpu.VMEM((3, 16, T, W), BF),
            pltpu.SemaphoreType.DMA((3,)),
            pltpu.VMEM((8, S), F32),
            pltpu.VMEM((PEERS, 8, S), F32),
            pltpu.SemaphoreType.DMA((PEERS,)),
            pltpu.SemaphoreType.DMA((PEERS,)),
            pltpu.SemaphoreType.DMA((PEERS,)),
            pltpu.SemaphoreType.DMA((PEERS,)),
        ],
        compiler_params=params(2, 56),
        cost_estimate=pl.CostEstimate(flops=3 * 10**10, bytes_accessed=10**7, transcendentals=0),
        name="attention",
    )(normed, wq, bank, up, qgain, kgain, cosine, sine)


def load_out(mine, other, wo, sem):
    half = lax.rem(lax.axis_index("row"), 2)
    copies = []
    for index, (src, side) in enumerate(((mine, half), (other, 1 - half))):
        for p in range(PEERS):
            copies.append(
                pltpu.make_async_copy(
                    src.at[p],
                    wo.at[span(side * (D // 2), D // 2), W * p : W * p + W],
                    sem.at[index * PEERS + p],
                )
            )
    return copies


def member_of(routes, rows):
    lane = lanes(rows)
    found = lane == routes[:, 0:1] + 64
    for j in range(1, 8):
        found = found | (lane == routes[:, j : j + 1] + 64)
    return found


def state_kernel(
    att_t, mine, other, resid, extra, gain, bank, ru, routes,
    pay, state, prob_out, branch, lat_out,
    wo, sem,
):
    loads = load_out(mine, other, wo, sem)
    for load in loads:
        load.start()
    lane = lanes(T)
    lat = jnp.zeros((T, PAD), F32)
    for p in range(PEERS):
        lat += nt(att_t[p], extra[p])
    lat = jnp.where(lane < RANK, lat, 0.0)
    lat_out[...] = lat
    moved = pltpu.roll(lat, RANK, 1).astype(BF)
    x = jnp.concatenate([att_t[p] for p in range(PEERS)], axis=1)
    for load in loads:
        load.wait()
    total = jnp.zeros((T, 1), F32)
    for p in range(PEERS):
        feats = slice(W * p, W * p + W)
        part = nt(x, wo[feats, :]) + nn(moved, extra[p])
        branch[:, feats] = part.astype(BF)
        st = resid[p].astype(F32) + part
        state[:, feats] = st
        total += jnp.sum(st * st, axis=1, keepdims=True)
    r = lax.rsqrt(total / D + EPS)
    first = jnp.zeros((T, PAD), F32)
    for p in range(PEERS):
        feats = slice(W * p, W * p + W)
        m = (state[:, feats] * r * gain[:, feats]).astype(BF)
        pay[:, feats] = m
        first += nn(m, bank[feats, 0:PAD])
    code = jnp.where((lane >= 48) & (lane < 64), first, 0.0).astype(BF)
    valid = (lane >= 64) & (lane < 80)
    logits = jnp.where(valid, first + nn(code, ru[...]), -1e30)
    shifted = jnp.where(valid, jnp.exp(logits - jnp.max(logits, axis=1, keepdims=True)), 0.0)
    prob = shifted / jnp.sum(shifted, axis=1, keepdims=True)
    prob_out[...] = prob
    gate = jnp.where(member_of(routes, T), prob, 0.0)
    high = gate.astype(BF).astype(F32)
    low = pltpu.roll(gate - high, RANK, 1)
    pay[:, D:] = jnp.where(lane < 64, code.astype(F32), jnp.where(lane < 80, high, low)).astype(BF)


def to_state(att_t, mine, other, resid, extra, gain, bank, ru, routes):
    return pl.pallas_call(
        state_kernel,
        out_shape=(
            jax.ShapeDtypeStruct((T, D + PAD), BF),
            jax.ShapeDtypeStruct((T, D), F32),
            jax.ShapeDtypeStruct((T, PAD), F32),
            jax.ShapeDtypeStruct((T, D), BF),
            jax.ShapeDtypeStruct((T, PAD), F32),
        ),
        in_specs=[VMEM, ANY, ANY, VMEM, VMEM, VMEM, VMEM, VMEM, VMEM],
        out_specs=(VMEM,) * 5,
        scratch_shapes=[pltpu.VMEM((D, D), BF), pltpu.SemaphoreType.DMA((2 * PEERS,))],
        compiler_params=params(None, 40),
        cost_estimate=pl.CostEstimate(flops=10**10, bytes_accessed=10**7, transcendentals=0),
        name="state",
    )(att_t, mine, other, resid, extra, gain, bank, ru, routes)


SHIFTS = ((0, 0), (1, 0), (0, 3), (1, 3), (0, 1), (1, 1), (0, 2), (1, 2))
CHUNK = 256


def expert_kernel(*refs):
    pay, branch, cot, bank, upin, ad = refs[0:6]
    pin, pout = refs[6:14], refs[14:22]
    mixed, summed, xfull, gup, glow, glift, gdown = refs[22:29]
    (win, wd, cbuf, obuf, rbuf, a1, act, hid, vg, gg, ug, mix, xacc,
     aup, alow, alift, adown,
     lsem, csend, crecv, csem, send1, recv1, send2, recv2) = refs[29:]
    c = lax.axis_index("col")
    r = lax.axis_index("row")
    half = lax.rem(r, 2)
    partner = r + 1 - 2 * half
    barrier = greet()
    pl.semaphore_signal(barrier, inc=1, device_id={"row": partner}, device_id_type=MESH)

    def offset(shift, side):
        plane = lax.rem(r // 8 + shift[0], 2)
        place = lax.rem(lax.rem(r, 8) // 2 + shift[1], 4)
        return (plane * 8 + place * 2 + side) * T

    def pairs(i, side):
        at = span(offset(SHIFTS[i], side), T)
        return (
            (pin[i], win.at[:, :, at, :], 2 * i),
            (pout[i], wd.at[:, :, at], 2 * i + 1),
        )

    def across(i, side):
        return [
            pltpu.make_async_remote_copy(
                src_ref=src, dst_ref=dst, send_sem=csend.at[n], recv_sem=crecv.at[n],
                device_id={"row": partner}, device_id_type=MESH,
            )
            for src, dst, n in pairs(i, side)
        ]

    def local(i):
        return [pltpu.make_async_copy(src, dst, lsem.at[n]) for src, dst, n in pairs(i, half)]

    def cot_copy(j, slot):
        base = lax.rem(c // 2 + j, 4) * CHUNK
        return pltpu.make_async_copy(cot.at[:, span(base, CHUNK), :], cbuf.at[slot], csem.at[slot])

    pl.semaphore_wait(barrier, PEERS)
    for k in (1, 7, 6, 2, 5, 3, 4):
        to_peer(pay, xfull.at[span(c * T, T)], send1.at[peer_of(k)], recv1.at[c], peer_of(k)).start()
    for i in range(8):
        for copy in across(i, half):
            copy.start()
    for i in range(8):
        for copy in local(i):
            copy.start()
    cot_copy(0, 0).start()
    xfull[span(c * T, T), :] = pay[...]
    aup[...] = jnp.zeros_like(aup)
    alow[...] = jnp.zeros_like(alow)
    alift[...] = jnp.zeros_like(alift)
    adown[...] = jnp.zeros_like(adown)
    lane = lanes(CHUNK)
    for i in range(8):
        for copy in local(i):
            copy.wait()
        for copy in across(i, half):
            copy.wait_send()
        for copy in across(i, 1 - half):
            copy.wait_recv()

    def chunk(j, carry):
        p = lax.rem(c // 2 + j, 4)
        rows = span(p * CHUNK, CHUNK)
        slot = lax.rem(j, 2)
        for t in range(2):
            src = 2 * p + t

            @pl.when(src != c)
            def _():
                to_peer(
                    pay, xfull.at[span(src * T, T)], send1.at[src], recv1.at[src], src
                ).wait_recv()

        cot_copy(j, slot).wait()

        @pl.when(j < 3)
        def _():
            cot_copy(j + 1, 1 - slot).start()

        mix[...] = jnp.zeros_like(mix)

        @pl.when(j == 0)
        def _():
            mix[span(lax.rem(c, 2) * T, T), :] = branch[...].astype(F32)

        extras = xfull[rows, D : D + PAD].astype(F32)
        inlat = nn(xfull[rows, 0:D], bank[:, PAD : 2 * PAD]).astype(BF)
        gate_grads = []
        ilg_total = jnp.zeros((CHUNK, PAD), F32)
        for e in range(2):
            spot = 64 + 2 * c + e
            gate = jnp.sum(
                jnp.where((lane == spot) | (lane == spot + RANK), extras, 0.0),
                axis=1, keepdims=True,
            )

            @pl.loop(0, FF // 256)
            def _(f):
                fs = span(f * 256, 256)
                x = xfull[rows, 0:D]
                g = nn(x, win[e, 0, :, fs]) + nn(inlat, upin[2 * e, :, fs])
                u = nn(x, win[e, 1, :, fs]) + nn(inlat, upin[2 * e + 1, :, fs])
                sg = 1.0 / (1.0 + jnp.exp(-g))
                silu = g * sg
                act[:, fs] = silu
                a1[:, fs] = u * sg * (1.0 + g * (1.0 - sg))
                hid[:, fs] = (silu * u).astype(BF)

            dl = nn(hid[...], ad[e]).astype(BF)

            def down(d, gsum):
                ds = span(d * 256, 256)
                ev = nn(hid[...], wd[e, :, ds]) + nt(dl, bank[ds, 0:PAD])
                ct = cbuf[slot, d].astype(F32)
                vg[:, ds] = (ct * gate).astype(BF)
                total = mix[:, ds] + ev * gate
                if e == 0:
                    mix[:, ds] = total
                else:
                    mixed[d, rows, :] = total.astype(BF)
                return gsum + jnp.sum(ev * ct, axis=1, keepdims=True)

            gate_grads.append(lax.fori_loop(0, D // 256, down, jnp.zeros((CHUNK, 1), F32)))
            low = 80 + RANK * e
            dlg = jnp.where(
                (lane >= low) & (lane < low + RANK), nn(vg[...], bank[:, 0:PAD]), 0.0
            ).astype(BF)

            @pl.loop(0, FF // 256)
            def _(f):
                fs = span(f * 256, 256)
                hg = nt(vg[...], wd[e, fs, :]) + nt(dlg, ad[e, fs, :])
                gg[:, fs] = (hg * a1[:, fs]).astype(BF)
                ug[:, fs] = (hg * act[:, fs]).astype(BF)

            ilg32 = nt(gg[...], upin[2 * e]) + nt(ug[...], upin[2 * e + 1])
            ilg_total += ilg32
            ilg = ilg32.astype(BF)

            @pl.loop(0, D // 256)
            def _(d):
                ds = span(d * 256, 256)
                t = (
                    nt(gg[...], win[e, 0, ds, :])
                    + nt(ug[...], win[e, 1, ds, :])
                    + nt(ilg, bank[ds, PAD : 2 * PAD])
                )
                if e == 0:
                    xacc[:, ds] = t
                else:
                    obuf[rows, ds] = (xacc[:, ds] + t).astype(BF)

            for n, grad in ((2 * e, gg), (2 * e + 1, ug)):
                aup[n] += tn(inlat, grad[...])[RANK * n : RANK * n + RANK, :]
            alow[e] += tn(dlg, hid[...])[low : low + RANK, :]
            alift[e] += tn(dl, vg[...])[low : low + RANK, :]
        adown[...] += tn(ilg_total.astype(BF), xfull[rows, 0:D])[0 : 4 * RANK, :]
        obuf[rows, D : D + PAD] = jnp.where(
            lane == 64 + 2 * c, gate_grads[0], jnp.where(lane == 65 + 2 * c, gate_grads[1], 0.0)
        ).astype(BF)
        for t in range(2):
            dest = 2 * p + t

            @pl.when(dest != c)
            def _():
                to_peer(
                    obuf.at[span(dest * T, T)], rbuf.at[c], send2.at[dest], recv2.at[c], dest
                ).start()

        return carry

    lax.fori_loop(0, 4, chunk, 0)
    gup[...] = aup[...].astype(BF)
    glow[...] = alow[...].astype(BF)
    glift[...] = alift[...].astype(BF)
    gdown[...] = adown[...].astype(BF)
    for k in range(1, PEERS):
        q = peer_of(k)
        to_peer(pay, xfull.at[span(q * T, T)], send1.at[q], recv1.at[q], q).wait_send()
        to_peer(obuf.at[span(q * T, T)], rbuf.at[q], send2.at[q], recv2.at[q], q).wait()

    @pl.loop(0, T // 32)
    def _(i):
        at = span(i * 32, 32)
        total = obuf[span(c * T + i * 32, 32), :].astype(F32)
        for k in range(1, PEERS):
            total += rbuf[peer_of(k), at, :].astype(F32)
        summed[at, :] = total


def experts(pay, branch, cot, bank, upin, ad, pin, pout):
    sems = pltpu.SemaphoreType.DMA
    return pl.pallas_call(
        expert_kernel,
        out_shape=(
            jax.ShapeDtypeStruct((PEERS, S, W), BF),
            jax.ShapeDtypeStruct((T, D + PAD), F32),
            jax.ShapeDtypeStruct((S, D + PAD), BF),
            jax.ShapeDtypeStruct((4, RANK, FF), BF),
            jax.ShapeDtypeStruct((2, RANK, FF), BF),
            jax.ShapeDtypeStruct((2, RANK, D), BF),
            jax.ShapeDtypeStruct((4 * RANK, D), BF),
        ),
        in_specs=[VMEM, VMEM, ANY, VMEM, VMEM, VMEM] + [ANY] * 16,
        out_specs=(VMEM,) * 7,
        scratch_shapes=[
            pltpu.VMEM((2, 2, D, FF), BF),
            pltpu.VMEM((2, FF, D), BF),
            pltpu.VMEM((2, PEERS, CHUNK, W), BF),
            pltpu.VMEM((S, D + PAD), BF),
            pltpu.VMEM((PEERS, T, D + PAD), BF),
            pltpu.VMEM((CHUNK, FF), F32),
            pltpu.VMEM((CHUNK, FF), F32),
            pltpu.VMEM((CHUNK, FF), BF),
            pltpu.VMEM((CHUNK, D), BF),
            pltpu.VMEM((CHUNK, FF), BF),
            pltpu.VMEM((CHUNK, FF), BF),
            pltpu.VMEM((CHUNK, D), F32),
            pltpu.VMEM((CHUNK, D), F32),
            pltpu.VMEM((4, RANK, FF), F32),
            pltpu.VMEM((2, RANK, FF), F32),
            pltpu.VMEM((2, RANK, D), F32),
            pltpu.VMEM((4 * RANK, D), F32),
            sems((16,)), sems((16,)), sems((16,)), sems((2,)),
            sems((PEERS,)), sems((PEERS,)), sems((PEERS,)), sems((PEERS,)),
        ],
        compiler_params=params(3, 63),
        cost_estimate=pl.CostEstimate(flops=10**11, bytes_accessed=10**7, transcendentals=0),
        name="experts",
    )(pay, branch, cot, bank, upin, ad, *pin, *pout)


def back_kernel(
    summed, state, prob, routes, bank, ru, gain, cot_t, mine, other, extra, lat_o,
    q, k_, v, att, cols, qraw, kraw, qgain, kgain, cosine, sine, up, lat, xfull, normed,
    pg, bgc, stat3, lcg, gqkvup, goutdown, goutup, grup, growdown,
    wo, sem, bg, sbuf, abuf, dq, dk, dv, stat, inbox, ex,
    send1, recv1, send2, recv2, send3, recv3,
):
    c = lax.axis_index("col")
    barrier = greet()
    loads = load_out(mine, other, wo, sem)
    for load in loads:
        load.start()
    lane = lanes(T)
    p_ = prob[...]
    gg = jnp.where(member_of(routes, T), summed[:, D : D + PAD], 0.0)
    lgrad = (p_ * (gg - jnp.sum(p_ * gg, axis=1, keepdims=True))).astype(BF)
    rlg = nt(lgrad, ru[...]).astype(BF)
    both = jnp.where(lane < 64, rlg.astype(F32), lgrad.astype(F32)).astype(BF)
    total = jnp.zeros((T, 1), F32)
    for p in range(PEERS):
        feats = slice(W * p, W * p + W)
        st = state[:, feats]
        total += jnp.sum(st * st, axis=1, keepdims=True)
    r = lax.rsqrt(total / D + EPS)
    mean = jnp.zeros((T, 1), F32)
    for p in range(PEERS):
        feats = slice(W * p, W * p + W)
        m = (summed[:, feats] + nt(both, bank[feats, 0:PAD])) * gain[:, feats]
        mean += jnp.sum(state[:, feats] * m, axis=1, keepdims=True)
    mean = mean / D
    olg = jnp.zeros((T, PAD), F32)
    for p in range(PEERS):
        feats = slice(W * p, W * p + W)
        m = (summed[:, feats] + nt(both, bank[feats, 0:PAD])) * gain[:, feats]
        st = state[:, feats]
        grad = (cot_t[p].astype(F32) + r * m - st * (r * r * r) * mean).astype(BF)
        bg[p] = grad
        olg += nt(grad, extra[p])
    olg = jnp.where((lane >= RANK) & (lane < 2 * RANK), olg, 0.0)
    moved = pltpu.roll(olg, PAD - RANK, 1).astype(BF)
    info = jnp.where(
        lane < RANK, lat_o[...], jnp.where(lane < 2 * RANK, olg, both.astype(F32))
    ).astype(BF)
    x = jnp.concatenate([bg[p] for p in range(PEERS)], axis=1)
    for load in loads:
        load.wait()
    pl.semaphore_wait(barrier, PEERS - 1)
    for n in (4, 3, 5, 2, 6, 1, 7, 0):
        d = peer_of(n)
        part = nn(x, wo[:, span(d * W, W)]) + nn(moved, extra[d])
        sbuf[d, :, 0:W] = part.astype(BF)
        sbuf[d, :, W : W + PAD] = info
        if n:
            to_peer(sbuf.at[d], abuf.at[c], send1.at[n], recv1.at[n], d).start()
        else:
            abuf[c] = sbuf[c]
            bgc[c] = bg[c]
    for n in ORDER:
        d = peer_of(n)
        to_peer(bg.at[d], bgc.at[c], send2.at[n], recv2.at[n], d).start()
    for n in ORDER:
        d = peer_of(n)
        to_peer(sbuf.at[d], abuf.at[source_of(n)], send1.at[n], recv1.at[n], d).wait()
    for p in range(PEERS):
        ex[T * p : T * p + T, :] = abuf[p, :, W : W + PAD]

    blocks = 4
    size = S // blocks
    for h in range(2):
        feats = slice(HEAD * h, HEAD * h + HEAD)
        for i in reversed(range(blocks)):
            rows = slice(i * size, (i + 1) * size)
            seen = (i + 1) * size
            allowed = lax.broadcasted_iota(jnp.int32, (size, seen), 1) <= (
                lax.broadcasted_iota(jnp.int32, (size, seen), 0) + i * size
            )
            g = jnp.concatenate([abuf[2 * i, :, feats], abuf[2 * i + 1, :, feats]], axis=0)
            qb = q[rows, feats]
            kb = k_[0:seen, feats]
            score = nt(qb, kb) * FACTOR
            full = jnp.where(allowed, jnp.exp(score - cols[rows, 2 + h : 3 + h]), 0.0)
            wgrad = nt(g, v[0:seen, feats])
            center = jnp.sum(full * wgrad, axis=1, keepdims=True)
            sgrad = (full * (wgrad - center)).astype(BF)
            dq[rows, feats] = nn(sgrad, kb) * FACTOR
            dvp = tn(full.astype(BF), g)
            dkp = tn(sgrad, qb) * FACTOR
            if i == blocks - 1:
                dv[0:seen, feats] = dvp
                dk[0:seen, feats] = dkp
            else:
                dv[0:seen, feats] += dvp
                dk[0:seen, feats] += dkp
    for i in range(blocks):
        rows = slice(i * size, (i + 1) * size)
        dots = []
        for raw, gain_, grads in ((qraw, qgain, dq), (kraw, kgain, dk)):
            dot = jnp.zeros((size, 1), F32)
            for h in range(2):
                feats = slice(HEAD * h, HEAD * h + HEAD)
                y = grads[rows, feats]
                y = y * cosine[rows, :] - pltpu.roll(y, HEAD // 2, 1) * sine[rows, :]
                y = y * gain_[:, feats]
                grads[rows, feats] = y
                dot += jnp.sum(y * raw[rows, feats], axis=1, keepdims=True)
            dots.append(dot)
        stat[:, rows] = columns_to_rows(*dots)
    swap_start(stat, inbox, send3, recv3)
    goutdown[...] = tn(ex[...], att[...])[RANK : 2 * RANK, :].astype(BF)
    grup[...] = tn(xfull[:, D : D + PAD], ex[...])[48:64, :].astype(BF)
    growdown[3 * RANK : 4 * RANK, :] = tn(ex[...], xfull[:, 0:D])[48:64, :].astype(BF)
    dots = swap_finish(stat, inbox, send3, recv3)
    wide = lanes(size)
    for i in range(blocks):
        rows = slice(i * size, (i + 1) * size)
        column = rows_to_columns(dots[:, rows])
        stat_sum = jnp.zeros((size, 1), F32)
        code = jnp.zeros((size, PAD), F32)
        for n, (raw, grads) in enumerate(((qraw, dq), (kraw, dk))):
            rs = cols[rows, n : n + 1]
            x = raw[rows, :]
            y = rs * grads[rows, :] - x * (rs * rs * rs * column[:, n : n + 1] / D)
            y = y.astype(BF)
            pg[n, rows, :] = y
            stat_sum += jnp.sum(y.astype(F32) * x, axis=1, keepdims=True)
            code += nt(y, up[:, W * n : W * n + W])
        y = dv[rows, :].astype(BF)
        pg[2, rows, :] = y
        stat_sum += jnp.sum(y.astype(F32) * v[rows, :].astype(F32), axis=1, keepdims=True)
        code += nt(y, up[:, 2 * W : 3 * W])
        lcg[rows, :] = jnp.where(wide < 3 * RANK, code, 0.0).astype(BF)
        stat3[:, rows] = columns_to_rows(stat_sum, stat_sum)
    for n in range(3):
        gqkvup[n] = tn(lat[...], pg[n])[RANK * n : RANK * n + RANK, :].astype(BF)
    growdown[0 : 3 * RANK, :] = tn(lcg[...], normed[...])[0 : 3 * RANK, :].astype(BF)
    for n in ORDER:
        d = peer_of(n)
        to_peer(bg.at[d], bgc.at[source_of(n)], send2.at[n], recv2.at[n], d).wait()
    acc = jnp.zeros((PAD, W), F32)
    for p in range(PEERS):
        acc += tn(ex[T * p : T * p + T, :], bgc[p])
    goutup[...] = acc[0:RANK, :].astype(BF)


def back(*args):
    sems = pltpu.SemaphoreType.DMA((PEERS,))
    kinds = [VMEM] * len(args)
    kinds[8] = ANY
    kinds[9] = ANY
    return pl.pallas_call(
        back_kernel,
        out_shape=(
            jax.ShapeDtypeStruct((3, S, W), BF),
            jax.ShapeDtypeStruct((PEERS, T, W), BF),
            jax.ShapeDtypeStruct((8, S), F32),
            jax.ShapeDtypeStruct((S, PAD), BF),
            jax.ShapeDtypeStruct((3, RANK, W), BF),
            jax.ShapeDtypeStruct((RANK, W), BF),
            jax.ShapeDtypeStruct((RANK, W), BF),
            jax.ShapeDtypeStruct((RANK, PAD), BF),
            jax.ShapeDtypeStruct((4 * RANK, D), BF),
        ),
        in_specs=kinds,
        out_specs=(VMEM,) * 9,
        scratch_shapes=[
            pltpu.VMEM((D, D), BF),
            pltpu.SemaphoreType.DMA((2 * PEERS,)),
            pltpu.VMEM((PEERS, T, W), BF),
            pltpu.VMEM((PEERS, T, W + PAD), BF),
            pltpu.VMEM((PEERS, T, W + PAD), BF),
            pltpu.VMEM((S, W), F32),
            pltpu.VMEM((S, W), F32),
            pltpu.VMEM((S, W), F32),
            pltpu.VMEM((8, S), F32),
            pltpu.VMEM((PEERS, 8, S), F32),
            pltpu.VMEM((S, PAD), BF),
            sems, sems, sems, sems, sems, sems,
        ],
        compiler_params=params(4, 62),
        cost_estimate=pl.CostEstimate(flops=4 * 10**10, bytes_accessed=10**7, transcendentals=0),
        name="back",
    )(*args)


def input_kernel(
    pg, lcg, wq, bank, stat3, bgc, tokens, rinv, gain,
    out,
    w, wsem, own, sbuf, rbuf, inbox, send, recv, send3, recv3,
):
    c = lax.axis_index("col")
    barrier = greet()
    loads = [
        pltpu.make_async_copy(wq.at[:, T * k : T * k + T, :], w.at[k], wsem.at[k]) for k in range(3)
    ]
    for load in loads:
        load.start()
    for load in loads:
        load.wait()
    pl.semaphore_wait(barrier, PEERS - 1)
    swap_start(stat3, inbox, send3, recv3)
    for n in (4, 3, 5, 2, 6, 1, 7, 0):
        d = peer_of(n)
        tall = span(d * W, W)

        @pl.loop(0, 4)
        def _(i):
            rows = span(i * 256, 256)
            part = nt(lcg[rows, :], bank[tall, 0:PAD])
            for k in range(3):
                part += nt(pg[k, rows, :], w[k, pl.ds(2 * d, 2)].reshape(W, W))
            if n:
                sbuf[n, rows, :] = part.astype(BF)
            else:
                own[rows, :] = part

        if n:
            to_peer(sbuf.at[n], rbuf.at[n], send.at[n], recv.at[n], d).start()
    dots = swap_finish(stat3, inbox, send3, recv3)
    for n in (4, 3, 5, 2, 6, 1, 7):
        to_peer(sbuf.at[n], rbuf.at[n], send.at[n], recv.at[n], peer_of(n)).wait()
    for i in range(4):
        rows = slice(256 * i, 256 * i + 256)
        column = rows_to_columns(dots[:, rows])[:, 0:1]
        total = own[rows, :]
        for n in range(1, PEERS):
            total += rbuf[n, rows, :].astype(F32)
        r = rinv[rows, 0:1]
        grad = bgc[rows, :].astype(F32) + r * (total * gain[...])
        out[rows, :] = grad - tokens[rows, :].astype(F32) * (r * r * column / D)


def to_input(pg, lcg, wq, bank, stat3, bgc, tokens, rinv, gain):
    sems = pltpu.SemaphoreType.DMA((PEERS,))
    return pl.pallas_call(
        input_kernel,
        out_shape=jax.ShapeDtypeStruct((S, W), F32),
        in_specs=[VMEM, VMEM, ANY, VMEM, VMEM, VMEM, VMEM, VMEM, VMEM],
        out_specs=VMEM,
        scratch_shapes=[
            pltpu.VMEM((3, 16, T, W), BF),
            pltpu.SemaphoreType.DMA((3,)),
            pltpu.VMEM((S, W), F32),
            pltpu.VMEM((PEERS, S, W), BF),
            pltpu.VMEM((PEERS, S, W), BF),
            pltpu.VMEM((PEERS, 8, S), F32),
            sems, sems, sems, sems,
        ],
        compiler_params=params(5, 48),
        cost_estimate=pl.CostEstimate(flops=5 * 10**10, bytes_accessed=10**7, transcendentals=0),
        name="input",
    )(pg, lcg, wq, bank, stat3, bgc, tokens, rinv, gain)


def rope_tables():
    half = HEAD // 2
    frequency = (10000.0 ** (-(np.arange(half, dtype=np.float32) * 2.0) / HEAD)).astype(np.float32)
    angle = np.arange(S, dtype=np.float32)[:, None] * frequency[None, :]
    cosine, sine = np.cos(angle), np.sin(angle)
    return (
        np.concatenate([cosine, cosine], axis=1).astype(np.float32),
        np.concatenate([-sine, sine], axis=1).astype(np.float32),
    )


def row_id(plane, place, side):
    return plane * 8 + place * 2 + side


DEVICES = [(y, x, k) for y in range(2) for x in range(4) for k in range(2)]


def along_row(array, move):
    pairs = [(row_id(*d), row_id(*move(*d))) for d in DEVICES]
    return lax.ppermute(array, "row", pairs)


def plane_swap(y, x, k):
    return (1 - y, x, k)


def place_up(y, x, k):
    return (y, (x + 1) % 4, k)


def place_down(y, x, k):
    return (y, (x + 3) % 4, k)


def place_far(y, x, k):
    return (y, (x + 2) % 4, k)


def core_swap(y, x, k):
    return (y, x, 1 - k)


def pieces_in(w):
    o = along_row(w, plane_swap)
    l0, r0 = along_row(w, place_up), along_row(w, place_down)
    l1, r1 = along_row(o, place_up), along_row(o, place_down)
    f0, f1 = along_row(l0, place_up), along_row(r1, place_down)
    return [w, o, l0, l1, r0, r1, f0, f1]


def pieces_out(w):
    l0, r0, f0 = along_row(w, place_up), along_row(w, place_down), along_row(w, place_far)
    o, l1, r1, f1 = (along_row(a, plane_swap) for a in (w, l0, r0, f0))
    return [w, o, l0, l1, r0, r1, f0, f1]


def by_set(picked, blocks):
    return jnp.einsum("sr,rnd->snd", picked, blocks, preferred_element_type=F32)


def body(
    tokens, cotangent, routes, adapter_set, attn_gain, mixer_gain, query_gain, key_gain,
    qkv_weight, qkv_down, qkv_up, out_weight, out_down, out_up,
    router_weight, router_down, router_up,
    expert_in, expert_in_down, expert_in_up, expert_out, expert_out_down, expert_out_up,
):
    c = lax.axis_index("col")
    side = lax.axis_index("row") % 2
    start = adapter_set[0] * RANK

    out_up_pick = lax.dynamic_slice_in_dim(out_up, start, RANK, 0)
    out_down_pick = lax.dynamic_slice_in_dim(out_down, start, RANK, 1)
    pay0 = jnp.concatenate([tokens, out_down_pick.T, out_up_pick], axis=0)

    shard = jnp.concatenate([qkv_weight.reshape(3 * T, W), out_weight.T], axis=0)
    wq = lax.all_gather(shard, "row", axis=0)
    sets = lax.all_gather(adapter_set, "row", axis=0, tiled=True)
    picked = (sets[None, :] == jnp.arange(SETS, dtype=jnp.int32)[:, None]).astype(BF)

    down = jnp.concatenate(
        [
            jnp.moveaxis(qkv_down, 0, 1),
            router_down[:, None],
            jnp.moveaxis(expert_out_up, 2, 0),
            jnp.moveaxis(expert_in_down.reshape(4, T, PAD), 0, 1),
        ],
        axis=1,
    ).reshape(T, 10, SETS, RANK)
    down = jnp.einsum("dnsj,sr->rdnj", down, picked, preferred_element_type=F32).astype(BF)
    bank = jnp.concatenate(
        [
            down[:, :, :4].reshape(16, T, 64),
            jnp.broadcast_to(router_weight[None], (16, T, 16)),
            down[:, :, 4:6].reshape(16, T, 32),
            jnp.zeros((16, T, 16), BF),
            down[:, :, 6:].reshape(16, T, 64),
            jnp.zeros((16, T, 64), BF),
        ],
        axis=2,
    )
    bank = lax.all_to_all(bank, "row", split_axis=0, concat_axis=0, tiled=True).reshape(D, 2 * PAD)

    qkv_up_pick = lax.dynamic_slice_in_dim(qkv_up, start, RANK, 1)
    up = jnp.concatenate(
        [jnp.pad(qkv_up_pick[k], ((RANK * k, PAD - RANK * k - RANK), (0, 0))) for k in range(3)],
        axis=1,
    )
    in_up_pick = lax.dynamic_slice_in_dim(expert_in_up, start, RANK, 2).reshape(4, RANK, FF)
    upin = jnp.stack(
        [jnp.pad(in_up_pick[n], ((RANK * n, PAD - RANK * n - RANK), (0, 0))) for n in range(4)]
    )
    lower_pick = lax.dynamic_slice_in_dim(expert_out_down, start, RANK, 2)
    ad = jnp.stack(
        [jnp.pad(lower_pick[e], ((0, 0), (80 + RANK * e, 32 - RANK * e))) for e in range(2)]
    )
    ru = jnp.pad(lax.dynamic_slice_in_dim(router_up, start, RANK, 0), ((48, 64), (64, 48)))
    routes_t = lax.dynamic_slice_in_dim(routes, c * T, T, 0)
    cosine, sine = rope_tables()

    pin = pieces_in(expert_in)
    pout = pieces_out(expert_out)

    normed, rinv, resid, extra = gather_tokens(pay0, attn_gain[None])

    half = lax.dynamic_slice(wq, (side * 8, 3 * T, 0), (8, T, W)).reshape(D // 2, W)
    half = lax.all_gather(half, "col", axis=0)
    other = along_row(half, core_swap)
    cot = lax.all_gather(cotangent, "col", axis=0)

    qg, kg = query_gain[None], key_gain[None]
    att_t, att, q, k, v, qraw, kraw, cols, lat = attention(
        normed, wq, bank, up, qg, kg, cosine, sine
    )
    pay, state, prob, branch, lat_o = to_state(
        att_t, half, other, resid, extra, mixer_gain[None], bank, ru, routes_t
    )
    mixture, summed, xfull, gup, glow, glift, gdown = experts(
        pay, branch, cot, bank, upin, ad, pin, pout
    )
    mixture = lax.psum_scatter(mixture.reshape(PEERS * S, W), "col", scatter_dimension=0, tiled=True)
    mixed = (tokens.astype(F32) + mixture.astype(F32)).astype(BF)

    tall = jnp.concatenate([gdown, glift.reshape(2 * RANK, D)], axis=0)
    tall = jnp.moveaxis(tall.reshape(6 * RANK, 16, T), 1, 0)
    tall = lax.all_to_all(tall, "row", split_axis=0, concat_axis=0, tiled=True)
    flat = jnp.concatenate([gup.reshape(4 * RANK, FF), glow.reshape(2 * RANK, FF)], axis=0)
    flat = lax.all_gather(flat, "row", axis=0)

    cot_t = lax.dynamic_slice_in_dim(cot, c * T, T, 1)
    pg, bgc, stat3, lcg, gqkvup, goutdown, goutup, grup, gtall = back(
        summed, state, prob, routes_t, bank, ru, mixer_gain[None], cot_t, half, other, extra,
        lat_o, q, k, v, att, cols, qraw, kraw, qg, kg, cosine, sine, up, lat, xfull, normed,
    )
    low = jnp.moveaxis(gtall.reshape(4 * RANK, 16, T), 1, 0)
    low = lax.all_to_all(low, "row", split_axis=0, concat_axis=0, tiled=True)
    thin = jnp.concatenate(
        [gqkvup.reshape(3 * RANK, W), goutdown, goutup, jnp.pad(grup, ((0, 0), (0, W - PAD)))],
        axis=0,
    )
    thin = lax.all_gather(thin, "row", axis=0)

    gain_mine = lax.dynamic_slice_in_dim(attn_gain, c * W, W, 0)[None]
    tokens_grad = to_input(
        pg, lcg, wq, bank, stat3, bgc.reshape(S, W), tokens, rinv, gain_mine
    )

    tall = by_set(picked, tall)
    in_down_grad = (
        tall[:, : 4 * RANK].reshape(SETS, 2, 2, RANK, T).transpose(1, 2, 4, 0, 3)
        .reshape(2, 2, T, SETS * RANK)
    )
    lift_grad = (
        tall[:, 4 * RANK :].reshape(SETS, 2, RANK, T).transpose(1, 0, 2, 3)
        .reshape(2, SETS * RANK, T)
    )
    flat = by_set(picked, flat)
    in_up_grad = (
        flat[:, : 4 * RANK].reshape(SETS, 2, 2, RANK, FF).transpose(1, 2, 0, 3, 4)
        .reshape(2, 2, SETS * RANK, FF)
    )
    lower_grad = (
        flat[:, 4 * RANK :].reshape(SETS, 2, RANK, FF).transpose(1, 3, 0, 2)
        .reshape(2, FF, SETS * RANK)
    )
    low = by_set(picked, low)
    router_down_grad = low[:, 3 * RANK :].transpose(2, 0, 1).reshape(T, SETS * RANK)
    qkv_down_grad = lax.psum(low[:, : 3 * RANK].astype(BF), "col").astype(F32)
    qkv_down_grad = (
        qkv_down_grad.reshape(SETS, 3, RANK, T).transpose(1, 3, 0, 2).reshape(3, T, SETS * RANK)
    )
    thin = by_set(picked, thin)
    qkv_up_grad = (
        thin[:, : 3 * RANK].reshape(SETS, 3, RANK, W).transpose(1, 0, 2, 3)
        .reshape(3, SETS * RANK, W)
    )
    out_down_grad = thin[:, 3 * RANK : 4 * RANK].transpose(2, 0, 1).reshape(W, SETS * RANK)
    out_up_grad = thin[:, 4 * RANK : 5 * RANK].reshape(SETS * RANK, W)
    router_up_grad = thin[:, 5 * RANK :, 64:80].reshape(SETS * RANK, 16)
    return (
        mixed, tokens_grad, qkv_down_grad, qkv_up_grad, out_down_grad, out_up_grad,
        router_down_grad, router_up_grad, in_down_grad, in_up_grad, lower_grad, lift_grad,
    )


def solution(mesh):
    in_specs = (
        P("row", "col"), P("row", "col"), P("row", None), P("row"), P(), P(), P("col"), P("col"),
        P(None, "row", "col"), P(None, "row", None), P(None, None, "col"),
        P("col", "row"), P("col", None), P(None, "col"),
        P("row", None), P("row", None), P(),
        P("col", None, "row", None), P("col", None, "row", None), P("col", None, None, None),
        P("col", None, "row"), P("col", None, None), P("col", None, "row"),
    )
    out_specs = (
        P("row", "col"), P("row", "col"), P(None, "row", None), P(None, None, "col"),
        P("col", None), P(None, "col"), P("row", None), P(),
        P("col", None, "row", None), P("col", None, None, None), P("col", None, None),
        P("col", None, "row"),
    )
    return jax.shard_map(body, mesh=mesh, in_specs=in_specs, out_specs=out_specs, check_vma=False)
```

```python
import functools

import jax
import jax.numpy as jnp
import numpy as np
from jax import lax
from jax.experimental import pallas as pl
from jax.experimental.pallas import tpu as pltpu
from jax.sharding import PartitionSpec as P

D = 2048
HEAD = 128
FF = 1024
RANK = 16
SETS = 8
S = 1024
W = 256
T = 128
PEERS = 8
PAD = 128
EPS = 1e-05
FACTOR = HEAD ** (-0.5)
F32 = jnp.float32
BF = jnp.bfloat16
MESH = pl.DeviceIdType.MESH
VMEM = pl.BlockSpec(memory_space=pltpu.VMEM)
ANY = pl.BlockSpec(memory_space=pl.ANY)

NN = (((1,), (0,)), ((), ()))
NT = (((1,), (1,)), ((), ()))
TN = (((0,), (0,)), ((), ()))


def nn(a, b):
    return lax.dot_general(a, b, NN, preferred_element_type=F32)


def nt(a, b):
    return lax.dot_general(a, b, NT, preferred_element_type=F32)


def tn(a, b):
    return lax.dot_general(a, b, TN, preferred_element_type=F32)


def lanes(rows):
    return lax.broadcasted_iota(jnp.int32, (rows, PAD), 1)


def span(start, size):
    return pl.ds(pl.multiple_of(start, size), size)


def params(collective=None, limit=62):
    return pltpu.CompilerParams(
        collective_id=collective,
        has_side_effects=collective is not None,
        vmem_limit_bytes=limit * 2**20,
    )


def greet():
    c = lax.axis_index("col")
    barrier = pltpu.get_barrier_semaphore()
    for k in range(1, PEERS):
        pl.semaphore_signal(
            barrier, inc=1, device_id={"col": lax.rem(c + k, PEERS)}, device_id_type=MESH
        )
    return barrier


def to_peer(src, dst, send, recv, peer):
    return pltpu.make_async_remote_copy(
        src_ref=src,
        dst_ref=dst,
        send_sem=send,
        recv_sem=recv,
        device_id={"col": peer},
        device_id_type=MESH,
    )


def peer_of(k):
    return lax.rem(lax.axis_index("col") + k, PEERS)


def source_of(k):
    return lax.rem(lax.axis_index("col") + PEERS - k, PEERS)


ORDER = (4, 1, 7, 5, 3, 2, 6)


PLACES = ((0, 0), (0, 1), (1, 0), (3, 0), (1, 1), (3, 1), (2, 0), (2, 1))
NEAR = ((0, 1), (1, 0), (3, 0))


def place(rel):
    c = lax.axis_index("col")
    return lax.rem(c // 4 + rel[1], 2) * 4 + lax.rem(lax.rem(c, 4) + rel[0], 4)


def greet_near():
    barrier = pltpu.get_barrier_semaphore()
    for rel in NEAR:
        pl.semaphore_signal(barrier, inc=1, device_id={"col": place(rel)}, device_id_type=MESH)
    return barrier


class Gather:
    MOVES = {
        "a0": ((0, 0), (0, 1), 0, (0, 1), 0),
        "a1": ((0, 0), (3, 0), 0, (1, 0), 2),
        "a2": ((0, 0), (1, 0), 0, (3, 0), 1),
        "b1": ((0, 1), (3, 1), 0, (1, 0), 4),
        "b2": ((0, 1), (1, 1), 0, (3, 0), 3),
        "c1": ((3, 0), (2, 0), 1, (1, 0), 5),
        "c2": ((1, 0), (2, 0), 2, (3, 0), 6),
        "d1": ((3, 1), (2, 1), 1, (1, 0), 7),
        "d2": ((1, 1), (2, 1), 2, (3, 0), 8),
    }
    FROM = (
        ((0, 1), 0), ((1, 0), 0), ((3, 0), 0), ((1, 1), 0), ((3, 1), 0),
        ((2, 0), 1), ((2, 0), 2), ((2, 1), 1), ((2, 1), 2),
    )

    def __init__(self, here, there, rows, send, recv):
        self.here, self.there, self.rows, self.send, self.recv = here, there, rows, send, recv

    def part(self, which):
        half = self.rows // 2
        return ((0, self.rows), (0, half), (half, half))[which]

    def move(self, name):
        src, dst, which, to, arrives = self.MOVES[name]
        lo, n = self.part(which)
        return to_peer(
            self.here(src, lo, n), self.there(src, dst, lo, n),
            self.send.at[list(self.MOVES).index(name)], self.recv.at[arrives], place(to),
        )

    def start(self, *names):
        for name in names:
            self.move(name).start()

    def wait(self, *arrivals):
        for i in arrivals:
            rel, which = self.FROM[i]
            lo, n = self.part(which)
            ref = self.here(rel, lo, n)
            to_peer(ref, ref, self.send.at[0], self.recv.at[i], place((0, 1))).wait_recv()

    def sent(self):
        for name in self.MOVES:
            self.move(name).wait_send()


def row_place(shift):
    r = lax.axis_index("row")
    plane = lax.rem(r // 8 + shift[0], 2)
    spot = lax.rem(lax.rem(r, 8) // 2 + shift[1], 4)
    return plane * 8 + spot * 2 + lax.rem(r, 2)


PLANE, UP, DOWN, FAR = (1, 0), (0, 1), (0, 3), (0, 2)


def greet_row(barrier, *shifts):
    for shift in shifts:
        pl.semaphore_signal(
            barrier, inc=1, device_id={"row": row_place(shift)}, device_id_type=MESH
        )


def along(src, dst, send, recv, shift):
    return pltpu.make_async_remote_copy(
        src_ref=src, dst_ref=dst, send_sem=send, recv_sem=recv,
        device_id={"row": row_place(shift)}, device_id_type=MESH,
    )


def tokens_kernel(
    pay, gain, cot, win, wout, normed, rinv, resid, extra, cots, wo, wl, wr, ql, qr, qf,
    buf, send, recv, send2, recv2, sem, send3, recv3,
):
    c = lax.axis_index("col")
    barrier = greet_near()
    greet_row(barrier, PLANE, UP, DOWN, FAR)
    weights = [
        along(src, dst, send3.at[n], recv3.at[n], shift)
        for n, (src, dst, shift) in enumerate(
            (
                (win, wo, PLANE), (win, wl, UP), (win, wr, DOWN),
                (wout, ql, UP), (wout, qr, DOWN), (wout, qf, FAR),
            )
        )
    ]
    keep = pltpu.make_async_copy(cot, cots.at[c], sem)
    keep.start()
    buf[c] = pay[...]
    pl.semaphore_wait(barrier, 7)
    ring = Gather(
        lambda rel, lo, n: buf.at[place(rel), lo : lo + n],
        lambda src, dst, lo, n: buf.at[place(src), lo : lo + n],
        pay.shape[0], send, recv,
    )

    def cot_part(rel, lo, n):
        if rel == (0, 0):
            return cot.at[lo : lo + n]
        return cots.at[place(rel), lo : lo + n]

    second = Gather(
        cot_part, lambda src, dst, lo, n: cots.at[place(src), lo : lo + n], S, send2, recv2
    )
    ring.start("a0", "a1", "a2")
    for copy in weights:
        copy.start()
    ring.wait(0)
    ring.start("b1", "b2")
    ring.wait(1, 2)
    ring.start("c1", "c2")
    ring.wait(3, 4)
    ring.start("d1", "d2")
    second.start("a0", "a1", "a2")
    ring.wait(5, 6, 7, 8)
    extra[...] = jnp.zeros_like(extra)
    for p in range(PEERS):
        resid[p] = buf[p, span(c * T, T), :]
        extra[p, 0 : 2 * RANK, :] = buf[p, S : S + 2 * RANK, :]

    @pl.loop(0, S // 64)
    def _(i):
        rows = span(i * 64, 64)
        total = jnp.zeros((64, 1), F32)
        for p in range(PEERS):
            x = buf[p, rows, :].astype(F32)
            total += jnp.sum(x * x, axis=1, keepdims=True)
        r = lax.rsqrt(total / D + EPS)
        for p in range(PEERS):
            x = buf[p, rows, :].astype(F32)
            normed[rows, W * p : W * p + W] = (x * r * gain[:, W * p : W * p + W]).astype(BF)
        rinv[rows, :] = jnp.broadcast_to(r, (64, PAD))

    second.wait(0)
    second.start("b1", "b2")
    second.wait(1, 2)
    second.start("c1", "c2")
    second.wait(3, 4)
    second.start("d1", "d2")
    second.wait(5, 6, 7, 8)
    ring.sent()
    second.sent()
    keep.wait()
    for copy in weights:
        copy.wait()


def gather_tokens(pay, gain, cot, win, wout):
    rows = pay.shape[0]
    return pl.pallas_call(
        tokens_kernel,
        out_shape=(
            jax.ShapeDtypeStruct((S, D), BF),
            jax.ShapeDtypeStruct((S, PAD), F32),
            jax.ShapeDtypeStruct((PEERS, T, W), BF),
            jax.ShapeDtypeStruct((PEERS, PAD, W), BF),
            jax.ShapeDtypeStruct((PEERS, S, W), BF),
        )
        + (jax.ShapeDtypeStruct(win.shape, BF),) * 3
        + (jax.ShapeDtypeStruct(wout.shape, BF),) * 3,
        in_specs=[VMEM, VMEM, ANY, ANY, ANY],
        out_specs=(VMEM, VMEM, VMEM, VMEM) + (ANY,) * 7,
        scratch_shapes=[
            pltpu.VMEM((PEERS, rows, W), BF),
            pltpu.SemaphoreType.DMA((9,)),
            pltpu.SemaphoreType.DMA((9,)),
            pltpu.SemaphoreType.DMA((9,)),
            pltpu.SemaphoreType.DMA((9,)),
            pltpu.SemaphoreType.DMA,
            pltpu.SemaphoreType.DMA((6,)),
            pltpu.SemaphoreType.DMA((6,)),
        ],
        compiler_params=params(1, 32),
        cost_estimate=pl.CostEstimate(flops=5 * 10**10, bytes_accessed=10**7, transcendentals=0),
        name="tokens",
    )(pay, gain, cot, win, wout)


def columns_to_rows(first, second):
    lane = lanes(first.shape[0])
    tile = jnp.where(lane == 0, first, jnp.where(lane == 1, second, 0.0))
    return jnp.transpose(tile)[0:8, :]


def rows_to_columns(rows):
    padded = jnp.concatenate([rows, jnp.zeros((PAD - 8, rows.shape[1]), F32)], axis=0)
    return jnp.transpose(padded)


def swap_start(stat, inbox, send, recv):
    c = lax.axis_index("col")
    for k in ORDER:
        to_peer(stat, inbox.at[c], send.at[k], recv.at[k], peer_of(k)).start()


def swap_finish(stat, inbox, send, recv):
    for k in ORDER:
        to_peer(stat, inbox.at[source_of(k)], send.at[k], recv.at[k], peer_of(k)).wait()
    total = stat[...]
    for k in range(1, PEERS):
        total += inbox[source_of(k)]
    return total


def attention_kernel(
    normed, wq, picks, up, qgain, kgain, cosine, sine, po, pl0, pr0, x0, xl, xr, xf,
    att_t, att, qo, ko, vo, qraw, kraw, cols, lat, bank, wmine, wother,
    pl1, pr1, pf0, pf1, y0, yl, yr, yf,
    w, wsem, stat, inbox, ssem, rsem, asend, arecv, osend, orecv, xsend, xrecv, psend, precv,
):
    c = lax.axis_index("col")
    side = lax.rem(lax.axis_index("row"), 2)
    partner = lax.axis_index("row") + 1 - 2 * side
    barrier = greet()
    pl.semaphore_signal(barrier, inc=1, device_id={"row": partner}, device_id_type=MESH)
    greet_row(barrier, PLANE, UP, DOWN)
    first, last = pl.ds(0, 1), pl.ds(1, 1)
    weights = [
        along(src, dst, psend.at[n], precv.at[n], shift)
        for n, (src, dst, shift) in enumerate(
            (
                (po, pl1, UP), (po, pr1, DOWN),
                (pl0.at[first], pf0.at[first], UP), (pr0.at[last], pf0.at[last], DOWN),
                (x0, y0, PLANE), (xl, yl, PLANE), (xr, yr, PLANE), (xf, yf, PLANE),
                (pl1.at[first], pf1.at[first], UP), (pr1.at[last], pf1.at[last], DOWN),
            )
        )
    ]

    def out_part(rel, lo, n):
        if rel == (0, 0):
            return wq.at[pl.ds(8 * side + lo, n), 6 * T : 7 * T, :]
        return wmine.at[place(rel), lo : lo + n]

    ring = Gather(
        out_part, lambda src, dst, lo, n: wmine.at[place(src), lo : lo + n], 8, osend, orecv
    )

    def across(rel):
        n = PLACES.index(rel)
        return pltpu.make_async_remote_copy(
            src_ref=out_part(rel, 0, 8), dst_ref=wother.at[place(rel)],
            send_sem=xsend.at[n], recv_sem=xrecv.at[n],
            device_id={"row": partner}, device_id_type=MESH,
        )

    keep = pltpu.make_async_copy(out_part((0, 0), 0, 8), wmine.at[c], wsem.at[6])
    keep.start()
    loads = [
        pltpu.make_async_copy(wq.at[:, T * k : T * k + T, :], w.at[k], wsem.at[k]) for k in range(6)
    ]
    for load in loads:
        load.start()
    pl.semaphore_wait(barrier, PEERS + 3)
    ring.start("a0", "a1", "a2")
    for copy in weights[:8]:
        copy.start()
    across((0, 0)).start()
    for load in loads:
        load.wait()

    @pl.loop(0, 16)
    def _(i):
        chosen = nn(w[3, i, :, 0:PAD], picks[0]) + nn(w[3, i, :, PAD : 2 * PAD], picks[1])
        chosen += nn(w[4, i, :, 0:PAD], picks[2]) + nn(w[4, i, :, PAD : 2 * PAD], picks[3])
        bank[span(i * T, T), :] = (chosen + w[5, i, :, 0:PAD].astype(F32)).astype(BF)

    blocks = 4
    rows_of = S // blocks
    lane = lanes(rows_of)
    for i in range(blocks):
        rows = slice(i * rows_of, (i + 1) * rows_of)
        x = normed[rows, :]
        code = jnp.where(lane < 3 * RANK, nn(x, bank[:, 0:PAD]), 0.0).astype(BF)
        lat[rows, :] = code
        parts = [
            nn(x, w[k].reshape(D, W)) + nn(code, up[:, W * k : W * k + W]) for k in range(3)
        ]
        qraw[rows, :] = parts[0]
        kraw[rows, :] = parts[1]
        vo[rows, :] = parts[2].astype(BF)
        stat[:, rows] = columns_to_rows(
            jnp.sum(parts[0] * parts[0], axis=1, keepdims=True),
            jnp.sum(parts[1] * parts[1], axis=1, keepdims=True),
        )
    swap_start(stat, inbox, ssem, rsem)
    ring.wait(0)
    ring.start("b1", "b2")
    ring.wait(1, 2)
    ring.start("c1", "c2")
    for rel in NEAR:
        across(rel).start()
    total = swap_finish(stat, inbox, ssem, rsem)
    scale = lax.rsqrt(total / D + EPS)
    for i in range(blocks):
        rows = slice(i * rows_of, (i + 1) * rows_of)
        column = rows_to_columns(scale[:, rows])
        cols[rows, :] = column
        for index, (raw, gain, out) in enumerate(((qraw, qgain, qo), (kraw, kgain, ko))):
            for h in range(2):
                feats = slice(HEAD * h, HEAD * h + HEAD)
                x = raw[rows, feats] * column[:, index : index + 1] * gain[:, feats]
                y = x * cosine[rows, :] + pltpu.roll(x, HEAD // 2, 1) * sine[rows, :]
                out[rows, feats] = y.astype(BF)
    ring.wait(3, 4)
    ring.start("d1", "d2")
    across((1, 1)).start()
    across((3, 1)).start()
    weights[0].wait_recv()
    weights[1].wait_recv()
    weights[8].start()
    weights[9].start()
    for i in range(blocks):
        rows = slice(i * rows_of, (i + 1) * rows_of)
        seen = (i + 1) * rows_of
        allowed = lax.broadcasted_iota(jnp.int32, (rows_of, seen), 1) <= (
            lax.broadcasted_iota(jnp.int32, (rows_of, seen), 0) + i * rows_of
        )
        logs = []
        for h in range(2):
            feats = slice(HEAD * h, HEAD * h + HEAD)
            score = nt(qo[rows, feats], ko[0:seen, feats]) * FACTOR
            score = jnp.where(allowed, score, -1e30)
            top = jnp.max(score, axis=1, keepdims=True)
            weight = jnp.exp(score - top)
            norm = jnp.sum(weight, axis=1, keepdims=True)
            attend = (weight * (1.0 / norm)).astype(BF)
            att[rows, feats] = nn(attend, vo[0:seen, feats]).astype(BF)
            logs.append(top + jnp.log(norm))
        cols[rows, :] = jnp.where(
            lane == 2, logs[0], jnp.where(lane == 3, logs[1], cols[rows, :])
        )
        for p in (2 * i, 2 * i + 1):
            mine = slice(T * p, T * p + T)

            @pl.when(c != p)
            def _():
                to_peer(att.at[mine], att_t.at[c], asend.at[p], arecv.at[c], p).start()

            @pl.when(c == p)
            def _():
                att_t[p] = att[mine, :]

    ring.wait(5, 6, 7, 8)
    across((2, 0)).start()
    across((2, 1)).start()
    for p in range(PEERS):

        @pl.when(c != p)
        def _():
            to_peer(
                att.at[T * p : T * p + T], att_t.at[p], asend.at[p], arecv.at[p], p
            ).wait()

    ring.sent()
    keep.wait()
    for rel in PLACES:
        across(rel).wait()
    weights[0].wait_send()
    weights[1].wait_send()
    for copy in weights[2:]:
        copy.wait()


def attention(normed, wq, picks, up, qgain, kgain, cosine, sine, inner, outer):
    full = jax.ShapeDtypeStruct((S, W), BF)
    wide = jax.ShapeDtypeStruct((S, W), F32)
    return pl.pallas_call(
        attention_kernel,
        out_shape=(
            jax.ShapeDtypeStruct((PEERS, T, W), BF),
            full, full, full, full, wide, wide,
            jax.ShapeDtypeStruct((S, PAD), F32),
            jax.ShapeDtypeStruct((S, PAD), BF),
            jax.ShapeDtypeStruct((D, PAD), BF),
            jax.ShapeDtypeStruct((PEERS, 8, T, W), BF),
            jax.ShapeDtypeStruct((PEERS, 8, T, W), BF),
        )
        + (jax.ShapeDtypeStruct(inner[0].shape, BF),) * 4
        + (jax.ShapeDtypeStruct(outer[0].shape, BF),) * 4,
        in_specs=[VMEM, ANY, VMEM, VMEM, VMEM, VMEM, VMEM, VMEM] + [ANY] * 7,
        out_specs=(VMEM,) * 10 + (ANY,) * 10,
        scratch_shapes=[
            pltpu.VMEM((6, 16, T, W), BF),
            pltpu.SemaphoreType.DMA((7,)),
            pltpu.VMEM((8, S), F32),
            pltpu.VMEM((PEERS, 8, S), F32),
            pltpu.SemaphoreType.DMA((PEERS,)),
            pltpu.SemaphoreType.DMA((PEERS,)),
            pltpu.SemaphoreType.DMA((PEERS,)),
            pltpu.SemaphoreType.DMA((PEERS,)),
            pltpu.SemaphoreType.DMA((9,)),
            pltpu.SemaphoreType.DMA((9,)),
            pltpu.SemaphoreType.DMA((PEERS,)),
            pltpu.SemaphoreType.DMA((PEERS,)),
            pltpu.SemaphoreType.DMA((10,)),
            pltpu.SemaphoreType.DMA((10,)),
        ],
        compiler_params=params(2, 56),
        cost_estimate=pl.CostEstimate(flops=3 * 10**10, bytes_accessed=10**7, transcendentals=0),
        name="attention",
    )(normed, wq, picks, up, qgain, kgain, cosine, sine, *inner, *outer)


def load_out(mine, other, wo, sem):
    half = lax.rem(lax.axis_index("row"), 2)
    copies = []
    for index, (src, side) in enumerate(((mine, half), (other, 1 - half))):
        for p in range(PEERS):
            copies.append(
                pltpu.make_async_copy(
                    src.at[p],
                    wo.at[span(side * (D // 2), D // 2), W * p : W * p + W],
                    sem.at[index * PEERS + p],
                )
            )
    return copies


def member_of(routes, rows):
    lane = lanes(rows)
    found = lane == routes[:, 0:1] + 64
    for j in range(1, 8):
        found = found | (lane == routes[:, j : j + 1] + 64)
    return found


def state_kernel(
    att_t, mine, other, resid, extra, gain, bank, ru, routes,
    pay, state, prob_out, branch, lat_out,
    wo, sem,
):
    loads = load_out(mine, other, wo, sem)
    for load in loads:
        load.start()
    lane = lanes(T)
    lat = jnp.zeros((T, PAD), F32)
    for p in range(PEERS):
        lat += nt(att_t[p], extra[p])
    lat = jnp.where(lane < RANK, lat, 0.0)
    lat_out[...] = lat
    moved = pltpu.roll(lat, RANK, 1).astype(BF)
    x = jnp.concatenate([att_t[p] for p in range(PEERS)], axis=1)
    for load in loads:
        load.wait()
    total = jnp.zeros((T, 1), F32)
    for p in range(PEERS):
        feats = slice(W * p, W * p + W)
        part = nt(x, wo[feats, :]) + nn(moved, extra[p])
        branch[:, feats] = part.astype(BF)
        st = resid[p].astype(F32) + part
        state[:, feats] = st
        total += jnp.sum(st * st, axis=1, keepdims=True)
    r = lax.rsqrt(total / D + EPS)
    first = jnp.zeros((T, PAD), F32)
    for p in range(PEERS):
        feats = slice(W * p, W * p + W)
        m = (state[:, feats] * r * gain[:, feats]).astype(BF)
        pay[:, feats] = m
        first += nn(m, bank[feats, 0:PAD])
    code = jnp.where((lane >= 48) & (lane < 64), first, 0.0).astype(BF)
    valid = (lane >= 64) & (lane < 80)
    logits = jnp.where(valid, first + nn(code, ru[...]), -1e30)
    shifted = jnp.where(valid, jnp.exp(logits - jnp.max(logits, axis=1, keepdims=True)), 0.0)
    prob = shifted / jnp.sum(shifted, axis=1, keepdims=True)
    prob_out[...] = prob
    gate = jnp.where(member_of(routes, T), prob, 0.0)
    high = gate.astype(BF).astype(F32)
    low = pltpu.roll(gate - high, RANK, 1)
    pay[:, D:] = jnp.where(lane < 64, code.astype(F32), jnp.where(lane < 80, high, low)).astype(BF)


def to_state(att_t, mine, other, resid, extra, gain, bank, ru, routes):
    return pl.pallas_call(
        state_kernel,
        out_shape=(
            jax.ShapeDtypeStruct((T, D + PAD), BF),
            jax.ShapeDtypeStruct((T, D), F32),
            jax.ShapeDtypeStruct((T, PAD), F32),
            jax.ShapeDtypeStruct((T, D), BF),
            jax.ShapeDtypeStruct((T, PAD), F32),
        ),
        in_specs=[VMEM, ANY, ANY, VMEM, VMEM, VMEM, VMEM, VMEM, VMEM],
        out_specs=(VMEM,) * 5,
        scratch_shapes=[pltpu.VMEM((D, D), BF), pltpu.SemaphoreType.DMA((2 * PEERS,))],
        compiler_params=params(None, 40),
        cost_estimate=pl.CostEstimate(flops=10**10, bytes_accessed=10**7, transcendentals=0),
        name="state",
    )(att_t, mine, other, resid, extra, gain, bank, ru, routes)


SHIFTS = ((0, 0), (1, 0), (0, 3), (1, 3), (0, 1), (1, 1), (0, 2), (1, 2))
CHUNK = 256
TILE = 512
STEPS = (1, 2, 3)
LAST = 0


def expert_kernel(*refs):
    pay, branch, cot, ebank, upin, ad = refs[0:6]
    pin, pout = refs[6:14], refs[14:22]
    mixed, summed, xout, gup, glow, glift, gdown = refs[22:29]
    (xfull, win, wd, cbuf, obuf, rbuf, a1, act, hid, vg, gg, ug, mix, xacc,
     aup, alow, alift, adown,
     lsem, csend, crecv, csem, send1, recv1, send2, recv2, xsem, mbank, bsend, brecv) = refs[29:]
    c = lax.axis_index("col")
    r = lax.axis_index("row")
    half = lax.rem(r, 2)
    partner = r + 1 - 2 * half
    barrier = greet()

    def offset(shift, side):
        plane = lax.rem(r // 8 + shift[0], 2)
        place = lax.rem(lax.rem(r, 8) // 2 + shift[1], 4)
        return (plane * 8 + place * 2 + side) * T

    def pairs(i, side):
        at = span(offset(SHIFTS[i], side), T)
        return (
            (pin[i], win.at[:, :, at, :], 2 * i),
            (pout[i], wd.at[:, :, at], 2 * i + 1),
        )

    def across(i, side):
        return [
            pltpu.make_async_remote_copy(
                src_ref=src, dst_ref=dst, send_sem=csend.at[n], recv_sem=crecv.at[n],
                device_id={"row": partner}, device_id_type=MESH,
            )
            for src, dst, n in pairs(i, side)
        ]

    def local(i):
        return [pltpu.make_async_copy(src, dst, lsem.at[n]) for src, dst, n in pairs(i, half)]

    sources = [place(rel) for rel in PLACES]

    def source(step, t):
        chosen = sources[2 * LAST + t]
        for j in range(3):
            chosen = jnp.where(step == j, sources[2 * STEPS[j] + t], chosen)
        return chosen

    def cot_copies(step, slot):
        return [
            pltpu.make_async_copy(
                cot.at[:, span(source(step, t) * T, T), :],
                cbuf.at[slot, :, T * t : T * t + T, :],
                csem.at[2 * slot + t],
            )
            for t in range(2)
        ]

    ring = Gather(
        lambda rel, lo, n: xfull.at[pl.ds(T * PLACES.index(rel) + lo, n)],
        lambda src, dst, lo, n: xfull.at[pl.ds(T * PLACES.index(dst) + lo, n)],
        T, send1, recv1,
    )
    for n in range(1, 16):
        pl.semaphore_signal(
            barrier, inc=1, device_id={"row": lax.rem(r + n, 16)}, device_id_type=MESH
        )

    def bank_copy(n):
        q = lax.rem(r + n, 16)
        return pltpu.make_async_remote_copy(
            src_ref=ebank.at[q], dst_ref=mbank.at[r], send_sem=bsend.at[n], recv_sem=brecv.at[n],
            device_id={"row": q}, device_id_type=MESH,
        )

    def bank_arrival(n):
        q = lax.rem(r + 16 - n, 16)
        return pltpu.make_async_remote_copy(
            src_ref=ebank.at[q], dst_ref=mbank.at[q], send_sem=bsend.at[n], recv_sem=brecv.at[n],
            device_id={"row": q}, device_id_type=MESH,
        )

    def bank(at):
        return mbank[at // T : (at + TILE) // T].reshape(TILE, PAD)

    def whole_bank():
        return mbank[...].reshape(D, PAD)

    xfull[0:T, :] = pay[...]
    mbank[r] = ebank[r]
    pl.semaphore_wait(barrier, PEERS + 14)
    ring.start("a0", "a1", "a2")
    for n in range(1, 16):
        bank_copy(n).start()
    for i in range(8):
        for copy in across(i, half):
            copy.start()
    for i in range(8):
        for copy in local(i):
            copy.start()
    for copy in cot_copies(0, 0):
        copy.start()
    aup[...] = jnp.zeros_like(aup)
    alow[...] = jnp.zeros_like(alow)
    alift[...] = jnp.zeros_like(alift)
    adown[...] = jnp.zeros_like(adown)
    lane = lanes(CHUNK)
    ring.wait(0)
    ring.start("b1", "b2")
    ring.wait(1, 2)
    ring.start("c1", "c2")
    for n in range(1, 16):
        bank_arrival(n).wait_recv()
    for n in range(1, 16):
        bank_copy(n).wait_send()
    for i in range(8):
        for copy in local(i):
            copy.wait()
        for copy in across(i, half):
            copy.wait_send()
        for copy in across(i, 1 - half):
            copy.wait_recv()

    def chunk(j, carry):
        rows = span(lax.rem(j + STEPS[0], 4) * CHUNK, CHUNK)
        slot = lax.rem(j, 2)

        @pl.when(j == 1)
        def _():
            ring.wait(3, 4)
            ring.start("d1", "d2")

        @pl.when(j == 2)
        def _():
            ring.wait(5, 6, 7, 8)

        for copy in cot_copies(j, slot):
            copy.wait()

        @pl.when(j < 3)
        def _():
            for copy in cot_copies(j + 1, 1 - slot):
                copy.start()

        mix[...] = jnp.zeros_like(mix)

        @pl.when(j == 3)
        def _():
            mix[0:T, :] = branch[...].astype(F32)

        extras = xfull[rows, D : D + PAD].astype(F32)
        inlat = nn(xfull[rows, 0:D], whole_bank()).astype(BF)
        gate_grads = []
        ilg_total = jnp.zeros((CHUNK, PAD), F32)
        for e in range(2):
            spot = 64 + 2 * c + e
            gate = jnp.sum(
                jnp.where((lane == spot) | (lane == spot + RANK), extras, 0.0),
                axis=1, keepdims=True,
            )

            for f in range(FF // TILE):
                fs = slice(f * TILE, f * TILE + TILE)
                x = xfull[rows, 0:D]
                g = nn(x, win[e, 0, :, fs]) + nn(inlat, upin[2 * e, :, fs])
                u = nn(x, win[e, 1, :, fs]) + nn(inlat, upin[2 * e + 1, :, fs])
                sg = 1.0 / (1.0 + jnp.exp(-g))
                silu = g * sg
                act[:, fs] = silu
                a1[:, fs] = u * sg * (1.0 + g * (1.0 - sg))
                hid[:, fs] = (silu * u).astype(BF)

            dl = nn(hid[...], ad[e]).astype(BF)

            gsum = jnp.zeros((CHUNK, 1), F32)
            for d in range(D // TILE):
                ds = slice(d * TILE, d * TILE + TILE)
                ev = nn(hid[...], wd[e, :, ds]) + nt(dl, bank(d * TILE))
                halves = [cbuf[slot, 2 * d + m] for m in range(TILE // W)]
                ct = jnp.concatenate(halves, axis=1).astype(F32)
                vg[:, ds] = (ct * gate).astype(BF)
                total = mix[:, ds] + ev * gate
                if e == 0:
                    mix[:, ds] = total
                else:
                    for t in range(2):
                        for m in range(TILE // W):
                            mixed[2 * d + m, span(source(j, t) * T, T), :] = total[
                                T * t : T * t + T, W * m : W * m + W
                            ].astype(BF)
                gsum += jnp.sum(ev * ct, axis=1, keepdims=True)
            gate_grads.append(gsum)
            low = 80 + RANK * e
            dlg = jnp.where(
                (lane >= low) & (lane < low + RANK), nn(vg[...], whole_bank()), 0.0
            ).astype(BF)

            for f in range(FF // TILE):
                fs = slice(f * TILE, f * TILE + TILE)
                hg = nt(vg[...], wd[e, fs, :]) + nt(dlg, ad[e, fs, :])
                gg[:, fs] = (hg * a1[:, fs]).astype(BF)
                ug[:, fs] = (hg * act[:, fs]).astype(BF)

            ilg32 = nt(gg[...], upin[2 * e]) + nt(ug[...], upin[2 * e + 1])
            ilg_total += ilg32
            ilg = ilg32.astype(BF)

            for d in range(D // TILE):
                ds = slice(d * TILE, d * TILE + TILE)
                t = (
                    nt(gg[...], win[e, 0, ds, :])
                    + nt(ug[...], win[e, 1, ds, :])
                    + nt(ilg, bank(d * TILE))
                )
                if e == 0:
                    xacc[:, ds] = t
                else:
                    obuf[rows, ds] = (xacc[:, ds] + t).astype(BF)

            for n, grad in ((2 * e, gg), (2 * e + 1, ug)):
                aup[n] += tn(inlat, grad[...])[RANK * n : RANK * n + RANK, :]
            alow[e] += tn(dlg, hid[...])[low : low + RANK, :]
            alift[e] += tn(dl, vg[...])[low : low + RANK, :]
        adown[...] += tn(ilg_total.astype(BF), xfull[rows, 0:D])[0 : 4 * RANK, :]
        obuf[rows, D : D + PAD] = jnp.where(
            lane == 64 + 2 * c, gate_grads[0], jnp.where(lane == 65 + 2 * c, gate_grads[1], 0.0)
        ).astype(BF)
        for step in range(4):

            @pl.when(j == step)
            def _():
                for t in range(2):
                    n = 2 * ((step + STEPS[0]) % 4) + t
                    if n:
                        back_to(n).start()

        return carry

    def back_to(n):
        rel = PLACES[n]
        seen = PLACES.index(((4 - rel[0]) % 4, rel[1]))
        return to_peer(
            obuf.at[pl.ds(T * n, T)], rbuf.at[seen], send2.at[n], recv2.at[seen], place(rel)
        )

    lax.fori_loop(0, 4, chunk, 0)
    keep = [
        pltpu.make_async_copy(
            xfull.at[pl.ds(T * n, T)], xout.at[span(sources[n] * T, T)], xsem.at[n]
        )
        for n in range(PEERS)
    ]
    for copy in keep:
        copy.start()
    gup[...] = aup[...].astype(BF)
    glow[...] = alow[...].astype(BF)
    glift[...] = alift[...].astype(BF)
    gdown[...] = adown[...].astype(BF)
    ring.sent()
    for n in range(1, PEERS):
        back_to(n).wait_send()
        to_peer(
            obuf.at[pl.ds(T * n, T)], rbuf.at[n], send2.at[n], recv2.at[n], place(PLACES[n])
        ).wait_recv()
    for copy in keep:
        copy.wait()

    @pl.loop(0, T // 32)
    def _(i):
        at = span(i * 32, 32)
        total = obuf[at, :].astype(F32)
        for n in range(1, PEERS):
            total += rbuf[n, at, :].astype(F32)
        summed[at, :] = total


def experts(pay, branch, cot, bank, upin, ad, pin, pout):
    sems = pltpu.SemaphoreType.DMA
    return pl.pallas_call(
        expert_kernel,
        out_shape=(
            jax.ShapeDtypeStruct((PEERS, S, W), BF),
            jax.ShapeDtypeStruct((T, D + PAD), F32),
            jax.ShapeDtypeStruct((S, D + PAD), BF),
            jax.ShapeDtypeStruct((4, RANK, FF), BF),
            jax.ShapeDtypeStruct((2, RANK, FF), BF),
            jax.ShapeDtypeStruct((2, RANK, D), BF),
            jax.ShapeDtypeStruct((4 * RANK, D), BF),
        ),
        in_specs=[VMEM, VMEM, ANY, VMEM, VMEM, VMEM] + [ANY] * 16,
        out_specs=(VMEM, VMEM, ANY, VMEM, VMEM, VMEM, VMEM),
        scratch_shapes=[
            pltpu.VMEM((S, D + PAD), BF),
            pltpu.VMEM((2, 2, D, FF), BF),
            pltpu.VMEM((2, FF, D), BF),
            pltpu.VMEM((2, PEERS, CHUNK, W), BF),
            pltpu.VMEM((S, D + PAD), BF),
            pltpu.VMEM((PEERS, T, D + PAD), BF),
            pltpu.VMEM((CHUNK, FF), F32),
            pltpu.VMEM((CHUNK, FF), F32),
            pltpu.VMEM((CHUNK, FF), BF),
            pltpu.VMEM((CHUNK, D), BF),
            pltpu.VMEM((CHUNK, FF), BF),
            pltpu.VMEM((CHUNK, FF), BF),
            pltpu.VMEM((CHUNK, D), F32),
            pltpu.VMEM((CHUNK, D), F32),
            pltpu.VMEM((4, RANK, FF), F32),
            pltpu.VMEM((2, RANK, FF), F32),
            pltpu.VMEM((2, RANK, D), F32),
            pltpu.VMEM((4 * RANK, D), F32),
            sems((16,)), sems((16,)), sems((16,)), sems((4,)),
            sems((9,)), sems((9,)), sems((PEERS,)), sems((PEERS,)), sems((PEERS,)),
            pltpu.VMEM((16, T, PAD), BF), sems((16,)), sems((16,)),
        ],
        compiler_params=params(3, 63),
        cost_estimate=pl.CostEstimate(flops=10**11, bytes_accessed=10**7, transcendentals=0),
        name="experts",
    )(pay, branch, cot, bank, upin, ad, *pin, *pout)


def back_kernel(
    summed, state, prob, routes, bank, ru, gain, cot_t, mine, other, extra, lat_o,
    q, k_, v, att, cols, qraw, kraw, qgain, kgain, cosine, sine, up, lat, xfull, normed,
    mixture, tokens,
    mixed, pg, bgc, stat3, lcg, gqkvup, goutdown, goutup, grup, growdown,
    wo, sem, bg, sbuf, abuf, dq, dk, dv, stat, inbox, ex,
    send1, recv1, send2, recv2, send3, recv3, mbuf, send4, recv4,
):
    c = lax.axis_index("col")
    barrier = greet()
    own = pltpu.make_async_copy(mixture.at[c], mbuf.at[0], send4.at[0])
    own.start()
    loads = load_out(mine, other, wo, sem)
    for load in loads:
        load.start()
    lane = lanes(T)
    p_ = prob[...]
    gg = jnp.where(member_of(routes, T), summed[:, D : D + PAD], 0.0)
    lgrad = (p_ * (gg - jnp.sum(p_ * gg, axis=1, keepdims=True))).astype(BF)
    rlg = nt(lgrad, ru[...]).astype(BF)
    both = jnp.where(lane < 64, rlg.astype(F32), lgrad.astype(F32)).astype(BF)
    total = jnp.zeros((T, 1), F32)
    for p in range(PEERS):
        feats = slice(W * p, W * p + W)
        st = state[:, feats]
        total += jnp.sum(st * st, axis=1, keepdims=True)
    r = lax.rsqrt(total / D + EPS)
    mean = jnp.zeros((T, 1), F32)
    for p in range(PEERS):
        feats = slice(W * p, W * p + W)
        m = (summed[:, feats] + nt(both, bank[feats, 0:PAD])) * gain[:, feats]
        mean += jnp.sum(state[:, feats] * m, axis=1, keepdims=True)
    mean = mean / D
    olg = jnp.zeros((T, PAD), F32)
    for p in range(PEERS):
        feats = slice(W * p, W * p + W)
        m = (summed[:, feats] + nt(both, bank[feats, 0:PAD])) * gain[:, feats]
        st = state[:, feats]
        grad = (cot_t[p].astype(F32) + r * m - st * (r * r * r) * mean).astype(BF)
        bg[p] = grad
        olg += nt(grad, extra[p])
    olg = jnp.where((lane >= RANK) & (lane < 2 * RANK), olg, 0.0)
    moved = pltpu.roll(olg, PAD - RANK, 1).astype(BF)
    info = jnp.where(
        lane < RANK, lat_o[...], jnp.where(lane < 2 * RANK, olg, both.astype(F32))
    ).astype(BF)
    x = jnp.concatenate([bg[p] for p in range(PEERS)], axis=1)
    for load in loads:
        load.wait()
    pl.semaphore_wait(barrier, PEERS - 1)
    for n in (4, 3, 5, 2, 6, 1, 7, 0):
        d = peer_of(n)
        part = nn(x, wo[:, span(d * W, W)]) + nn(moved, extra[d])
        sbuf[d, :, 0:W] = part.astype(BF)
        sbuf[d, :, W : W + PAD] = info
        if n:
            to_peer(sbuf.at[d], abuf.at[c], send1.at[n], recv1.at[n], d).start()
        else:
            abuf[c] = sbuf[c]
            bgc[c] = bg[c]
    for n in ORDER:
        d = peer_of(n)
        to_peer(bg.at[d], bgc.at[c], send2.at[n], recv2.at[n], d).start()
    for n in ORDER:
        d = peer_of(n)
        to_peer(mixture.at[d], mbuf.at[n], send4.at[n], recv4.at[n], d).start()
    for n in ORDER:
        d = peer_of(n)
        to_peer(sbuf.at[d], abuf.at[source_of(n)], send1.at[n], recv1.at[n], d).wait()
    for p in range(PEERS):
        ex[T * p : T * p + T, :] = abuf[p, :, W : W + PAD]

    blocks = 4
    size = S // blocks
    for h in range(2):
        feats = slice(HEAD * h, HEAD * h + HEAD)
        for i in reversed(range(blocks)):
            rows = slice(i * size, (i + 1) * size)
            seen = (i + 1) * size
            allowed = lax.broadcasted_iota(jnp.int32, (size, seen), 1) <= (
                lax.broadcasted_iota(jnp.int32, (size, seen), 0) + i * size
            )
            g = jnp.concatenate([abuf[2 * i, :, feats], abuf[2 * i + 1, :, feats]], axis=0)
            qb = q[rows, feats]
            kb = k_[0:seen, feats]
            score = nt(qb, kb) * FACTOR
            full = jnp.where(allowed, jnp.exp(score - cols[rows, 2 + h : 3 + h]), 0.0)
            wgrad = nt(g, v[0:seen, feats])
            center = jnp.sum(full * wgrad, axis=1, keepdims=True)
            sgrad = (full * (wgrad - center)).astype(BF)
            dq[rows, feats] = nn(sgrad, kb) * FACTOR
            dvp = tn(full.astype(BF), g)
            dkp = tn(sgrad, qb) * FACTOR
            if i == blocks - 1:
                dv[0:seen, feats] = dvp
                dk[0:seen, feats] = dkp
            else:
                dv[0:seen, feats] += dvp
                dk[0:seen, feats] += dkp
    for i in range(blocks):
        rows = slice(i * size, (i + 1) * size)
        dots = []
        for raw, gain_, grads in ((qraw, qgain, dq), (kraw, kgain, dk)):
            dot = jnp.zeros((size, 1), F32)
            for h in range(2):
                feats = slice(HEAD * h, HEAD * h + HEAD)
                y = grads[rows, feats]
                y = y * cosine[rows, :] - pltpu.roll(y, HEAD // 2, 1) * sine[rows, :]
                y = y * gain_[:, feats]
                grads[rows, feats] = y
                dot += jnp.sum(y * raw[rows, feats], axis=1, keepdims=True)
            dots.append(dot)
        stat[:, rows] = columns_to_rows(*dots)
    swap_start(stat, inbox, send3, recv3)
    goutdown[...] = tn(ex[...], att[...])[RANK : 2 * RANK, :].astype(BF)
    grup[...] = tn(xfull[:, D : D + PAD], ex[...])[48:64, :].astype(BF)
    growdown[3 * RANK : 4 * RANK, :] = tn(ex[...], xfull[:, 0:D])[48:64, :].astype(BF)
    dots = swap_finish(stat, inbox, send3, recv3)
    wide = lanes(size)
    for i in range(blocks):
        rows = slice(i * size, (i + 1) * size)
        column = rows_to_columns(dots[:, rows])
        stat_sum = jnp.zeros((size, 1), F32)
        code = jnp.zeros((size, PAD), F32)
        for n, (raw, grads) in enumerate(((qraw, dq), (kraw, dk))):
            rs = cols[rows, n : n + 1]
            x = raw[rows, :]
            y = rs * grads[rows, :] - x * (rs * rs * rs * column[:, n : n + 1] / D)
            y = y.astype(BF)
            pg[n, rows, :] = y
            stat_sum += jnp.sum(y.astype(F32) * x, axis=1, keepdims=True)
            code += nt(y, up[:, W * n : W * n + W])
        y = dv[rows, :].astype(BF)
        pg[2, rows, :] = y
        stat_sum += jnp.sum(y.astype(F32) * v[rows, :].astype(F32), axis=1, keepdims=True)
        code += nt(y, up[:, 2 * W : 3 * W])
        lcg[rows, :] = jnp.where(wide < 3 * RANK, code, 0.0).astype(BF)
        stat3[:, rows] = columns_to_rows(stat_sum, stat_sum)
    for n in range(3):
        gqkvup[n] = tn(lat[...], pg[n])[RANK * n : RANK * n + RANK, :].astype(BF)
    growdown[0 : 3 * RANK, :] = tn(lcg[...], normed[...])[0 : 3 * RANK, :].astype(BF)
    for n in ORDER:
        d = peer_of(n)
        to_peer(bg.at[d], bgc.at[source_of(n)], send2.at[n], recv2.at[n], d).wait()
    acc = jnp.zeros((PAD, W), F32)
    for p in range(PEERS):
        acc += tn(ex[T * p : T * p + T, :], bgc[p])
    goutup[...] = acc[0:RANK, :].astype(BF)
    own.wait()
    for n in ORDER:
        d = peer_of(n)
        to_peer(mixture.at[d], mbuf.at[n], send4.at[n], recv4.at[n], d).wait()

    @pl.loop(0, S // 64)
    def _(i):
        rows = span(i * 64, 64)
        total = tokens[rows, :].astype(F32)
        for n in range(PEERS):
            total += mbuf[n, rows, :].astype(F32)
        mixed[rows, :] = total.astype(BF)


def back(*args):
    sems = pltpu.SemaphoreType.DMA((PEERS,))
    kinds = [VMEM] * len(args)
    kinds[8] = ANY
    kinds[9] = ANY
    kinds[27] = ANY
    return pl.pallas_call(
        back_kernel,
        out_shape=(
            jax.ShapeDtypeStruct((S, W), BF),
            jax.ShapeDtypeStruct((3, S, W), BF),
            jax.ShapeDtypeStruct((PEERS, T, W), BF),
            jax.ShapeDtypeStruct((8, S), F32),
            jax.ShapeDtypeStruct((S, PAD), BF),
            jax.ShapeDtypeStruct((3, RANK, W), BF),
            jax.ShapeDtypeStruct((RANK, W), BF),
            jax.ShapeDtypeStruct((RANK, W), BF),
            jax.ShapeDtypeStruct((RANK, PAD), BF),
            jax.ShapeDtypeStruct((4 * RANK, D), BF),
        ),
        in_specs=kinds,
        out_specs=(VMEM,) * 10,
        scratch_shapes=[
            pltpu.VMEM((D, D), BF),
            pltpu.SemaphoreType.DMA((2 * PEERS,)),
            pltpu.VMEM((PEERS, T, W), BF),
            pltpu.VMEM((PEERS, T, W + PAD), BF),
            pltpu.VMEM((PEERS, T, W + PAD), BF),
            pltpu.VMEM((S, W), F32),
            pltpu.VMEM((S, W), F32),
            pltpu.VMEM((S, W), F32),
            pltpu.VMEM((8, S), F32),
            pltpu.VMEM((PEERS, 8, S), F32),
            pltpu.VMEM((S, PAD), BF),
            sems, sems, sems, sems, sems, sems,
            pltpu.VMEM((PEERS, S, W), BF),
            sems, sems,
        ],
        compiler_params=params(4, 62),
        cost_estimate=pl.CostEstimate(flops=4 * 10**10, bytes_accessed=10**7, transcendentals=0),
        name="back",
    )(*args)


GROUPS = 10


def input_kernel(
    pg, lcg, wq, bank, stat3, bgc, tokens, rinv, gain,
    picked, gdown, glift, growdown, gqkvup, goutdown, goutup, grup, flat,
    out, gin, glif, grout, gqkvdown, gqkvup_all, gout, goutup_all, grup_all, ginup, glower,
    w, wsem, own, sbuf, rbuf, inbox, fbuf, fsem,
    tall, thin, tallbuf, thinbuf, tallsum, thinsum, lowsum, mine, theirs,
    send, recv, send3, recv3, send4, recv4, send5, recv5, send6, recv6,
):
    c = lax.axis_index("col")
    r = lax.axis_index("row")
    barrier = greet()
    for n in range(1, 16):
        pl.semaphore_signal(
            barrier, inc=1, device_id={"row": lax.rem(r + n, 16)}, device_id_type=MESH
        )
    loads = [
        pltpu.make_async_copy(wq.at[:, T * k : T * k + T, :], w.at[k], wsem.at[k]) for k in range(3)
    ]
    for load in loads:
        load.start()
    flat_load = pltpu.make_async_copy(flat, fbuf, fsem)
    flat_load.start()
    tall[0 : 4 * RANK, :] = gdown[...]
    tall[4 * RANK : 6 * RANK, :] = glift[...]
    tall[6 * RANK : 10 * RANK, :] = growdown[...]
    thin[0 : 3 * RANK, :] = gqkvup[...]
    thin[3 * RANK : 4 * RANK, :] = goutdown[...]
    thin[4 * RANK : 5 * RANK, :] = goutup[...]
    thin[5 * RANK : 6 * RANK, 0:PAD] = grup[...]
    thin[5 * RANK : 6 * RANK, PAD:W] = jnp.zeros((RANK, PAD), BF)
    for load in loads:
        load.wait()
    pl.semaphore_wait(barrier, PEERS - 1 + 15)

    def row_copies(n):
        p = lax.rem(r + n, 16)
        where = {"row": p}
        return [
            pltpu.make_async_remote_copy(
                src_ref=tall.at[:, span(p * T, T)], dst_ref=tallbuf.at[r],
                send_sem=send4.at[n], recv_sem=recv4.at[n],
                device_id=where, device_id_type=MESH,
            ),
            pltpu.make_async_remote_copy(
                src_ref=thin, dst_ref=thinbuf.at[r], send_sem=send5.at[n], recv_sem=recv5.at[n],
                device_id=where, device_id_type=MESH,
            ),
        ]

    def row_arrivals(n):
        p = lax.rem(r + 16 - n, 16)
        where = {"row": p}
        return [
            pltpu.make_async_remote_copy(
                src_ref=tallbuf.at[p], dst_ref=tallbuf.at[p],
                send_sem=send4.at[n], recv_sem=recv4.at[n],
                device_id=where, device_id_type=MESH,
            ),
            pltpu.make_async_remote_copy(
                src_ref=thin, dst_ref=thinbuf.at[p], send_sem=send5.at[n], recv_sem=recv5.at[n],
                device_id=where, device_id_type=MESH,
            ),
        ]

    for n in range(1, 16):
        for copy in row_copies(n):
            copy.start()
    tallbuf[r] = tall[:, span(r * T, T)]
    thinbuf[r] = thin[...]
    swap_start(stat3, inbox, send3, recv3)
    for n in (4, 3, 5, 2, 6, 1, 7, 0):
        d = peer_of(n)
        wide = span(d * W, W)

        @pl.loop(0, 4)
        def _(i):
            rows = span(i * 256, 256)
            part = nt(lcg[rows, :], bank[wide, 0:PAD])
            for k in range(3):
                part += nt(pg[k, rows, :], w[k, pl.ds(2 * d, 2)].reshape(W, W))
            if n:
                sbuf[n, rows, :] = part.astype(BF)
            else:
                own[rows, :] = part

        if n:
            to_peer(sbuf.at[n], rbuf.at[n], send.at[n], recv.at[n], d).start()

    for n in range(1, 16):
        for copy in row_arrivals(n):
            copy.wait_recv()

    def summed(s, shape, read):
        return lax.fori_loop(
            0, 16, lambda q, acc: acc + picked[s, q] * read(q).astype(F32), jnp.zeros(shape, F32)
        )

    @pl.loop(0, SETS)
    def _(s):
        at = span(s * RANK, RANK)
        total = summed(s, (GROUPS * RANK, T), lambda q: tallbuf[q])
        for g in range(GROUPS):
            tallsum[g, at, :] = total[RANK * g : RANK * g + RANK, :]

    mine[...] = tallsum[6:9].astype(BF)
    theirs[c] = mine[...]
    for k in ORDER:
        to_peer(mine, theirs.at[c], send6.at[k], recv6.at[k], peer_of(k)).start()
    flat_load.wait()

    @pl.loop(0, SETS)
    def _(s):
        at = span(s * RANK, RANK)
        total = summed(s, (6 * RANK, W), lambda q: thinbuf[q])
        for g in range(6):
            thinsum[g, at, :] = total[RANK * g : RANK * g + RANK, :]
        for g in range(6):
            total = summed(s, (RANK, FF), lambda q: fbuf[q, RANK * g : RANK * g + RANK, :])
            if g < 4:
                ginup[g, at, :] = total
            else:
                lowsum[g - 4, at, :] = total

    for g in range(4):
        gin[g] = jnp.transpose(tallsum[g])
    for g in range(2):
        glif[g] = tallsum[4 + g]
        for m in range(FF // PAD):
            glower[g, PAD * m : PAD * m + PAD, :] = jnp.transpose(
                lowsum[g, :, PAD * m : PAD * m + PAD]
            )
    grout[...] = jnp.transpose(tallsum[9])
    for k in range(3):
        gqkvup_all[k] = thinsum[k]
    for m in range(2):
        gout[PAD * m : PAD * m + PAD, :] = jnp.transpose(thinsum[3, :, PAD * m : PAD * m + PAD])
    goutup_all[...] = thinsum[4]
    grup_all[...] = thinsum[5, :, 0:PAD]
    for k in ORDER:
        to_peer(mine, theirs.at[source_of(k)], send6.at[k], recv6.at[k], peer_of(k)).wait()
    for k in range(3):
        total = theirs[0, k].astype(F32)
        for p in range(1, PEERS):
            total += theirs[p, k].astype(F32)
        gqkvdown[k] = jnp.transpose(total)
    for n in range(1, 16):
        for copy in row_copies(n):
            copy.wait_send()
    dots = swap_finish(stat3, inbox, send3, recv3)
    for n in (4, 3, 5, 2, 6, 1, 7):
        to_peer(sbuf.at[n], rbuf.at[n], send.at[n], recv.at[n], peer_of(n)).wait()
    for i in range(4):
        rows = slice(256 * i, 256 * i + 256)
        column = rows_to_columns(dots[:, rows])[:, 0:1]
        total = own[rows, :]
        for n in range(1, PEERS):
            total += rbuf[n, rows, :].astype(F32)
        q = rinv[rows, 0:1]
        grad = bgc[rows, :].astype(F32) + q * (total * gain[...])
        out[rows, :] = grad - tokens[rows, :].astype(F32) * (q * q * column / D)


def to_input(*args):
    sems = pltpu.SemaphoreType.DMA((PEERS,))
    more = pltpu.SemaphoreType.DMA((16,))
    kinds = [VMEM] * len(args)
    kinds[2] = ANY
    kinds[9] = pl.BlockSpec(memory_space=pltpu.SMEM)
    kinds[17] = ANY
    square = (PAD, PAD)
    return pl.pallas_call(
        input_kernel,
        out_shape=tuple(
            jax.ShapeDtypeStruct(shape, F32)
            for shape in (
                (S, W), (4, *square), (2, *square), square, (3, *square), (3, PAD, W), (W, PAD),
                (PAD, W), square, (4, PAD, FF), (2, FF, PAD),
            )
        ),
        in_specs=kinds,
        out_specs=(VMEM,) * 11,
        scratch_shapes=[
            pltpu.VMEM((3, 16, T, W), BF),
            pltpu.SemaphoreType.DMA((3,)),
            pltpu.VMEM((S, W), F32),
            pltpu.VMEM((PEERS, S, W), BF),
            pltpu.VMEM((PEERS, S, W), BF),
            pltpu.VMEM((PEERS, 8, S), F32),
            pltpu.VMEM((16, 6 * RANK, FF), BF),
            pltpu.SemaphoreType.DMA,
            pltpu.VMEM((GROUPS * RANK, D), BF),
            pltpu.VMEM((6 * RANK, W), BF),
            pltpu.VMEM((16, GROUPS * RANK, T), BF),
            pltpu.VMEM((16, 6 * RANK, W), BF),
            pltpu.VMEM((GROUPS, *square), F32),
            pltpu.VMEM((6, PAD, W), F32),
            pltpu.VMEM((2, PAD, FF), F32),
            pltpu.VMEM((3, *square), BF),
            pltpu.VMEM((PEERS, 3, *square), BF),
            sems, sems, sems, sems, more, more, more, more, sems, sems,
        ],
        compiler_params=params(5, 56),
        cost_estimate=pl.CostEstimate(flops=5 * 10**10, bytes_accessed=10**7, transcendentals=0),
        name="input",
    )(*args)


def rope_tables():
    half = HEAD // 2
    frequency = (10000.0 ** (-(np.arange(half, dtype=np.float32) * 2.0) / HEAD)).astype(np.float32)
    angle = np.arange(S, dtype=np.float32)[:, None] * frequency[None, :]
    cosine, sine = np.cos(angle), np.sin(angle)
    return (
        np.concatenate([cosine, cosine], axis=1).astype(np.float32),
        np.concatenate([-sine, sine], axis=1).astype(np.float32),
    )


def body(
    tokens, cotangent, routes, adapter_set, attn_gain, mixer_gain, query_gain, key_gain,
    qkv_weight, qkv_down, qkv_up, out_weight, out_down, out_up,
    router_weight, router_down, router_up,
    expert_in, expert_in_down, expert_in_up, expert_out, expert_out_down, expert_out_up,
):
    c = lax.axis_index("col")
    start = adapter_set[0] * RANK

    out_up_pick = lax.dynamic_slice_in_dim(out_up, start, RANK, 0)
    out_down_pick = lax.dynamic_slice_in_dim(out_down, start, RANK, 1)
    pay0 = jnp.concatenate([tokens, out_down_pick.T, out_up_pick], axis=0)

    flag = jnp.broadcast_to(adapter_set.astype(BF)[:, None], (T, PAD))
    shard = jnp.concatenate(
        [
            qkv_weight.reshape(3 * T, W),
            jnp.concatenate([qkv_down[0], qkv_down[1]], axis=1),
            jnp.concatenate([qkv_down[2], router_down], axis=1),
            jnp.concatenate([jnp.pad(router_weight, ((0, 0), (64, 48))), flag], axis=1),
            out_weight.T,
        ],
        axis=0,
    )
    wq = lax.all_gather(shard, "row", axis=0)
    sets = wq[:, 5 * T, PAD].astype(F32)
    picked = (sets[None, :] == jnp.arange(SETS, dtype=F32)[:, None]).astype(F32)
    spot = jnp.arange(PAD, dtype=jnp.int32)
    rank = spot[None, :, None] - start
    picks = (
        (rank >= 0) & (rank < RANK)
        & (rank + RANK * jnp.arange(4, dtype=jnp.int32)[:, None, None] == spot[None, None, :])
    ).astype(BF)

    down = jnp.concatenate(
        [
            jnp.moveaxis(expert_out_up, 2, 0),
            jnp.moveaxis(expert_in_down.reshape(4, T, PAD), 0, 1),
        ],
        axis=1,
    ).reshape(T, 6, SETS, RANK)
    down = jnp.einsum(
        "dnsj,sr->rdnj", down, picked.astype(BF), preferred_element_type=F32
    ).astype(BF).reshape(16, T, 6 * RANK)
    ebank = jnp.concatenate(
        [
            down[:, :, 2 * RANK :], jnp.zeros((16, T, 16), BF), down[:, :, : 2 * RANK],
            jnp.zeros((16, T, 16), BF),
        ],
        axis=2,
    )

    qkv_up_pick = lax.dynamic_slice_in_dim(qkv_up, start, RANK, 1)
    up = jnp.concatenate(
        [jnp.pad(qkv_up_pick[k], ((RANK * k, PAD - RANK * k - RANK), (0, 0))) for k in range(3)],
        axis=1,
    )
    in_up_pick = lax.dynamic_slice_in_dim(expert_in_up, start, RANK, 2).reshape(4, RANK, FF)
    upin = jnp.stack(
        [jnp.pad(in_up_pick[n], ((RANK * n, PAD - RANK * n - RANK), (0, 0))) for n in range(4)]
    )
    lower_pick = lax.dynamic_slice_in_dim(expert_out_down, start, RANK, 2)
    ad = jnp.stack(
        [jnp.pad(lower_pick[e], ((0, 0), (80 + RANK * e, 32 - RANK * e))) for e in range(2)]
    )
    ru = jnp.pad(lax.dynamic_slice_in_dim(router_up, start, RANK, 0), ((48, 64), (64, 48)))
    routes_t = lax.dynamic_slice_in_dim(routes, c * T, T, 0)
    cosine, sine = rope_tables()

    normed, rinv, resid, extra, cot, po, pl0, pr0, xl, xr, xf = gather_tokens(
        pay0, attn_gain[None], cotangent, expert_in, expert_out
    )
    qg, kg = query_gain[None], key_gain[None]
    (
        att_t, att, q, k, v, qraw, kraw, cols, lat, bank, half, other,
        pl1, pr1, pf0, pf1, y0, yl, yr, yf,
    ) = attention(
        normed, wq, picks, up, qg, kg, cosine, sine,
        (po, pl0, pr0), (expert_out, xl, xr, xf),
    )
    pin = [expert_in, po, pl0, pl1, pr0, pr1, pf0, pf1]
    pout = [expert_out, y0, xl, yl, xr, yr, xf, yf]
    half, other = half.reshape(PEERS, S, W), other.reshape(PEERS, S, W)
    pay, state, prob, branch, lat_o = to_state(
        att_t, half, other, resid, extra, mixer_gain[None], bank, ru, routes_t
    )
    mixture, summed, xfull, gup, glow, glift, gdown = experts(
        pay, branch, cot, ebank, upin, ad, pin, pout
    )
    flat = jnp.concatenate([gup.reshape(4 * RANK, FF), glow.reshape(2 * RANK, FF)], axis=0)
    flat = lax.all_gather(flat, "row", axis=0)
    cot_t = lax.dynamic_slice_in_dim(cot, c * T, T, 1)
    mixed, pg, bgc, stat3, lcg, gqkvup, goutdown, goutup, grup, gtall = back(
        summed, state, prob, routes_t, bank, ru, mixer_gain[None], cot_t, half, other, extra,
        lat_o, q, k, v, att, cols, qraw, kraw, qg, kg, cosine, sine, up, lat, xfull, normed,
        mixture, tokens,
    )
    gain_mine = lax.dynamic_slice_in_dim(attn_gain, c * W, W, 0)[None]
    (
        tokens_grad, in_down_grad, lift_grad, router_down_grad, qkv_down_grad, qkv_up_grad,
        out_down_grad, out_up_grad, router_up_grad, in_up_grad, lower_grad,
    ) = to_input(
        pg, lcg, wq, bank, stat3, bgc.reshape(S, W), tokens, rinv, gain_mine,
        picked, gdown, glift.reshape(2 * RANK, D), gtall, gqkvup.reshape(3 * RANK, W),
        goutdown, goutup, grup, flat,
    )
    in_down_grad = in_down_grad.reshape(2, 2, T, PAD)
    in_up_grad = in_up_grad.reshape(2, 2, PAD, FF)
    router_up_grad = router_up_grad[:, 64:80]
    return (
        mixed, tokens_grad, qkv_down_grad, qkv_up_grad, out_down_grad, out_up_grad,
        router_down_grad, router_up_grad, in_down_grad, in_up_grad, lower_grad, lift_grad,
    )


def solution(mesh):
    in_specs = (
        P("row", "col"), P("row", "col"), P("row", None), P("row"), P(), P(), P("col"), P("col"),
        P(None, "row", "col"), P(None, "row", None), P(None, None, "col"),
        P("col", "row"), P("col", None), P(None, "col"),
        P("row", None), P("row", None), P(),
        P("col", None, "row", None), P("col", None, "row", None), P("col", None, None, None),
        P("col", None, "row"), P("col", None, None), P("col", None, "row"),
    )
    out_specs = (
        P("row", "col"), P("row", "col"), P(None, "row", None), P(None, None, "col"),
        P("col", None), P(None, "col"), P("row", None), P(),
        P("col", None, "row", None), P("col", None, None, None), P("col", None, None),
        P("col", None, "row"),
    )
    return jax.shard_map(body, mesh=mesh, in_specs=in_specs, out_specs=out_specs, check_vma=False)
```

```python
import functools

import jax
import jax.numpy as jnp
import numpy as np
from jax import lax
from jax.experimental import pallas as pl
from jax.experimental.pallas import tpu as pltpu
from jax.sharding import PartitionSpec as P

D = 2048
HEAD = 128
FF = 1024
RANK = 16
SETS = 8
S = 1024
W = 256
T = 128
PEERS = 8
PAD = 128
EPS = 1e-05
FACTOR = HEAD ** (-0.5)
F32 = jnp.float32
BF = jnp.bfloat16
MESH = pl.DeviceIdType.MESH
VMEM = pl.BlockSpec(memory_space=pltpu.VMEM)
ANY = pl.BlockSpec(memory_space=pl.ANY)

NN = (((1,), (0,)), ((), ()))
NT = (((1,), (1,)), ((), ()))
TN = (((0,), (0,)), ((), ()))


def nn(a, b):
    return lax.dot_general(a, b, NN, preferred_element_type=F32)


def nt(a, b):
    return lax.dot_general(a, b, NT, preferred_element_type=F32)


def tn(a, b):
    return lax.dot_general(a, b, TN, preferred_element_type=F32)


def lanes(rows):
    return lax.broadcasted_iota(jnp.int32, (rows, PAD), 1)


def span(start, size):
    return pl.ds(pl.multiple_of(start, size), size)


def params(collective=None, limit=62):
    return pltpu.CompilerParams(
        collective_id=collective,
        has_side_effects=collective is not None,
        vmem_limit_bytes=limit * 2**20,
    )


def greet():
    c = lax.axis_index("col")
    barrier = pltpu.get_barrier_semaphore()
    for k in range(1, PEERS):
        pl.semaphore_signal(
            barrier, inc=1, device_id={"col": lax.rem(c + k, PEERS)}, device_id_type=MESH
        )
    return barrier


def to_peer(src, dst, send, recv, peer):
    return pltpu.make_async_remote_copy(
        src_ref=src,
        dst_ref=dst,
        send_sem=send,
        recv_sem=recv,
        device_id={"col": peer},
        device_id_type=MESH,
    )


def peer_of(k):
    return lax.rem(lax.axis_index("col") + k, PEERS)


def source_of(k):
    return lax.rem(lax.axis_index("col") + PEERS - k, PEERS)


ORDER = (4, 1, 7, 5, 3, 2, 6)


PLACES = ((0, 0), (0, 1), (1, 0), (3, 0), (1, 1), (3, 1), (2, 0), (2, 1))
NEAR = ((0, 1), (1, 0), (3, 0))


def place(rel):
    c = lax.axis_index("col")
    return lax.rem(c // 4 + rel[1], 2) * 4 + lax.rem(lax.rem(c, 4) + rel[0], 4)


def greet_near():
    barrier = pltpu.get_barrier_semaphore()
    for rel in NEAR:
        pl.semaphore_signal(barrier, inc=1, device_id={"col": place(rel)}, device_id_type=MESH)
    return barrier


class Gather:
    MOVES = {
        "a0": ((0, 0), (0, 1), 0, (0, 1), 0),
        "a1": ((0, 0), (3, 0), 0, (1, 0), 2),
        "a2": ((0, 0), (1, 0), 0, (3, 0), 1),
        "b1": ((0, 1), (3, 1), 0, (1, 0), 4),
        "b2": ((0, 1), (1, 1), 0, (3, 0), 3),
        "c1": ((3, 0), (2, 0), 1, (1, 0), 5),
        "c2": ((1, 0), (2, 0), 2, (3, 0), 6),
        "d1": ((3, 1), (2, 1), 1, (1, 0), 7),
        "d2": ((1, 1), (2, 1), 2, (3, 0), 8),
    }
    FROM = (
        ((0, 1), 0), ((1, 0), 0), ((3, 0), 0), ((1, 1), 0), ((3, 1), 0),
        ((2, 0), 1), ((2, 0), 2), ((2, 1), 1), ((2, 1), 2),
    )

    def __init__(self, here, there, rows, send, recv, axis="col"):
        self.here, self.there, self.rows, self.send, self.recv = here, there, rows, send, recv
        self.axis = axis

    def copy(self, src, dst, send, recv, to):
        to = place(to) if self.axis == "col" else row_place((to[1], to[0]))
        return pltpu.make_async_remote_copy(
            src_ref=src, dst_ref=dst, send_sem=send, recv_sem=recv,
            device_id={self.axis: to}, device_id_type=MESH,
        )

    def part(self, which):
        half = self.rows // 2
        return ((0, self.rows), (0, half), (half, half))[which]

    def move(self, name):
        src, dst, which, to, arrives = self.MOVES[name]
        lo, n = self.part(which)
        return self.copy(
            self.here(src, lo, n), self.there(src, dst, lo, n),
            self.send.at[list(self.MOVES).index(name)], self.recv.at[arrives], to,
        )

    def start(self, *names):
        for name in names:
            self.move(name).start()

    def wait(self, *arrivals):
        for i in arrivals:
            rel, which = self.FROM[i]
            lo, n = self.part(which)
            ref = self.here(rel, lo, n)
            self.copy(ref, ref, self.send.at[0], self.recv.at[i], (0, 1)).wait_recv()

    def sent(self):
        for name in self.MOVES:
            self.move(name).wait_send()


def row_place(shift):
    r = lax.axis_index("row")
    plane = lax.rem(r // 8 + shift[0], 2)
    spot = lax.rem(lax.rem(r, 8) // 2 + shift[1], 4)
    return plane * 8 + spot * 2 + lax.rem(r, 2)


PLANE, UP, DOWN, FAR = (1, 0), (0, 1), (0, 3), (0, 2)


def greet_row(barrier, *shifts):
    for shift in shifts:
        pl.semaphore_signal(
            barrier, inc=1, device_id={"row": row_place(shift)}, device_id_type=MESH
        )


def along(src, dst, send, recv, shift):
    return pltpu.make_async_remote_copy(
        src_ref=src, dst_ref=dst, send_sem=send, recv_sem=recv,
        device_id={"row": row_place(shift)}, device_id_type=MESH,
    )


class RowGather:
    def __init__(self, shard, out, rows, sems):
        self.send, self.recv, self.xsend, self.xrecv, self.sem = sems
        self.shard, self.out, self.rows = shard, out, rows
        self.ring = Gather(
            self.part, lambda src, dst, lo, n: out.at[self.at(src), lo : lo + n],
            rows, self.send, self.recv, "row",
        )
        self.keep = pltpu.make_async_copy(shard, out.at[lax.axis_index("row")], self.sem)

    def at(self, rel):
        return row_place((rel[1], rel[0]))

    def part(self, rel, lo, n):
        if rel == (0, 0):
            return self.shard.at[lo : lo + n]
        return self.out.at[self.at(rel), lo : lo + n]

    def across(self, rel):
        r = lax.axis_index("row")
        n = PLACES.index(rel)
        return pltpu.make_async_remote_copy(
            src_ref=self.part(rel, 0, self.rows), dst_ref=self.out.at[self.at(rel)],
            send_sem=self.xsend.at[n], recv_sem=self.xrecv.at[n],
            device_id={"row": r + 1 - 2 * lax.rem(r, 2)}, device_id_type=MESH,
        )

    def start(self):
        self.ring.start("a0", "a1", "a2")
        self.keep.start()
        self.across((0, 0)).start()

    def step(self, i):
        waits, sends = (
            ((0,), ("b1", "b2")), ((1, 2), ("c1", "c2")), ((3, 4), ("d1", "d2")), ((5, 6, 7, 8), ())
        )[i]
        places = (((0, 1),), ((1, 0), (3, 0)), ((1, 1), (3, 1)), ((2, 0), (2, 1)))[i]
        self.ring.wait(*waits)
        self.ring.start(*sends)
        for rel in places:
            self.across(rel).start()

    def finish(self):
        self.ring.sent()
        self.keep.wait()
        r = lax.axis_index("row")
        for rel in PLACES:
            self.across(rel).wait_send()
        for rel in PLACES:
            n = PLACES.index(rel)
            q = self.at(rel) + 1 - 2 * lax.rem(r, 2)
            pltpu.make_async_remote_copy(
                src_ref=self.part(rel, 0, self.rows), dst_ref=self.out.at[q],
                send_sem=self.xsend.at[n], recv_sem=self.xrecv.at[n],
                device_id={"row": r + 1 - 2 * lax.rem(r, 2)}, device_id_type=MESH,
            ).wait_recv()


def row_sems():
    sems = pltpu.SemaphoreType.DMA
    return [sems((9,)), sems((9,)), sems((PEERS,)), sems((PEERS,)), sems]


def greet_partner(barrier):
    r = lax.axis_index("row")
    pl.semaphore_signal(
        barrier, inc=1, device_id={"row": r + 1 - 2 * lax.rem(r, 2)}, device_id_type=MESH
    )


def tokens_kernel(
    pay, gain, cot, win, wout, shard,
    normed, rinv, resid, extra, cots, wo, wl, wr, ql, qr, qf, qo, wq,
    buf, send, recv, send2, recv2, sem, send3, recv3, *sems,
):
    c = lax.axis_index("col")
    barrier = greet_near()
    greet_row(barrier, PLANE, UP, DOWN, FAR)
    greet_partner(barrier)
    rows_in = RowGather(shard, wq, shard.shape[0], sems)
    weights = [
        along(src, dst, send3.at[n], recv3.at[n], shift)
        for n, (src, dst, shift) in enumerate(
            (
                (win, wo, PLANE), (wout, qo, PLANE), (win, wl, UP), (win, wr, DOWN),
                (wout, ql, UP), (wout, qr, DOWN), (wout, qf, FAR),
            )
        )
    ]
    keep = pltpu.make_async_copy(cot, cots.at[c], sem)
    keep.start()
    buf[c] = pay[...]
    pl.semaphore_wait(barrier, 8)
    ring = Gather(
        lambda rel, lo, n: buf.at[place(rel), lo : lo + n],
        lambda src, dst, lo, n: buf.at[place(src), lo : lo + n],
        pay.shape[0], send, recv,
    )

    def cot_part(rel, lo, n):
        if rel == (0, 0):
            return cot.at[lo : lo + n]
        return cots.at[place(rel), lo : lo + n]

    second = Gather(
        cot_part, lambda src, dst, lo, n: cots.at[place(src), lo : lo + n], S, send2, recv2
    )
    ring.start("a0", "a1", "a2")
    rows_in.start()
    for copy in weights[:2]:
        copy.start()
    ring.wait(0)
    ring.start("b1", "b2")
    rows_in.step(0)
    ring.wait(1, 2)
    ring.start("c1", "c2")
    rows_in.step(1)
    for copy in weights[2:]:
        copy.start()
    ring.wait(3, 4)
    ring.start("d1", "d2")
    second.start("a0", "a1", "a2")
    ring.wait(5, 6, 7, 8)
    extra[...] = jnp.zeros_like(extra)
    for p in range(PEERS):
        resid[p] = buf[p, span(c * T, T), :]
        extra[p, 0 : 2 * RANK, :] = buf[p, S : S + 2 * RANK, :]

    @pl.loop(0, S // 64)
    def _(i):
        rows = span(i * 64, 64)
        total = jnp.zeros((64, 1), F32)
        for p in range(PEERS):
            x = buf[p, rows, :].astype(F32)
            total += jnp.sum(x * x, axis=1, keepdims=True)
        r = lax.rsqrt(total / D + EPS)
        for p in range(PEERS):
            x = buf[p, rows, :].astype(F32)
            normed[rows, W * p : W * p + W] = (x * r * gain[:, W * p : W * p + W]).astype(BF)
        rinv[rows, :] = jnp.broadcast_to(r, (64, PAD))

    rows_in.step(2)
    second.wait(0)
    second.start("b1", "b2")
    second.wait(1, 2)
    second.start("c1", "c2")
    rows_in.step(3)
    second.wait(3, 4)
    second.start("d1", "d2")
    second.wait(5, 6, 7, 8)
    ring.sent()
    second.sent()
    keep.wait()
    rows_in.finish()
    for copy in weights:
        copy.wait()


def gather_tokens(pay, gain, cot, win, wout, shard):
    rows = pay.shape[0]
    return pl.pallas_call(
        tokens_kernel,
        out_shape=(
            jax.ShapeDtypeStruct((S, D), BF),
            jax.ShapeDtypeStruct((S, PAD), F32),
            jax.ShapeDtypeStruct((PEERS, T, W), BF),
            jax.ShapeDtypeStruct((PEERS, PAD, W), BF),
            jax.ShapeDtypeStruct((PEERS, S, W), BF),
        )
        + (jax.ShapeDtypeStruct(win.shape, BF),) * 3
        + (jax.ShapeDtypeStruct(wout.shape, BF),) * 4
        + (jax.ShapeDtypeStruct((16, *shard.shape), BF),),
        in_specs=[VMEM, VMEM, ANY, ANY, ANY, ANY],
        out_specs=(VMEM, VMEM, VMEM, VMEM) + (ANY,) * 9,
        scratch_shapes=[
            pltpu.VMEM((PEERS, rows, W), BF),
            pltpu.SemaphoreType.DMA((9,)),
            pltpu.SemaphoreType.DMA((9,)),
            pltpu.SemaphoreType.DMA((9,)),
            pltpu.SemaphoreType.DMA((9,)),
            pltpu.SemaphoreType.DMA,
            pltpu.SemaphoreType.DMA((7,)),
            pltpu.SemaphoreType.DMA((7,)),
            *row_sems(),
        ],
        compiler_params=params(1, 63),
        cost_estimate=pl.CostEstimate(flops=5 * 10**10, bytes_accessed=10**7, transcendentals=0),
        name="tokens",
    )(pay, gain, cot, win, wout, shard)


def columns_to_rows(first, second):
    lane = lanes(first.shape[0])
    tile = jnp.where(lane == 0, first, jnp.where(lane == 1, second, 0.0))
    return jnp.transpose(tile)[0:8, :]


def rows_to_columns(rows):
    padded = jnp.concatenate([rows, jnp.zeros((PAD - 8, rows.shape[1]), F32)], axis=0)
    return jnp.transpose(padded)


def swap_start(stat, inbox, send, recv):
    c = lax.axis_index("col")
    for k in ORDER:
        to_peer(stat, inbox.at[c], send.at[k], recv.at[k], peer_of(k)).start()


def swap_finish(stat, inbox, send, recv):
    for k in ORDER:
        to_peer(stat, inbox.at[source_of(k)], send.at[k], recv.at[k], peer_of(k)).wait()
    total = stat[...]
    for k in range(1, PEERS):
        total += inbox[source_of(k)]
    return total


def attention_kernel(
    normed_in, wq, picks, up, qgain, kgain, cosine, sine,
    p0, po, pl0, pr0, x0, xo, xl, xr, xf,
    att_t, att, qo, ko, vo, qraw, kraw, cols, lat, bank, wmine, wother,
    pl1, pr1, pf0, pf1, yl, yr, yf, *rest,
):
    swapped, rest = rest[0:9], rest[9:]
    (
        w, wsem, stat, inbox, ssem, rsem, asend, arecv, osend, orecv, xsend, xrecv, psend, precv,
        normed, nsem, esend, erecv,
    ) = rest
    c = lax.axis_index("col")
    side = lax.rem(lax.axis_index("row"), 2)
    partner = lax.axis_index("row") + 1 - 2 * side
    barrier = greet()
    pl.semaphore_signal(barrier, inc=1, device_id={"row": partner}, device_id_type=MESH)
    greet_row(barrier, PLANE, UP, DOWN)
    first, last = pl.ds(0, 1), pl.ds(1, 1)
    weights = [
        along(src, dst, psend.at[n], precv.at[n], shift)
        for n, (src, dst, shift) in enumerate(
            (
                (po, pl1, UP), (po, pr1, DOWN),
                (pl0.at[first], pf0.at[first], UP), (pr0.at[last], pf0.at[last], DOWN),
                (xl, yl, PLANE), (xr, yr, PLANE), (xf, yf, PLANE),
                (pl1.at[first], pf1.at[first], UP), (pr1.at[last], pf1.at[last], DOWN),
            )
        )
    ]

    early = [
        pltpu.make_async_remote_copy(
            src_ref=src, dst_ref=dst, send_sem=esend.at[n], recv_sem=erecv.at[n],
            device_id={"row": partner}, device_id_type=MESH,
        )
        for n, (src, dst) in enumerate(zip((p0, po, pl0, pr0, x0, xo, xl, xr, xf), swapped))
    ]
    fetch = pltpu.make_async_copy(normed_in, normed, nsem)
    fetch.start()

    def out_part(rel, lo, n):
        if rel == (0, 0):
            return wq.at[pl.ds(8 * side + lo, n), 6 * T : 7 * T, :]
        return wmine.at[place(rel), lo : lo + n]

    ring = Gather(
        out_part, lambda src, dst, lo, n: wmine.at[place(src), lo : lo + n], 8, osend, orecv
    )

    def across(rel):
        n = PLACES.index(rel)
        return pltpu.make_async_remote_copy(
            src_ref=out_part(rel, 0, 8), dst_ref=wother.at[place(rel)],
            send_sem=xsend.at[n], recv_sem=xrecv.at[n],
            device_id={"row": partner}, device_id_type=MESH,
        )

    keep = pltpu.make_async_copy(out_part((0, 0), 0, 8), wmine.at[c], wsem.at[6])
    keep.start()
    loads = [
        pltpu.make_async_copy(
            wq.at[:, T * k : T * k + T, :], w.at[:, :, W * k : W * k + W], wsem.at[k]
        )
        for k in range(6)
    ]
    for load in loads:
        load.start()
    pl.semaphore_wait(barrier, PEERS + 3)
    ring.start("a0", "a1", "a2")
    for copy in weights[:7]:
        copy.start()
    for copy in early:
        copy.start()
    across((0, 0)).start()
    for load in loads:
        load.wait()
    fetch.wait()

    for i in range(4):
        tile = w[4 * i : 4 * i + 4, :, 3 * W :].reshape(4 * T, 3 * W)
        chosen = tile[:, 2 * W : 2 * W + PAD].astype(F32)
        for n in range(4):
            chosen += nn(tile[:, PAD * n : PAD * n + PAD], picks[n])
        bank[4 * T * i : 4 * T * i + 4 * T, :] = chosen.astype(BF)

    blocks = 4
    rows_of = S // blocks
    lane = lanes(rows_of)
    for i in range(blocks):
        rows = slice(i * rows_of, (i + 1) * rows_of)
        x = normed[rows, :]
        code = jnp.where(lane < 3 * RANK, nn(x, bank[...]), 0.0).astype(BF)
        lat[rows, :] = code
        parts = nn(x, w[:, :, 0 : 3 * W].reshape(D, 3 * W)) + nn(code, up[...])
        first_part, second_part = parts[:, 0:W], parts[:, W : 2 * W]
        qraw[rows, :] = first_part
        kraw[rows, :] = second_part
        vo[rows, :] = parts[:, 2 * W :].astype(BF)
        stat[:, rows] = columns_to_rows(
            jnp.sum(first_part * first_part, axis=1, keepdims=True),
            jnp.sum(second_part * second_part, axis=1, keepdims=True),
        )
    swap_start(stat, inbox, ssem, rsem)
    ring.wait(0)
    ring.start("b1", "b2")
    ring.wait(1, 2)
    ring.start("c1", "c2")
    for rel in NEAR:
        across(rel).start()
    ring.wait(3, 4)
    ring.start("d1", "d2")
    across((1, 1)).start()
    across((3, 1)).start()
    weights[0].wait_recv()
    weights[1].wait_recv()
    weights[7].start()
    weights[8].start()
    total = swap_finish(stat, inbox, ssem, rsem)
    scale = lax.rsqrt(total / D + EPS)
    for i in range(blocks):
        rows = slice(i * rows_of, (i + 1) * rows_of)
        column = rows_to_columns(scale[:, rows])
        cols[rows, :] = column
        for index, (raw, gain, out) in enumerate(((qraw, qgain, qo), (kraw, kgain, ko))):
            for h in range(2):
                feats = slice(HEAD * h, HEAD * h + HEAD)
                x = raw[rows, feats] * column[:, index : index + 1] * gain[:, feats]
                y = x * cosine[rows, :] + pltpu.roll(x, HEAD // 2, 1) * sine[rows, :]
                out[rows, feats] = y.astype(BF)
    for i in range(blocks):
        rows = slice(i * rows_of, (i + 1) * rows_of)
        seen = (i + 1) * rows_of
        allowed = lax.broadcasted_iota(jnp.int32, (rows_of, seen), 1) <= (
            lax.broadcasted_iota(jnp.int32, (rows_of, seen), 0) + i * rows_of
        )
        logs = []
        for h in range(2):
            feats = slice(HEAD * h, HEAD * h + HEAD)
            score = nt(qo[rows, feats], ko[0:seen, feats]) * FACTOR
            score = jnp.where(allowed, score, -1e30)
            top = jnp.max(score, axis=1, keepdims=True)
            weight = jnp.exp(score - top)
            norm = jnp.sum(weight, axis=1, keepdims=True)
            attend = (weight * (1.0 / norm)).astype(BF)
            att[rows, feats] = nn(attend, vo[0:seen, feats]).astype(BF)
            logs.append(top + jnp.log(norm))
        cols[rows, :] = jnp.where(
            lane == 2, logs[0], jnp.where(lane == 3, logs[1], cols[rows, :])
        )
        for p in (2 * i, 2 * i + 1):
            mine = slice(T * p, T * p + T)

            @pl.when(c != p)
            def _():
                to_peer(att.at[mine], att_t.at[c], asend.at[p], arecv.at[c], p).start()

            @pl.when(c == p)
            def _():
                att_t[p] = att[mine, :]

    ring.wait(5, 6, 7, 8)
    across((2, 0)).start()
    across((2, 1)).start()
    for p in range(PEERS):

        @pl.when(c != p)
        def _():
            to_peer(
                att.at[T * p : T * p + T], att_t.at[p], asend.at[p], arecv.at[p], p
            ).wait()

    ring.sent()
    keep.wait()
    for rel in PLACES:
        across(rel).wait()
    weights[0].wait_send()
    weights[1].wait_send()
    for copy in weights[2:]:
        copy.wait()
    for copy in early:
        copy.wait()


def attention(normed, wq, picks, up, qgain, kgain, cosine, sine, inner, outer):
    full = jax.ShapeDtypeStruct((S, W), BF)
    wide = jax.ShapeDtypeStruct((S, W), F32)
    return pl.pallas_call(
        attention_kernel,
        out_shape=(
            jax.ShapeDtypeStruct((PEERS, T, W), BF),
            full, full, full, full, wide, wide,
            jax.ShapeDtypeStruct((S, PAD), F32),
            jax.ShapeDtypeStruct((S, PAD), BF),
            jax.ShapeDtypeStruct((D, PAD), BF),
            jax.ShapeDtypeStruct((PEERS, 8, T, W), BF),
            jax.ShapeDtypeStruct((PEERS, 8, T, W), BF),
        )
        + (jax.ShapeDtypeStruct(inner[0].shape, BF),) * 4
        + (jax.ShapeDtypeStruct(outer[0].shape, BF),) * 3
        + (jax.ShapeDtypeStruct(inner[0].shape, BF),) * 4
        + (jax.ShapeDtypeStruct(outer[0].shape, BF),) * 5,
        in_specs=[ANY, ANY, VMEM, VMEM, VMEM, VMEM, VMEM, VMEM] + [ANY] * 9,
        out_specs=(VMEM,) * 10 + (ANY,) * 18,
        scratch_shapes=[
            pltpu.VMEM((16, T, 6 * W), BF),
            pltpu.SemaphoreType.DMA((7,)),
            pltpu.VMEM((8, S), F32),
            pltpu.VMEM((PEERS, 8, S), F32),
            pltpu.SemaphoreType.DMA((PEERS,)),
            pltpu.SemaphoreType.DMA((PEERS,)),
            pltpu.SemaphoreType.DMA((PEERS,)),
            pltpu.SemaphoreType.DMA((PEERS,)),
            pltpu.SemaphoreType.DMA((9,)),
            pltpu.SemaphoreType.DMA((9,)),
            pltpu.SemaphoreType.DMA((PEERS,)),
            pltpu.SemaphoreType.DMA((PEERS,)),
            pltpu.SemaphoreType.DMA((9,)),
            pltpu.SemaphoreType.DMA((9,)),
            pltpu.VMEM((S, D), BF),
            pltpu.SemaphoreType.DMA,
            pltpu.SemaphoreType.DMA((9,)),
            pltpu.SemaphoreType.DMA((9,)),
        ],
        compiler_params=params(2, 63),
        cost_estimate=pl.CostEstimate(flops=3 * 10**10, bytes_accessed=10**7, transcendentals=0),
        name="attention",
    )(normed, wq, picks, up, qgain, kgain, cosine, sine, *inner, *outer)


def load_out(mine, other, wo, sem):
    half = lax.rem(lax.axis_index("row"), 2)
    copies = []
    for index, (src, side) in enumerate(((mine, half), (other, 1 - half))):
        for p in range(PEERS):
            copies.append(
                pltpu.make_async_copy(
                    src.at[p],
                    wo.at[span(side * (D // 2), D // 2), W * p : W * p + W],
                    sem.at[index * PEERS + p],
                )
            )
    return copies


def member_of(routes, rows):
    lane = lanes(rows)
    found = lane == routes[:, 0:1] + 64
    for j in range(1, 8):
        found = found | (lane == routes[:, j : j + 1] + 64)
    return found


def state_kernel(
    att_t, mine, other, resid, extra, gain, bank, ru, routes,
    pay, state, prob_out, branch, lat_out,
    wo, sem,
):
    loads = load_out(mine, other, wo, sem)
    for load in loads:
        load.start()
    lane = lanes(T)
    lat = jnp.zeros((T, PAD), F32)
    for p in range(PEERS):
        lat += nt(att_t[p], extra[p])
    lat = jnp.where(lane < RANK, lat, 0.0)
    lat_out[...] = lat
    moved = pltpu.roll(lat, RANK, 1).astype(BF)
    x = jnp.concatenate([att_t[p] for p in range(PEERS)], axis=1)
    for load in loads:
        load.wait()
    total = jnp.zeros((T, 1), F32)
    for p in range(PEERS):
        feats = slice(W * p, W * p + W)
        part = nt(x, wo[feats, :]) + nn(moved, extra[p])
        branch[:, feats] = part.astype(BF)
        st = resid[p].astype(F32) + part
        state[:, feats] = st
        total += jnp.sum(st * st, axis=1, keepdims=True)
    r = lax.rsqrt(total / D + EPS)
    first = jnp.zeros((T, PAD), F32)
    for p in range(PEERS):
        feats = slice(W * p, W * p + W)
        m = (state[:, feats] * r * gain[:, feats]).astype(BF)
        pay[:, feats] = m
        first += nn(m, bank[feats, 0:PAD])
    code = jnp.where((lane >= 48) & (lane < 64), first, 0.0).astype(BF)
    valid = (lane >= 64) & (lane < 80)
    logits = jnp.where(valid, first + nn(code, ru[...]), -1e30)
    shifted = jnp.where(valid, jnp.exp(logits - jnp.max(logits, axis=1, keepdims=True)), 0.0)
    prob = shifted / jnp.sum(shifted, axis=1, keepdims=True)
    prob_out[...] = prob
    gate = jnp.where(member_of(routes, T), prob, 0.0)
    high = gate.astype(BF).astype(F32)
    low = pltpu.roll(gate - high, RANK, 1)
    pay[:, D:] = jnp.where(lane < 64, code.astype(F32), jnp.where(lane < 80, high, low)).astype(BF)


def to_state(att_t, mine, other, resid, extra, gain, bank, ru, routes):
    return pl.pallas_call(
        state_kernel,
        out_shape=(
            jax.ShapeDtypeStruct((T, D + PAD), BF),
            jax.ShapeDtypeStruct((T, D), F32),
            jax.ShapeDtypeStruct((T, PAD), F32),
            jax.ShapeDtypeStruct((T, D), BF),
            jax.ShapeDtypeStruct((T, PAD), F32),
        ),
        in_specs=[VMEM, ANY, ANY, VMEM, VMEM, VMEM, VMEM, VMEM, VMEM],
        out_specs=(VMEM,) * 5,
        scratch_shapes=[pltpu.VMEM((D, D), BF), pltpu.SemaphoreType.DMA((2 * PEERS,))],
        compiler_params=params(None, 63),
        cost_estimate=pl.CostEstimate(flops=10**10, bytes_accessed=10**7, transcendentals=0),
        name="state",
    )(att_t, mine, other, resid, extra, gain, bank, ru, routes)


EARLY_IN, LATE_IN = (0, 1, 2, 4), (3, 5, 6, 7)
EARLY_OUT, LATE_OUT = (0, 1, 2, 4, 6), (3, 5, 7)
SHIFTS = ((0, 0), (1, 0), (0, 3), (1, 3), (0, 1), (1, 1), (0, 2), (1, 2))
CHUNK = 256
TILE = 512
STEPS = (1, 2, 3)
LAST = 0


def expert_kernel(*refs):
    pay, branch, cot, ebank, upin, ad = refs[0:6]
    pin, pout, ein, eout = refs[6:14], refs[14:22], refs[22:26], refs[26:31]
    refs = refs[9:]
    mixed, summed, xout, gup, glow, glift, gdown = refs[22:29]
    (xfull, win, wd, cbuf, obuf, rbuf, a1, act, hid, vg, gg, ug, mix, xacc,
     aup, alow, alift, adown,
     lsem, csend, crecv, csem, send1, recv1, send2, recv2, xsem, mbank, bsend, brecv, esem) = refs[29:]
    c = lax.axis_index("col")
    r = lax.axis_index("row")
    half = lax.rem(r, 2)
    partner = r + 1 - 2 * half
    barrier = greet()

    def offset(shift, side):
        plane = lax.rem(r // 8 + shift[0], 2)
        place = lax.rem(lax.rem(r, 8) // 2 + shift[1], 4)
        return (plane * 8 + place * 2 + side) * T

    def inner(i, src, side):
        return (src, win.at[:, :, span(offset(SHIFTS[i], side), T), :], 2 * i)

    def outer(i, src, side):
        return (src, wd.at[:, :, span(offset(SHIFTS[i], side), T)], 2 * i + 1)

    def across(side):
        late = [inner(i, pin[i], side) for i in LATE_IN]
        late += [outer(i, pout[i], side) for i in LATE_OUT]
        return [
            pltpu.make_async_remote_copy(
                src_ref=src, dst_ref=dst, send_sem=csend.at[n], recv_sem=crecv.at[n],
                device_id={"row": partner}, device_id_type=MESH,
            )
            for src, dst, n in late
        ]

    def local():
        every = [inner(i, pin[i], half) for i in range(8)]
        every += [outer(i, pout[i], half) for i in range(8)]
        copies = [pltpu.make_async_copy(src, dst, lsem.at[n]) for src, dst, n in every]
        every = [inner(i, src, 1 - half) for i, src in zip(EARLY_IN, ein)]
        every += [outer(i, src, 1 - half) for i, src in zip(EARLY_OUT, eout)]
        copies += [pltpu.make_async_copy(src, dst, esem.at[n]) for src, dst, n in every]
        return copies

    sources = [place(rel) for rel in PLACES]

    def source(step, t):
        chosen = sources[2 * LAST + t]
        for j in range(3):
            chosen = jnp.where(step == j, sources[2 * STEPS[j] + t], chosen)
        return chosen

    def cot_copies(step, slot):
        return [
            pltpu.make_async_copy(
                cot.at[:, span(source(step, t) * T, T), :],
                cbuf.at[slot, :, T * t : T * t + T, :],
                csem.at[2 * slot + t],
            )
            for t in range(2)
        ]

    ring = Gather(
        lambda rel, lo, n: xfull.at[pl.ds(T * PLACES.index(rel) + lo, n)],
        lambda src, dst, lo, n: xfull.at[pl.ds(T * PLACES.index(dst) + lo, n)],
        T, send1, recv1,
    )
    for n in range(1, 16):
        pl.semaphore_signal(
            barrier, inc=1, device_id={"row": lax.rem(r + n, 16)}, device_id_type=MESH
        )

    def bank_copy(n):
        q = lax.rem(r + n, 16)
        return pltpu.make_async_remote_copy(
            src_ref=ebank.at[q], dst_ref=mbank.at[r], send_sem=bsend.at[n], recv_sem=brecv.at[n],
            device_id={"row": q}, device_id_type=MESH,
        )

    def bank_arrival(n):
        q = lax.rem(r + 16 - n, 16)
        return pltpu.make_async_remote_copy(
            src_ref=ebank.at[q], dst_ref=mbank.at[q], send_sem=bsend.at[n], recv_sem=brecv.at[n],
            device_id={"row": q}, device_id_type=MESH,
        )

    def bank(at):
        return mbank[at // T : (at + TILE) // T].reshape(TILE, PAD)

    def whole_bank():
        return mbank[...].reshape(D, PAD)

    xfull[0:T, :] = pay[...]
    mbank[r] = ebank[r]
    pl.semaphore_wait(barrier, PEERS + 14)
    ring.start("a0", "a1", "a2")
    for n in range(1, 16):
        bank_copy(n).start()
    for copy in across(half):
        copy.start()
    for copy in local():
        copy.start()
    for copy in cot_copies(0, 0):
        copy.start()
    aup[...] = jnp.zeros_like(aup)
    alow[...] = jnp.zeros_like(alow)
    alift[...] = jnp.zeros_like(alift)
    adown[...] = jnp.zeros_like(adown)
    lane = lanes(CHUNK)
    ring.wait(0)
    ring.start("b1", "b2")
    ring.wait(1, 2)
    ring.start("c1", "c2")
    for n in range(1, 16):
        bank_arrival(n).wait_recv()
    for n in range(1, 16):
        bank_copy(n).wait_send()
    for copy in local():
        copy.wait()
    for copy in across(half):
        copy.wait_send()
    for copy in across(1 - half):
        copy.wait_recv()

    def chunk(j, carry):
        rows = span(lax.rem(j + STEPS[0], 4) * CHUNK, CHUNK)
        slot = lax.rem(j, 2)

        @pl.when(j == 1)
        def _():
            ring.wait(3, 4)
            ring.start("d1", "d2")

        @pl.when(j == 2)
        def _():
            ring.wait(5, 6, 7, 8)

        for copy in cot_copies(j, slot):
            copy.wait()

        @pl.when(j < 3)
        def _():
            for copy in cot_copies(j + 1, 1 - slot):
                copy.start()

        mix[...] = jnp.zeros_like(mix)

        @pl.when(j == 3)
        def _():
            mix[0:T, :] = branch[...].astype(F32)

        extras = xfull[rows, D : D + PAD].astype(F32)
        inlat = nn(xfull[rows, 0:D], whole_bank()).astype(BF)
        gate_grads = []
        ilg_total = jnp.zeros((CHUNK, PAD), F32)
        for e in range(2):
            spot = 64 + 2 * c + e
            gate = jnp.sum(
                jnp.where((lane == spot) | (lane == spot + RANK), extras, 0.0),
                axis=1, keepdims=True,
            )

            for f in range(FF // TILE):
                fs = slice(f * TILE, f * TILE + TILE)
                x = xfull[rows, 0:D]
                g = nn(x, win[e, 0, :, fs]) + nn(inlat, upin[2 * e, :, fs])
                u = nn(x, win[e, 1, :, fs]) + nn(inlat, upin[2 * e + 1, :, fs])
                sg = 1.0 / (1.0 + jnp.exp(-g))
                silu = g * sg
                act[:, fs] = silu
                a1[:, fs] = u * sg * (1.0 + g * (1.0 - sg))
                hid[:, fs] = (silu * u).astype(BF)

            dl = nn(hid[...], ad[e]).astype(BF)

            gsum = jnp.zeros((CHUNK, 1), F32)
            for d in range(D // TILE):
                ds = slice(d * TILE, d * TILE + TILE)
                ev = nn(hid[...], wd[e, :, ds]) + nt(dl, bank(d * TILE))
                halves = [cbuf[slot, 2 * d + m] for m in range(TILE // W)]
                ct = jnp.concatenate(halves, axis=1).astype(F32)
                vg[:, ds] = (ct * gate).astype(BF)
                total = mix[:, ds] + ev * gate
                if e == 0:
                    mix[:, ds] = total
                else:
                    for t in range(2):
                        for m in range(TILE // W):
                            mixed[2 * d + m, span(source(j, t) * T, T), :] = total[
                                T * t : T * t + T, W * m : W * m + W
                            ].astype(BF)
                gsum += jnp.sum(ev * ct, axis=1, keepdims=True)
            gate_grads.append(gsum)
            low = 80 + RANK * e
            dlg = jnp.where(
                (lane >= low) & (lane < low + RANK), nn(vg[...], whole_bank()), 0.0
            ).astype(BF)

            for f in range(FF // TILE):
                fs = slice(f * TILE, f * TILE + TILE)
                hg = nt(vg[...], wd[e, fs, :]) + nt(dlg, ad[e, fs, :])
                gg[:, fs] = (hg * a1[:, fs]).astype(BF)
                ug[:, fs] = (hg * act[:, fs]).astype(BF)

            ilg32 = nt(gg[...], upin[2 * e]) + nt(ug[...], upin[2 * e + 1])
            ilg_total += ilg32
            ilg = ilg32.astype(BF)

            for d in range(D // TILE):
                ds = slice(d * TILE, d * TILE + TILE)
                t = (
                    nt(gg[...], win[e, 0, ds, :])
                    + nt(ug[...], win[e, 1, ds, :])
                    + nt(ilg, bank(d * TILE))
                )
                if e == 0:
                    xacc[:, ds] = t
                else:
                    obuf[rows, ds] = (xacc[:, ds] + t).astype(BF)

            for n, grad in ((2 * e, gg), (2 * e + 1, ug)):
                aup[n] += tn(inlat, grad[...])[RANK * n : RANK * n + RANK, :]
            alow[e] += tn(dlg, hid[...])[low : low + RANK, :]
            alift[e] += tn(dl, vg[...])[low : low + RANK, :]
        adown[...] += tn(ilg_total.astype(BF), xfull[rows, 0:D])[0 : 4 * RANK, :]
        obuf[rows, D : D + PAD] = jnp.where(
            lane == 64 + 2 * c, gate_grads[0], jnp.where(lane == 65 + 2 * c, gate_grads[1], 0.0)
        ).astype(BF)
        for step in range(4):

            @pl.when(j == step)
            def _():
                for t in range(2):
                    n = 2 * ((step + STEPS[0]) % 4) + t
                    if n:
                        back_to(n).start()

        return carry

    def back_to(n):
        rel = PLACES[n]
        seen = PLACES.index(((4 - rel[0]) % 4, rel[1]))
        return to_peer(
            obuf.at[pl.ds(T * n, T)], rbuf.at[seen], send2.at[n], recv2.at[seen], place(rel)
        )

    lax.fori_loop(0, 4, chunk, 0)
    keep = [
        pltpu.make_async_copy(
            xfull.at[pl.ds(T * n, T)], xout.at[span(sources[n] * T, T)], xsem.at[n]
        )
        for n in range(PEERS)
    ]
    for copy in keep:
        copy.start()
    gup[...] = aup[...].astype(BF)
    glow[...] = alow[...].astype(BF)
    glift[...] = alift[...].astype(BF)
    gdown[...] = adown[...].astype(BF)
    ring.sent()
    for n in range(1, PEERS):
        back_to(n).wait_send()
        to_peer(
            obuf.at[pl.ds(T * n, T)], rbuf.at[n], send2.at[n], recv2.at[n], place(PLACES[n])
        ).wait_recv()
    for copy in keep:
        copy.wait()

    @pl.loop(0, T // 32)
    def _(i):
        at = span(i * 32, 32)
        total = obuf[at, :].astype(F32)
        for n in range(1, PEERS):
            total += rbuf[n, at, :].astype(F32)
        summed[at, :] = total


def experts(pay, branch, cot, bank, upin, ad, pin, pout, ein, eout):
    sems = pltpu.SemaphoreType.DMA
    return pl.pallas_call(
        expert_kernel,
        out_shape=(
            jax.ShapeDtypeStruct((PEERS, S, W), BF),
            jax.ShapeDtypeStruct((T, D + PAD), F32),
            jax.ShapeDtypeStruct((S, D + PAD), BF),
            jax.ShapeDtypeStruct((4, RANK, FF), BF),
            jax.ShapeDtypeStruct((2, RANK, FF), BF),
            jax.ShapeDtypeStruct((2, RANK, D), BF),
            jax.ShapeDtypeStruct((4 * RANK, D), BF),
        ),
        in_specs=[VMEM, VMEM, ANY, VMEM, VMEM, VMEM] + [ANY] * 25,
        out_specs=(VMEM, VMEM, ANY, VMEM, VMEM, VMEM, VMEM),
        scratch_shapes=[
            pltpu.VMEM((S, D + PAD), BF),
            pltpu.VMEM((2, 2, D, FF), BF),
            pltpu.VMEM((2, FF, D), BF),
            pltpu.VMEM((2, PEERS, CHUNK, W), BF),
            pltpu.VMEM((S, D + PAD), BF),
            pltpu.VMEM((PEERS, T, D + PAD), BF),
            pltpu.VMEM((CHUNK, FF), F32),
            pltpu.VMEM((CHUNK, FF), F32),
            pltpu.VMEM((CHUNK, FF), BF),
            pltpu.VMEM((CHUNK, D), BF),
            pltpu.VMEM((CHUNK, FF), BF),
            pltpu.VMEM((CHUNK, FF), BF),
            pltpu.VMEM((CHUNK, D), F32),
            pltpu.VMEM((CHUNK, D), F32),
            pltpu.VMEM((4, RANK, FF), F32),
            pltpu.VMEM((2, RANK, FF), F32),
            pltpu.VMEM((2, RANK, D), F32),
            pltpu.VMEM((4 * RANK, D), F32),
            sems((16,)), sems((16,)), sems((16,)), sems((4,)),
            sems((9,)), sems((9,)), sems((PEERS,)), sems((PEERS,)), sems((PEERS,)),
            pltpu.VMEM((16, T, PAD), BF), sems((16,)), sems((16,)), sems((16,)),
        ],
        compiler_params=params(3, 63),
        cost_estimate=pl.CostEstimate(flops=10**11, bytes_accessed=10**7, transcendentals=0),
        name="experts",
    )(pay, branch, cot, bank, upin, ad, *pin, *pout, *ein, *eout)


def back_kernel(
    summed, state, prob, routes, bank, ru, gain, cot_t, mine, other, extra, lat_o,
    q, k_, v, att, cols, qraw, kraw, qgain, kgain, cosine, sine, up, lat, xfull_in, normed_in, flat_in,
    pg, bgc, stat3, lcg, gqkvup, goutdown, goutup, grup, growdown, flat,
    wo, sem, bg, sbuf, abuf, dq, dk, dv, stat, inbox, ex,
    send1, recv1, send2, recv2, send3, recv3, xfull, normed, fsem, *sems,
):
    c = lax.axis_index("col")
    barrier = greet()
    greet_row(barrier, PLANE, UP, DOWN)
    greet_partner(barrier)
    rows_in = RowGather(flat_in, flat, 6 * RANK, sems)
    loads = load_out(mine, other, wo, sem)
    for load in loads:
        load.start()
    fetches = [
        pltpu.make_async_copy(xfull_in, xfull, fsem.at[0]),
        pltpu.make_async_copy(normed_in, normed, fsem.at[1]),
    ]
    for copy in fetches:
        copy.start()
    lane = lanes(T)
    p_ = prob[...]
    gg = jnp.where(member_of(routes, T), summed[:, D : D + PAD], 0.0)
    lgrad = (p_ * (gg - jnp.sum(p_ * gg, axis=1, keepdims=True))).astype(BF)
    rlg = nt(lgrad, ru[...]).astype(BF)
    both = jnp.where(lane < 64, rlg.astype(F32), lgrad.astype(F32)).astype(BF)
    total = jnp.zeros((T, 1), F32)
    for p in range(PEERS):
        feats = slice(W * p, W * p + W)
        st = state[:, feats]
        total += jnp.sum(st * st, axis=1, keepdims=True)
    r = lax.rsqrt(total / D + EPS)
    mean = jnp.zeros((T, 1), F32)
    for p in range(PEERS):
        feats = slice(W * p, W * p + W)
        m = (summed[:, feats] + nt(both, bank[feats, 0:PAD])) * gain[:, feats]
        mean += jnp.sum(state[:, feats] * m, axis=1, keepdims=True)
    mean = mean / D
    olg = jnp.zeros((T, PAD), F32)
    for p in range(PEERS):
        feats = slice(W * p, W * p + W)
        m = (summed[:, feats] + nt(both, bank[feats, 0:PAD])) * gain[:, feats]
        st = state[:, feats]
        grad = (cot_t[p].astype(F32) + r * m - st * (r * r * r) * mean).astype(BF)
        bg[p] = grad
        olg += nt(grad, extra[p])
    olg = jnp.where((lane >= RANK) & (lane < 2 * RANK), olg, 0.0)
    moved = pltpu.roll(olg, PAD - RANK, 1).astype(BF)
    info = jnp.where(
        lane < RANK, lat_o[...], jnp.where(lane < 2 * RANK, olg, both.astype(F32))
    ).astype(BF)
    x = jnp.concatenate([bg[p] for p in range(PEERS)], axis=1)
    for load in loads:
        load.wait()
    pl.semaphore_wait(barrier, PEERS - 1 + 4)
    rows_in.start()
    for n in (4, 3, 5, 2, 6, 1, 7, 0):
        d = peer_of(n)
        part = nn(x, wo[:, span(d * W, W)]) + nn(moved, extra[d])
        sbuf[d, :, 0:W] = part.astype(BF)
        sbuf[d, :, W : W + PAD] = info
        if n:
            to_peer(sbuf.at[d], abuf.at[c], send1.at[n], recv1.at[n], d).start()
        else:
            abuf[c] = sbuf[c]
            bgc[c] = bg[c]
    for n in ORDER:
        d = peer_of(n)
        to_peer(bg.at[d], bgc.at[c], send2.at[n], recv2.at[n], d).start()
    for n in ORDER:
        d = peer_of(n)
        to_peer(sbuf.at[d], abuf.at[source_of(n)], send1.at[n], recv1.at[n], d).wait()
    rows_in.step(0)
    rows_in.step(1)
    for p in range(PEERS):
        ex[T * p : T * p + T, :] = abuf[p, :, W : W + PAD]

    blocks = 4
    size = S // blocks
    for h in range(2):
        feats = slice(HEAD * h, HEAD * h + HEAD)
        for i in reversed(range(blocks)):
            rows = slice(i * size, (i + 1) * size)
            seen = (i + 1) * size
            allowed = lax.broadcasted_iota(jnp.int32, (size, seen), 1) <= (
                lax.broadcasted_iota(jnp.int32, (size, seen), 0) + i * size
            )
            g = jnp.concatenate([abuf[2 * i, :, feats], abuf[2 * i + 1, :, feats]], axis=0)
            qb = q[rows, feats]
            kb = k_[0:seen, feats]
            score = nt(qb, kb) * FACTOR
            full = jnp.where(allowed, jnp.exp(score - cols[rows, 2 + h : 3 + h]), 0.0)
            wgrad = nt(g, v[0:seen, feats])
            center = jnp.sum(full * wgrad, axis=1, keepdims=True)
            sgrad = (full * (wgrad - center)).astype(BF)
            dq[rows, feats] = nn(sgrad, kb) * FACTOR
            dvp = tn(full.astype(BF), g)
            dkp = tn(sgrad, qb) * FACTOR
            if i == blocks - 1:
                dv[0:seen, feats] = dvp
                dk[0:seen, feats] = dkp
            else:
                dv[0:seen, feats] += dvp
                dk[0:seen, feats] += dkp
    for i in range(blocks):
        rows = slice(i * size, (i + 1) * size)
        dots = []
        for raw, gain_, grads in ((qraw, qgain, dq), (kraw, kgain, dk)):
            dot = jnp.zeros((size, 1), F32)
            for h in range(2):
                feats = slice(HEAD * h, HEAD * h + HEAD)
                y = grads[rows, feats]
                y = y * cosine[rows, :] - pltpu.roll(y, HEAD // 2, 1) * sine[rows, :]
                y = y * gain_[:, feats]
                grads[rows, feats] = y
                dot += jnp.sum(y * raw[rows, feats], axis=1, keepdims=True)
            dots.append(dot)
        stat[:, rows] = columns_to_rows(*dots)
    swap_start(stat, inbox, send3, recv3)
    rows_in.step(2)
    for copy in fetches:
        copy.wait()
    goutdown[...] = tn(ex[...], att[...])[RANK : 2 * RANK, :].astype(BF)
    grup[...] = tn(xfull[:, D : D + PAD], ex[...])[48:64, :].astype(BF)
    growdown[3 * RANK : 4 * RANK, :] = tn(ex[...], xfull[:, 0:D])[48:64, :].astype(BF)
    dots = swap_finish(stat, inbox, send3, recv3)
    wide = lanes(size)
    for i in range(blocks):
        rows = slice(i * size, (i + 1) * size)
        column = rows_to_columns(dots[:, rows])
        stat_sum = jnp.zeros((size, 1), F32)
        code = jnp.zeros((size, PAD), F32)
        for n, (raw, grads) in enumerate(((qraw, dq), (kraw, dk))):
            rs = cols[rows, n : n + 1]
            x = raw[rows, :]
            y = rs * grads[rows, :] - x * (rs * rs * rs * column[:, n : n + 1] / D)
            y = y.astype(BF)
            pg[rows, W * n : W * n + W] = y
            stat_sum += jnp.sum(y.astype(F32) * x, axis=1, keepdims=True)
            code += nt(y, up[:, W * n : W * n + W])
        y = dv[rows, :].astype(BF)
        pg[rows, 2 * W : 3 * W] = y
        stat_sum += jnp.sum(y.astype(F32) * v[rows, :].astype(F32), axis=1, keepdims=True)
        code += nt(y, up[:, 2 * W : 3 * W])
        lcg[rows, :] = jnp.where(wide < 3 * RANK, code, 0.0).astype(BF)
        stat3[:, rows] = columns_to_rows(stat_sum, stat_sum)
    for n in range(3):
        gqkvup[n] = tn(lat[...], pg[:, W * n : W * n + W])[RANK * n : RANK * n + RANK, :].astype(BF)
    growdown[0 : 3 * RANK, :] = tn(lcg[...], normed[...])[0 : 3 * RANK, :].astype(BF)
    for n in ORDER:
        d = peer_of(n)
        to_peer(bg.at[d], bgc.at[source_of(n)], send2.at[n], recv2.at[n], d).wait()
    acc = jnp.zeros((PAD, W), F32)
    for p in range(PEERS):
        acc += tn(ex[T * p : T * p + T, :], bgc[p])
    goutup[...] = acc[0:RANK, :].astype(BF)
    rows_in.step(3)
    rows_in.finish()


def back(*args):
    sems = pltpu.SemaphoreType.DMA((PEERS,))
    kinds = [VMEM] * len(args)
    kinds[8] = ANY
    kinds[9] = ANY
    kinds[25] = ANY
    kinds[26] = ANY
    kinds[27] = ANY
    return pl.pallas_call(
        back_kernel,
        out_shape=(
            jax.ShapeDtypeStruct((S, 3 * W), BF),
            jax.ShapeDtypeStruct((PEERS, T, W), BF),
            jax.ShapeDtypeStruct((8, S), F32),
            jax.ShapeDtypeStruct((S, PAD), BF),
            jax.ShapeDtypeStruct((3, RANK, W), BF),
            jax.ShapeDtypeStruct((RANK, W), BF),
            jax.ShapeDtypeStruct((RANK, W), BF),
            jax.ShapeDtypeStruct((RANK, PAD), BF),
            jax.ShapeDtypeStruct((4 * RANK, D), BF),
            jax.ShapeDtypeStruct((16, 6 * RANK, FF), BF),
        ),
        in_specs=kinds,
        out_specs=(VMEM,) * 9 + (ANY,),
        scratch_shapes=[
            pltpu.VMEM((D, D), BF),
            pltpu.SemaphoreType.DMA((2 * PEERS,)),
            pltpu.VMEM((PEERS, T, W), BF),
            pltpu.VMEM((PEERS, T, W + PAD), BF),
            pltpu.VMEM((PEERS, T, W + PAD), BF),
            pltpu.VMEM((S, W), F32),
            pltpu.VMEM((S, W), F32),
            pltpu.VMEM((S, W), F32),
            pltpu.VMEM((8, S), F32),
            pltpu.VMEM((PEERS, 8, S), F32),
            pltpu.VMEM((S, PAD), BF),
            sems, sems, sems, sems, sems, sems,
            pltpu.VMEM((S, D + PAD), BF),
            pltpu.VMEM((S, D), BF),
            pltpu.SemaphoreType.DMA((2,)),
            *row_sems(),
        ],
        compiler_params=params(4, 63),
        cost_estimate=pl.CostEstimate(flops=4 * 10**10, bytes_accessed=10**7, transcendentals=0),
        name="back",
    )(*args)


HALVES = (slice(0, S // 2), slice(S // 2, S))


class Scatter:
    def __init__(self, parts, passing, near, last, send, recv):
        self.parts, self.passing, self.near, self.last = parts, passing, near, last
        self.send, self.recv = send, recv

    def piece(self, rel, half):
        return self.parts.at[PLACES.index(rel), HALVES[half]]

    def copy(self, kind, y, half):
        up, down = (1, 0), (3, 0)
        if kind == "far":
            to, src, dst = (up, down)[half], self.piece((2, y), half), self.passing.at[half, y]
        elif kind == "plain":
            to, rel = ((down, (3, y)), (up, (1, y)))[half]
            src, dst = self.piece(rel, half), self.near.at[0, half, y]
        elif kind == "summed":
            to, rel = ((up, (1, y)), (down, (3, y)))[half]
            src, dst = self.piece(rel, half), self.near.at[1, half, y]
        else:
            to, src, dst = (0, 1), self.piece((0, 1), half), self.last.at[half]
        n = ("far", "plain", "summed", "plane").index(kind) * 4 + 2 * y + half
        return to_peer(src, dst, self.send.at[n], self.recv.at[n], place(to))

    def ready(self, slot):
        rel = PLACES[slot]
        if rel[0] == 2:
            for half in range(2):
                self.copy("far", rel[1], half).start()
        elif rel[0]:
            self.copy("plain", rel[1], 1 if rel[0] == 1 else 0).start()

    def add(self, rel, half, others):
        slot, at = PLACES.index(rel), HALVES[half].start

        @pl.loop(0, S // 2 // 128)
        def _(i):
            rows, there = span(i * 128, 128), pl.ds(pl.multiple_of(at + i * 128, 128), 128)
            total = self.parts[slot, there, :].astype(F32)
            for other in others:
                total += other[rows, :].astype(F32)
            self.parts[slot, there, :] = total.astype(BF)

    def middle(self):
        for y in range(2):
            for half in range(2):
                self.copy("far", y, half).wait_recv()
                rel = ((1, y), (3, y))[half]
                self.add(rel, half, [self.passing.at[half, y]])
                self.copy("summed", y, half).start()

    def end(self):
        for y in (1, 0):
            for half in range(2):
                self.copy("plain", y, half).wait_recv()
                self.copy("summed", y, half).wait_recv()
                if y:
                    self.add((0, 1), half, [self.near.at[k, half, 1] for k in range(2)])
                    self.copy("plane", 0, half).start()
        for half in range(2):
            self.copy("plane", 0, half).wait_recv()

    def arrived(self, half, rows):
        kept = [self.near[k, half, 0, rows, :].astype(F32) for k in range(2)]
        return kept[0] + kept[1] + self.last[half, rows, :].astype(F32)

    def sent(self):
        for kind in ("far", "plain", "summed"):
            for y in range(2):
                for half in range(2):
                    self.copy(kind, y, half).wait_send()
        for half in range(2):
            self.copy("plane", 0, half).wait_send()


GROUPS = 10


def input_kernel(
    pg, lcg, wq, bank, stat3, bgc, tokens, rinv, gain,
    picked, gdown, glift, growdown, gqkvup, goutdown, goutup, grup,
    out, gin, glif, grout, gqkvdown, gqkvup_all, gout, goutup_all, grup_all,
    w, wsem, own, sbuf, passing, near, last, inbox,
    tall, thin, tallbuf, thinbuf, tallsum, thinsum, mine, theirs,
    send, recv, send3, recv3, send4, recv4, send5, recv5, send6, recv6,
):
    c = lax.axis_index("col")
    r = lax.axis_index("row")
    barrier = greet()
    for n in range(1, 16):
        pl.semaphore_signal(
            barrier, inc=1, device_id={"row": lax.rem(r + n, 16)}, device_id_type=MESH
        )
    loads = [
        pltpu.make_async_copy(
            wq.at[:, T * k : T * k + T, :], w.at[:, :, W * k : W * k + W], wsem.at[k]
        )
        for k in range(3)
    ]
    for load in loads:
        load.start()
    for p in range(16):
        at = slice(T * p, T * p + T)
        tall[p, 0 : 4 * RANK, :] = gdown[:, at]
        tall[p, 4 * RANK : 6 * RANK, :] = glift[:, at]
        tall[p, 6 * RANK : 10 * RANK, :] = growdown[:, at]
    thin[0 : 3 * RANK, :] = gqkvup[...]
    thin[3 * RANK : 4 * RANK, :] = goutdown[...]
    thin[4 * RANK : 5 * RANK, :] = goutup[...]
    thin[5 * RANK : 6 * RANK, 0:PAD] = grup[...]
    thin[5 * RANK : 6 * RANK, PAD:W] = jnp.zeros((RANK, PAD), BF)
    for load in loads:
        load.wait()
    pl.semaphore_wait(barrier, PEERS - 1 + 15)

    def row_copies(n):
        p = lax.rem(r + n, 16)
        where = {"row": p}
        return [
            pltpu.make_async_remote_copy(
                src_ref=tall.at[p], dst_ref=tallbuf.at[r],
                send_sem=send4.at[n], recv_sem=recv4.at[n],
                device_id=where, device_id_type=MESH,
            ),
            pltpu.make_async_remote_copy(
                src_ref=thin, dst_ref=thinbuf.at[r], send_sem=send5.at[n], recv_sem=recv5.at[n],
                device_id=where, device_id_type=MESH,
            ),
        ]

    def row_arrivals(n):
        p = lax.rem(r + 16 - n, 16)
        where = {"row": p}
        return [
            pltpu.make_async_remote_copy(
                src_ref=tallbuf.at[p], dst_ref=tallbuf.at[p],
                send_sem=send4.at[n], recv_sem=recv4.at[n],
                device_id=where, device_id_type=MESH,
            ),
            pltpu.make_async_remote_copy(
                src_ref=thin, dst_ref=thinbuf.at[p], send_sem=send5.at[n], recv_sem=recv5.at[n],
                device_id=where, device_id_type=MESH,
            ),
        ]

    for n in range(1, 16):
        for copy in row_copies(n):
            copy.start()
    tallbuf[r] = tall[r]
    thinbuf[r] = thin[...]
    swap_start(stat3, inbox, send3, recv3)
    ring = Scatter(sbuf, passing, near, last, send, recv)
    for slot in (6, 7, 2, 3, 4, 5, 1, 0):
        d = place(PLACES[slot])
        wide = span(d * W, W)
        for i in range(2):
            rows = slice(512 * i, 512 * i + 512)
            part = nt(lcg[rows, :], bank[wide, 0:PAD])
            part += nt(pg[rows, :], w[pl.ds(2 * d, 2)].reshape(W, 3 * W))
            if slot:
                sbuf[slot, rows, :] = part.astype(BF)
            else:
                own[rows, :] = part
        ring.ready(slot)
    ring.middle()

    for n in range(1, 16):
        for copy in row_arrivals(n):
            copy.wait_recv()

    def summed(s, shape, read):
        return lax.fori_loop(
            0, 16, lambda q, acc: acc + picked[s, q] * read(q).astype(F32), jnp.zeros(shape, F32)
        )

    @pl.loop(0, SETS)
    def _(s):
        at = span(s * RANK, RANK)
        total = summed(s, (GROUPS * RANK, T), lambda q: tallbuf[q])
        for g in range(GROUPS):
            tallsum[g, at, :] = total[RANK * g : RANK * g + RANK, :]

    mine[...] = tallsum[6:9].astype(BF)
    theirs[c] = mine[...]
    for k in ORDER:
        to_peer(mine, theirs.at[c], send6.at[k], recv6.at[k], peer_of(k)).start()

    @pl.loop(0, SETS)
    def _(s):
        at = span(s * RANK, RANK)
        total = summed(s, (6 * RANK, W), lambda q: thinbuf[q])
        for g in range(6):
            thinsum[g, at, :] = total[RANK * g : RANK * g + RANK, :]

    for g in range(4):
        gin[g] = jnp.transpose(tallsum[g])
    for g in range(2):
        glif[g] = tallsum[4 + g]
    grout[...] = jnp.transpose(tallsum[9])
    for k in range(3):
        gqkvup_all[k] = thinsum[k]
    for m in range(2):
        gout[PAD * m : PAD * m + PAD, :] = jnp.transpose(thinsum[3, :, PAD * m : PAD * m + PAD])
    goutup_all[...] = thinsum[4]
    grup_all[...] = thinsum[5, :, 0:PAD]
    for k in ORDER:
        to_peer(mine, theirs.at[source_of(k)], send6.at[k], recv6.at[k], peer_of(k)).wait()
    for k in range(3):
        total = theirs[0, k].astype(F32)
        for p in range(1, PEERS):
            total += theirs[p, k].astype(F32)
        gqkvdown[k] = jnp.transpose(total)
    for n in range(1, 16):
        for copy in row_copies(n):
            copy.wait_send()
    dots = swap_finish(stat3, inbox, send3, recv3)
    ring.end()
    ring.sent()
    for i in range(4):
        rows = slice(256 * i, 256 * i + 256)
        column = rows_to_columns(dots[:, rows])[:, 0:1]
        total = own[rows, :] + ring.arrived(i // 2, slice(256 * (i % 2), 256 * (i % 2) + 256))
        q = rinv[rows, 0:1]
        grad = bgc[rows, :].astype(F32) + q * (total * gain[...])
        out[rows, :] = grad - tokens[rows, :].astype(F32) * (q * q * column / D)


def to_input(*args):
    sems = pltpu.SemaphoreType.DMA((PEERS,))
    more = pltpu.SemaphoreType.DMA((16,))
    kinds = [VMEM] * len(args)
    kinds[2] = ANY
    kinds[9] = pl.BlockSpec(memory_space=pltpu.SMEM)
    square = (PAD, PAD)
    return pl.pallas_call(
        input_kernel,
        out_shape=tuple(
            jax.ShapeDtypeStruct(shape, F32)
            for shape in (
                (S, W), (4, *square), (2, *square), square, (3, *square), (3, PAD, W), (W, PAD),
                (PAD, W), square,
            )
        ),
        in_specs=kinds,
        out_specs=(VMEM,) * 9,
        scratch_shapes=[
            pltpu.VMEM((16, T, 3 * W), BF),
            pltpu.SemaphoreType.DMA((3,)),
            pltpu.VMEM((S, W), F32),
            pltpu.VMEM((PEERS, S, W), BF),
            pltpu.VMEM((2, 2, S // 2, W), BF),
            pltpu.VMEM((2, 2, 2, S // 2, W), BF),
            pltpu.VMEM((2, S // 2, W), BF),
            pltpu.VMEM((PEERS, 8, S), F32),
            pltpu.VMEM((16, GROUPS * RANK, T), BF),
            pltpu.VMEM((6 * RANK, W), BF),
            pltpu.VMEM((16, GROUPS * RANK, T), BF),
            pltpu.VMEM((16, 6 * RANK, W), BF),
            pltpu.VMEM((GROUPS, *square), F32),
            pltpu.VMEM((6, PAD, W), F32),
            pltpu.VMEM((3, *square), BF),
            pltpu.VMEM((PEERS, 3, *square), BF),
            more, more, sems, sems, more, more, more, more, sems, sems,
        ],
        compiler_params=params(5, 63),
        cost_estimate=pl.CostEstimate(flops=5 * 10**10, bytes_accessed=10**7, transcendentals=0),
        name="input",
    )(*args)


def sums_kernel(sets, flat, ginup, glower, low):
    ginup[...] = jnp.zeros_like(ginup)
    low[...] = jnp.zeros_like(low)

    @pl.loop(0, 16)
    def _(q):
        at = span(sets[q] * RANK, RANK)
        for g in range(4):
            ginup[g, at, :] += flat[q, RANK * g : RANK * g + RANK, :].astype(F32)
        for g in range(2):
            low[g, at, :] += flat[q, RANK * (4 + g) : RANK * (5 + g), :].astype(F32)

    for g in range(2):
        for m in range(FF // PAD):
            glower[g, PAD * m : PAD * m + PAD, :] = jnp.transpose(low[g, :, PAD * m : PAD * m + PAD])


def sums(sets, flat):
    return pl.pallas_call(
        sums_kernel,
        out_shape=(
            jax.ShapeDtypeStruct((4, PAD, FF), F32), jax.ShapeDtypeStruct((2, FF, PAD), F32),
        ),
        in_specs=[pl.BlockSpec(memory_space=pltpu.SMEM), VMEM],
        out_specs=(VMEM, VMEM),
        scratch_shapes=[pltpu.VMEM((2, PAD, FF), F32)],
        compiler_params=params(None, 63),
        cost_estimate=pl.CostEstimate(flops=10**9, bytes_accessed=10**7, transcendentals=0),
        name="sums",
    )(sets, flat)


def rope_tables():
    half = HEAD // 2
    frequency = (10000.0 ** (-(np.arange(half, dtype=np.float32) * 2.0) / HEAD)).astype(np.float32)
    angle = np.arange(S, dtype=np.float32)[:, None] * frequency[None, :]
    cosine, sine = np.cos(angle), np.sin(angle)
    return (
        np.concatenate([cosine, cosine], axis=1).astype(np.float32),
        np.concatenate([-sine, sine], axis=1).astype(np.float32),
    )


def body(
    tokens, cotangent, routes, adapter_set, attn_gain, mixer_gain, query_gain, key_gain,
    qkv_weight, qkv_down, qkv_up, out_weight, out_down, out_up,
    router_weight, router_down, router_up,
    expert_in, expert_in_down, expert_in_up, expert_out, expert_out_down, expert_out_up,
):
    c = lax.axis_index("col")
    start = adapter_set[0] * RANK

    out_up_pick = lax.dynamic_slice_in_dim(out_up, start, RANK, 0)
    out_down_pick = lax.dynamic_slice_in_dim(out_down, start, RANK, 1)
    pay0 = jnp.concatenate([tokens, out_down_pick.T, out_up_pick], axis=0)

    flag = jnp.broadcast_to(adapter_set.astype(BF)[:, None], (T, PAD))
    shard = jnp.concatenate(
        [
            qkv_weight.reshape(3 * T, W),
            jnp.concatenate([qkv_down[0], qkv_down[1]], axis=1),
            jnp.concatenate([qkv_down[2], router_down], axis=1),
            jnp.concatenate([jnp.pad(router_weight, ((0, 0), (64, 48))), flag], axis=1),
            out_weight.T,
        ],
        axis=0,
    )
    normed, rinv, resid, extra, cot, po, pl0, pr0, xl, xr, xf, xo, wq = gather_tokens(
        pay0, attn_gain[None], cotangent, expert_in, expert_out, shard
    )
    sets = wq[:, 5 * T, PAD].astype(F32)
    picked = (sets[None, :] == jnp.arange(SETS, dtype=F32)[:, None]).astype(F32)
    spot = jnp.arange(PAD, dtype=jnp.int32)
    rank = spot[None, :, None] - start
    picks = (
        (rank >= 0) & (rank < RANK)
        & (rank + RANK * jnp.arange(4, dtype=jnp.int32)[:, None, None] == spot[None, None, :])
    ).astype(BF)

    down = jnp.concatenate(
        [
            jnp.moveaxis(expert_out_up, 2, 0),
            jnp.moveaxis(expert_in_down.reshape(4, T, PAD), 0, 1),
        ],
        axis=1,
    ).reshape(T, 6, SETS, RANK)
    down = jnp.einsum(
        "dnsj,sr->rdnj", down, picked.astype(BF), preferred_element_type=F32
    ).astype(BF).reshape(16, T, 6 * RANK)
    ebank = jnp.concatenate(
        [
            down[:, :, 2 * RANK :], jnp.zeros((16, T, 16), BF), down[:, :, : 2 * RANK],
            jnp.zeros((16, T, 16), BF),
        ],
        axis=2,
    )

    qkv_up_pick = lax.dynamic_slice_in_dim(qkv_up, start, RANK, 1)
    up = jnp.concatenate(
        [jnp.pad(qkv_up_pick[k], ((RANK * k, PAD - RANK * k - RANK), (0, 0))) for k in range(3)],
        axis=1,
    )
    in_up_pick = lax.dynamic_slice_in_dim(expert_in_up, start, RANK, 2).reshape(4, RANK, FF)
    upin = jnp.stack(
        [jnp.pad(in_up_pick[n], ((RANK * n, PAD - RANK * n - RANK), (0, 0))) for n in range(4)]
    )
    lower_pick = lax.dynamic_slice_in_dim(expert_out_down, start, RANK, 2)
    ad = jnp.stack(
        [jnp.pad(lower_pick[e], ((0, 0), (80 + RANK * e, 32 - RANK * e))) for e in range(2)]
    )
    ru = jnp.pad(lax.dynamic_slice_in_dim(router_up, start, RANK, 0), ((48, 64), (64, 48)))
    routes_t = lax.dynamic_slice_in_dim(routes, c * T, T, 0)
    cosine, sine = rope_tables()

    qg, kg = query_gain[None], key_gain[None]
    (
        att_t, att, q, k, v, qraw, kraw, cols, lat, bank, half, other,
        pl1, pr1, pf0, pf1, yl, yr, yf, *swapped,
    ) = attention(
        normed, wq, picks, up, qg, kg, cosine, sine,
        (expert_in, po, pl0, pr0), (expert_out, xo, xl, xr, xf),
    )
    pin = [expert_in, po, pl0, pl1, pr0, pr1, pf0, pf1]
    pout = [expert_out, xo, xl, yl, xr, yr, xf, yf]
    half, other = half.reshape(PEERS, S, W), other.reshape(PEERS, S, W)
    pay, state, prob, branch, lat_o = to_state(
        att_t, half, other, resid, extra, mixer_gain[None], bank, ru, routes_t
    )
    mixture, summed, xfull, gup, glow, glift, gdown = experts(
        pay, branch, cot, ebank, upin, ad, pin, pout, swapped[:4], swapped[4:]
    )
    mixture = lax.psum_scatter(mixture.reshape(PEERS * S, W), "col", scatter_dimension=0, tiled=True)
    flat = jnp.concatenate([gup.reshape(4 * RANK, FF), glow.reshape(2 * RANK, FF)], axis=0)

    cot_t = lax.dynamic_slice_in_dim(cot, c * T, T, 1)
    pg, bgc, stat3, lcg, gqkvup, goutdown, goutup, grup, gtall, flat = back(
        summed, state, prob, routes_t, bank, ru, mixer_gain[None], cot_t, half, other, extra,
        lat_o, q, k, v, att, cols, qraw, kraw, qg, kg, cosine, sine, up, lat, xfull, normed,
        flat,
    )
    pg, mixture = lax.optimization_barrier((pg, mixture))
    mixed = (tokens.astype(F32) + mixture.astype(F32)).astype(BF)
    gain_mine = lax.dynamic_slice_in_dim(attn_gain, c * W, W, 0)[None]
    (
        tokens_grad, in_down_grad, lift_grad, router_down_grad, qkv_down_grad, qkv_up_grad,
        out_down_grad, out_up_grad, router_up_grad,
    ) = to_input(
        pg, lcg, wq, bank, stat3, bgc.reshape(S, W), tokens, rinv, gain_mine,
        picked, gdown, glift.reshape(2 * RANK, D), gtall, gqkvup.reshape(3 * RANK, W),
        goutdown, goutup, grup,
    )
    in_up_grad, lower_grad = sums(sets.astype(jnp.int32), flat)
    in_down_grad = in_down_grad.reshape(2, 2, T, PAD)
    in_up_grad = in_up_grad.reshape(2, 2, PAD, FF)
    router_up_grad = router_up_grad[:, 64:80]
    return (
        mixed, tokens_grad, qkv_down_grad, qkv_up_grad, out_down_grad, out_up_grad,
        router_down_grad, router_up_grad, in_down_grad, in_up_grad, lower_grad, lift_grad,
    )


def solution(mesh):
    in_specs = (
        P("row", "col"), P("row", "col"), P("row", None), P("row"), P(), P(), P("col"), P("col"),
        P(None, "row", "col"), P(None, "row", None), P(None, None, "col"),
        P("col", "row"), P("col", None), P(None, "col"),
        P("row", None), P("row", None), P(),
        P("col", None, "row", None), P("col", None, "row", None), P("col", None, None, None),
        P("col", None, "row"), P("col", None, None), P("col", None, "row"),
    )
    out_specs = (
        P("row", "col"), P("row", "col"), P(None, "row", None), P(None, None, "col"),
        P("col", None), P(None, "col"), P("row", None), P(),
        P("col", None, "row", None), P("col", None, None, None), P("col", None, None),
        P("col", None, "row"),
    )
    return jax.shard_map(body, mesh=mesh, in_specs=in_specs, out_specs=out_specs, check_vma=False)
```

```python
import functools

import jax
import jax.numpy as jnp
import numpy as np
from jax import lax
from jax.experimental import pallas as pl
from jax.experimental.pallas import tpu as pltpu
from jax.sharding import PartitionSpec as P

D = 2048
HEAD = 128
FF = 1024
RANK = 16
SETS = 8
S = 1024
W = 256
T = 128
PEERS = 8
PAD = 128
EPS = 1e-05
FACTOR = HEAD ** (-0.5)
F32 = jnp.float32
BF = jnp.bfloat16
MESH = pl.DeviceIdType.MESH
VMEM = pl.BlockSpec(memory_space=pltpu.VMEM)
ANY = pl.BlockSpec(memory_space=pl.ANY)

NN = (((1,), (0,)), ((), ()))
NT = (((1,), (1,)), ((), ()))
TN = (((0,), (0,)), ((), ()))


def nn(a, b):
    return lax.dot_general(a, b, NN, preferred_element_type=F32)


def nt(a, b):
    return lax.dot_general(a, b, NT, preferred_element_type=F32)


def tn(a, b):
    return lax.dot_general(a, b, TN, preferred_element_type=F32)


def lanes(rows):
    return lax.broadcasted_iota(jnp.int32, (rows, PAD), 1)


def span(start, size):
    return pl.ds(pl.multiple_of(start, size), size)


def params(collective=None, limit=62):
    return pltpu.CompilerParams(
        collective_id=collective,
        has_side_effects=collective is not None,
        vmem_limit_bytes=limit * 2**20,
    )


def greet():
    c = lax.axis_index("col")
    barrier = pltpu.get_barrier_semaphore()
    for k in range(1, PEERS):
        pl.semaphore_signal(
            barrier, inc=1, device_id={"col": lax.rem(c + k, PEERS)}, device_id_type=MESH
        )
    return barrier


def to_peer(src, dst, send, recv, peer):
    return pltpu.make_async_remote_copy(
        src_ref=src,
        dst_ref=dst,
        send_sem=send,
        recv_sem=recv,
        device_id={"col": peer},
        device_id_type=MESH,
    )


def peer_of(k):
    return lax.rem(lax.axis_index("col") + k, PEERS)


def source_of(k):
    return lax.rem(lax.axis_index("col") + PEERS - k, PEERS)


ORDER = (4, 1, 7, 5, 3, 2, 6)


PLACES = ((0, 0), (0, 1), (1, 0), (3, 0), (1, 1), (3, 1), (2, 0), (2, 1))
NEAR = ((0, 1), (1, 0), (3, 0))


def place(rel):
    c = lax.axis_index("col")
    return lax.rem(c // 4 + rel[1], 2) * 4 + lax.rem(lax.rem(c, 4) + rel[0], 4)


def greet_near():
    barrier = pltpu.get_barrier_semaphore()
    for rel in NEAR:
        pl.semaphore_signal(barrier, inc=1, device_id={"col": place(rel)}, device_id_type=MESH)
    return barrier


class Gather:
    MOVES = {
        "a0": ((0, 0), (0, 1), 0, (0, 1), 0),
        "a1": ((0, 0), (3, 0), 0, (1, 0), 2),
        "a2": ((0, 0), (1, 0), 0, (3, 0), 1),
        "b1": ((0, 1), (3, 1), 0, (1, 0), 4),
        "b2": ((0, 1), (1, 1), 0, (3, 0), 3),
        "c1": ((3, 0), (2, 0), 1, (1, 0), 5),
        "c2": ((1, 0), (2, 0), 2, (3, 0), 6),
        "d1": ((3, 1), (2, 1), 1, (1, 0), 7),
        "d2": ((1, 1), (2, 1), 2, (3, 0), 8),
    }
    FROM = (
        ((0, 1), 0), ((1, 0), 0), ((3, 0), 0), ((1, 1), 0), ((3, 1), 0),
        ((2, 0), 1), ((2, 0), 2), ((2, 1), 1), ((2, 1), 2),
    )

    def __init__(self, here, there, rows, send, recv, axis="col"):
        self.here, self.there, self.rows, self.send, self.recv = here, there, rows, send, recv
        self.axis = axis

    def copy(self, src, dst, send, recv, to):
        to = place(to) if self.axis == "col" else row_place((to[1], to[0]))
        return pltpu.make_async_remote_copy(
            src_ref=src, dst_ref=dst, send_sem=send, recv_sem=recv,
            device_id={self.axis: to}, device_id_type=MESH,
        )

    def part(self, which):
        half = self.rows // 2
        return ((0, self.rows), (0, half), (half, half))[which]

    def move(self, name):
        src, dst, which, to, arrives = self.MOVES[name]
        lo, n = self.part(which)
        return self.copy(
            self.here(src, lo, n), self.there(src, dst, lo, n),
            self.send.at[list(self.MOVES).index(name)], self.recv.at[arrives], to,
        )

    def start(self, *names):
        for name in names:
            self.move(name).start()

    def wait(self, *arrivals):
        for i in arrivals:
            rel, which = self.FROM[i]
            lo, n = self.part(which)
            ref = self.here(rel, lo, n)
            self.copy(ref, ref, self.send.at[0], self.recv.at[i], (0, 1)).wait_recv()

    def sent(self):
        for name in self.MOVES:
            self.move(name).wait_send()


def row_place(shift):
    r = lax.axis_index("row")
    plane = lax.rem(r // 8 + shift[0], 2)
    spot = lax.rem(lax.rem(r, 8) // 2 + shift[1], 4)
    return plane * 8 + spot * 2 + lax.rem(r, 2)


PLANE, UP, DOWN, FAR = (1, 0), (0, 1), (0, 3), (0, 2)


def greet_row(barrier, *shifts):
    for shift in shifts:
        pl.semaphore_signal(
            barrier, inc=1, device_id={"row": row_place(shift)}, device_id_type=MESH
        )


def along(src, dst, send, recv, shift):
    return pltpu.make_async_remote_copy(
        src_ref=src, dst_ref=dst, send_sem=send, recv_sem=recv,
        device_id={"row": row_place(shift)}, device_id_type=MESH,
    )


class RowGather:
    def __init__(self, shard, out, rows, sems):
        self.send, self.recv, self.xsend, self.xrecv, self.sem = sems
        self.shard, self.out, self.rows = shard, out, rows
        self.ring = Gather(
            self.part, lambda src, dst, lo, n: out.at[self.at(src), lo : lo + n],
            rows, self.send, self.recv, "row",
        )
        self.keep = pltpu.make_async_copy(shard, out.at[lax.axis_index("row")], self.sem)

    def at(self, rel):
        return row_place((rel[1], rel[0]))

    def part(self, rel, lo, n):
        if rel == (0, 0):
            return self.shard.at[lo : lo + n]
        return self.out.at[self.at(rel), lo : lo + n]

    def across(self, rel):
        r = lax.axis_index("row")
        n = PLACES.index(rel)
        return pltpu.make_async_remote_copy(
            src_ref=self.part(rel, 0, self.rows), dst_ref=self.out.at[self.at(rel)],
            send_sem=self.xsend.at[n], recv_sem=self.xrecv.at[n],
            device_id={"row": r + 1 - 2 * lax.rem(r, 2)}, device_id_type=MESH,
        )

    def start(self):
        self.ring.start("a0", "a1", "a2")
        self.keep.start()
        self.across((0, 0)).start()

    def step(self, i):
        waits, sends = (
            ((0,), ("b1", "b2")), ((1, 2), ("c1", "c2")), ((3, 4), ("d1", "d2")), ((5, 6, 7, 8), ())
        )[i]
        places = (((0, 1),), ((1, 0), (3, 0)), ((1, 1), (3, 1)), ((2, 0), (2, 1)))[i]
        self.ring.wait(*waits)
        self.ring.start(*sends)
        for rel in places:
            self.across(rel).start()

    def finish(self):
        self.ring.sent()
        self.keep.wait()
        r = lax.axis_index("row")
        for rel in PLACES:
            self.across(rel).wait_send()
        for rel in PLACES:
            n = PLACES.index(rel)
            q = self.at(rel) + 1 - 2 * lax.rem(r, 2)
            pltpu.make_async_remote_copy(
                src_ref=self.part(rel, 0, self.rows), dst_ref=self.out.at[q],
                send_sem=self.xsend.at[n], recv_sem=self.xrecv.at[n],
                device_id={"row": r + 1 - 2 * lax.rem(r, 2)}, device_id_type=MESH,
            ).wait_recv()


def row_sems():
    sems = pltpu.SemaphoreType.DMA
    return [sems((9,)), sems((9,)), sems((PEERS,)), sems((PEERS,)), sems]


def greet_partner(barrier):
    r = lax.axis_index("row")
    pl.semaphore_signal(
        barrier, inc=1, device_id={"row": r + 1 - 2 * lax.rem(r, 2)}, device_id_type=MESH
    )


def tokens_kernel(
    pay, gain, cot, win, wout, shard,
    normed, rinv, resid, extra, cots, wo, wl, wr, ql, qr, qf, qo, wq,
    buf, send, recv, send2, recv2, sem, send3, recv3, *sems,
):
    c = lax.axis_index("col")
    barrier = greet_near()
    greet_row(barrier, PLANE, UP, DOWN, FAR)
    greet_partner(barrier)
    rows_in = RowGather(shard, wq, shard.shape[0], sems)
    weights = [
        along(src, dst, send3.at[n], recv3.at[n], shift)
        for n, (src, dst, shift) in enumerate(
            (
                (win, wo, PLANE), (wout, qo, PLANE), (win, wl, UP), (win, wr, DOWN),
                (wout, ql, UP), (wout, qr, DOWN), (wout, qf, FAR),
            )
        )
    ]
    keep = pltpu.make_async_copy(cot, cots.at[c], sem)
    keep.start()
    buf[c] = pay[...]
    pl.semaphore_wait(barrier, 8)
    ring = Gather(
        lambda rel, lo, n: buf.at[place(rel), lo : lo + n],
        lambda src, dst, lo, n: buf.at[place(src), lo : lo + n],
        pay.shape[0], send, recv,
    )

    def cot_part(rel, lo, n):
        if rel == (0, 0):
            return cot.at[lo : lo + n]
        return cots.at[place(rel), lo : lo + n]

    second = Gather(
        cot_part, lambda src, dst, lo, n: cots.at[place(src), lo : lo + n], S, send2, recv2
    )
    ring.start("a0", "a1", "a2")
    rows_in.start()
    ring.wait(0)
    ring.start("b1", "b2")
    rows_in.step(0)
    ring.wait(1, 2)
    ring.start("c1", "c2")
    rows_in.step(1)
    for copy in weights:
        copy.start()
    ring.wait(3, 4)
    ring.start("d1", "d2")
    second.start("a0", "a1", "a2")
    rows_in.step(2)
    ring.wait(5, 6, 7, 8)
    extra[...] = jnp.zeros_like(extra)
    for p in range(PEERS):
        resid[p] = buf[p, span(c * T, T), :]
        extra[p, 0 : 2 * RANK, :] = buf[p, S : S + 2 * RANK, :]

    @pl.loop(0, S // 64)
    def _(i):
        rows = span(i * 64, 64)
        total = jnp.zeros((64, 1), F32)
        for p in range(PEERS):
            x = buf[p, rows, :].astype(F32)
            total += jnp.sum(x * x, axis=1, keepdims=True)
        r = lax.rsqrt(total / D + EPS)
        for p in range(PEERS):
            x = buf[p, rows, :].astype(F32)
            normed[rows, W * p : W * p + W] = (x * r * gain[:, W * p : W * p + W]).astype(BF)
        rinv[rows, :] = jnp.broadcast_to(r, (64, PAD))

    second.wait(0)
    second.start("b1", "b2")
    second.wait(1, 2)
    second.start("c1", "c2")
    second.wait(3, 4)
    second.start("d1", "d2")
    rows_in.step(3)
    second.wait(5, 6, 7, 8)
    ring.sent()
    second.sent()
    keep.wait()
    rows_in.finish()
    for copy in weights:
        copy.wait()


def gather_tokens(pay, gain, cot, win, wout, shard):
    rows = pay.shape[0]
    return pl.pallas_call(
        tokens_kernel,
        out_shape=(
            jax.ShapeDtypeStruct((S, D), BF),
            jax.ShapeDtypeStruct((S, PAD), F32),
            jax.ShapeDtypeStruct((PEERS, T, W), BF),
            jax.ShapeDtypeStruct((PEERS, PAD, W), BF),
            jax.ShapeDtypeStruct((PEERS, S, W), BF),
        )
        + (jax.ShapeDtypeStruct(win.shape, BF),) * 3
        + (jax.ShapeDtypeStruct(wout.shape, BF),) * 4
        + (jax.ShapeDtypeStruct((16, *shard.shape), BF),),
        in_specs=[VMEM, VMEM, ANY, ANY, ANY, ANY],
        out_specs=(VMEM, VMEM, VMEM, VMEM) + (ANY,) * 9,
        scratch_shapes=[
            pltpu.VMEM((PEERS, rows, W), BF),
            pltpu.SemaphoreType.DMA((9,)),
            pltpu.SemaphoreType.DMA((9,)),
            pltpu.SemaphoreType.DMA((9,)),
            pltpu.SemaphoreType.DMA((9,)),
            pltpu.SemaphoreType.DMA,
            pltpu.SemaphoreType.DMA((7,)),
            pltpu.SemaphoreType.DMA((7,)),
            *row_sems(),
        ],
        compiler_params=params(1, 63),
        cost_estimate=pl.CostEstimate(flops=5 * 10**10, bytes_accessed=10**7, transcendentals=0),
        name="tokens",
    )(pay, gain, cot, win, wout, shard)


def columns_to_rows(first, second):
    lane = lanes(first.shape[0])
    tile = jnp.where(lane == 0, first, jnp.where(lane == 1, second, 0.0))
    return jnp.transpose(tile)[0:8, :]


def rows_to_columns(rows):
    padded = jnp.concatenate([rows, jnp.zeros((PAD - 8, rows.shape[1]), F32)], axis=0)
    return jnp.transpose(padded)


def swap_start(stat, inbox, send, recv):
    c = lax.axis_index("col")
    for k in ORDER:
        to_peer(stat, inbox.at[c], send.at[k], recv.at[k], peer_of(k)).start()


def swap_finish(stat, inbox, send, recv):
    for k in ORDER:
        to_peer(stat, inbox.at[source_of(k)], send.at[k], recv.at[k], peer_of(k)).wait()
    total = stat[...]
    for k in range(1, PEERS):
        total += inbox[source_of(k)]
    return total


def attention_kernel(
    normed_in, wq, picks, up, qgain, kgain, cosine, sine,
    p0, po, pl0, pr0, x0, xo, xl, xr, xf,
    att_t, att, qo, ko, vo, qraw, kraw, cols, lat, bank, wmine, wother,
    pl1, pr1, pf0, pf1, yl, yr, yf, *rest,
):
    swapped, rest = rest[0:9], rest[9:]
    (
        w, wsem, stat, inbox, ssem, rsem, asend, arecv, osend, orecv, xsend, xrecv, psend, precv,
        normed, nsem, esend, erecv,
    ) = rest
    c = lax.axis_index("col")
    side = lax.rem(lax.axis_index("row"), 2)
    partner = lax.axis_index("row") + 1 - 2 * side
    barrier = greet()
    pl.semaphore_signal(barrier, inc=1, device_id={"row": partner}, device_id_type=MESH)
    greet_row(barrier, PLANE, UP, DOWN)
    first, last = pl.ds(0, 1), pl.ds(1, 1)
    weights = [
        along(src, dst, psend.at[n], precv.at[n], shift)
        for n, (src, dst, shift) in enumerate(
            (
                (po, pl1, UP), (po, pr1, DOWN),
                (pl0.at[first], pf0.at[first], UP), (pr0.at[last], pf0.at[last], DOWN),
                (xl, yl, PLANE), (xr, yr, PLANE), (xf, yf, PLANE),
                (pl1.at[first], pf1.at[first], UP), (pr1.at[last], pf1.at[last], DOWN),
            )
        )
    ]

    early = [
        pltpu.make_async_remote_copy(
            src_ref=src, dst_ref=dst, send_sem=esend.at[n], recv_sem=erecv.at[n],
            device_id={"row": partner}, device_id_type=MESH,
        )
        for n, (src, dst) in enumerate(zip((p0, po, pl0, pr0, x0, xo, xl, xr, xf), swapped))
    ]
    fetch = pltpu.make_async_copy(normed_in, normed, nsem)
    fetch.start()

    def out_part(rel, lo, n):
        if rel == (0, 0):
            return wq.at[pl.ds(8 * side + lo, n), 6 * T : 7 * T, :]
        return wmine.at[place(rel), lo : lo + n]

    ring = Gather(
        out_part, lambda src, dst, lo, n: wmine.at[place(src), lo : lo + n], 8, osend, orecv
    )

    def across(rel):
        n = PLACES.index(rel)
        return pltpu.make_async_remote_copy(
            src_ref=out_part(rel, 0, 8), dst_ref=wother.at[place(rel)],
            send_sem=xsend.at[n], recv_sem=xrecv.at[n],
            device_id={"row": partner}, device_id_type=MESH,
        )

    keep = pltpu.make_async_copy(out_part((0, 0), 0, 8), wmine.at[c], wsem.at[6])
    keep.start()
    loads = [
        pltpu.make_async_copy(
            wq.at[:, T * k : T * k + T, :], w.at[:, :, W * k : W * k + W], wsem.at[k]
        )
        for k in range(6)
    ]
    for load in loads:
        load.start()
    pl.semaphore_wait(barrier, PEERS + 3)
    ring.start("a0", "a1", "a2")
    for copy in weights[:4]:
        copy.start()
    for copy in early:
        copy.start()
    across((0, 0)).start()
    for load in loads:
        load.wait()
    fetch.wait()

    for i in range(4):
        tile = w[4 * i : 4 * i + 4, :, 3 * W :].reshape(4 * T, 3 * W)
        chosen = tile[:, 2 * W : 2 * W + PAD].astype(F32)
        for n in range(4):
            chosen += nn(tile[:, PAD * n : PAD * n + PAD], picks[n])
        bank[4 * T * i : 4 * T * i + 4 * T, :] = chosen.astype(BF)

    blocks = 4
    rows_of = S // blocks
    lane = lanes(rows_of)
    for i in range(blocks):
        rows = slice(i * rows_of, (i + 1) * rows_of)
        x = normed[rows, :]
        code = jnp.where(lane < 3 * RANK, nn(x, bank[...]), 0.0).astype(BF)
        lat[rows, :] = code
        parts = nn(x, w[:, :, 0 : 3 * W].reshape(D, 3 * W)) + nn(code, up[...])
        first_part, second_part = parts[:, 0:W], parts[:, W : 2 * W]
        qraw[rows, :] = first_part
        kraw[rows, :] = second_part
        vo[rows, :] = parts[:, 2 * W :].astype(BF)
        stat[:, rows] = columns_to_rows(
            jnp.sum(first_part * first_part, axis=1, keepdims=True),
            jnp.sum(second_part * second_part, axis=1, keepdims=True),
        )
    swap_start(stat, inbox, ssem, rsem)
    ring.wait(0)
    ring.start("b1", "b2")
    for copy in weights[4:7]:
        copy.start()
    ring.wait(1, 2)
    ring.start("c1", "c2")
    for rel in NEAR:
        across(rel).start()
    total = swap_finish(stat, inbox, ssem, rsem)
    scale = lax.rsqrt(total / D + EPS)
    for i in range(blocks):
        rows = slice(i * rows_of, (i + 1) * rows_of)
        column = rows_to_columns(scale[:, rows])
        cols[rows, :] = column
        for index, (raw, gain, out) in enumerate(((qraw, qgain, qo), (kraw, kgain, ko))):
            for h in range(2):
                feats = slice(HEAD * h, HEAD * h + HEAD)
                x = raw[rows, feats] * column[:, index : index + 1] * gain[:, feats]
                y = x * cosine[rows, :] + pltpu.roll(x, HEAD // 2, 1) * sine[rows, :]
                out[rows, feats] = y.astype(BF)
    for i in range(blocks):
        rows = slice(i * rows_of, (i + 1) * rows_of)
        seen = (i + 1) * rows_of
        allowed = lax.broadcasted_iota(jnp.int32, (rows_of, seen), 1) <= (
            lax.broadcasted_iota(jnp.int32, (rows_of, seen), 0) + i * rows_of
        )
        logs = []
        for h in range(2):
            feats = slice(HEAD * h, HEAD * h + HEAD)
            score = nt(qo[rows, feats], ko[0:seen, feats]) * FACTOR
            score = jnp.where(allowed, score, -1e30)
            top = jnp.max(score, axis=1, keepdims=True)
            weight = jnp.exp(score - top)
            norm = jnp.sum(weight, axis=1, keepdims=True)
            attend = (weight * (1.0 / norm)).astype(BF)
            att[rows, feats] = nn(attend, vo[0:seen, feats]).astype(BF)
            logs.append(top + jnp.log(norm))
        cols[rows, :] = jnp.where(
            lane == 2, logs[0], jnp.where(lane == 3, logs[1], cols[rows, :])
        )
        for p in (2 * i, 2 * i + 1):
            mine = slice(T * p, T * p + T)

            @pl.when(c != p)
            def _():
                to_peer(att.at[mine], att_t.at[c], asend.at[p], arecv.at[c], p).start()

            @pl.when(c == p)
            def _():
                att_t[p] = att[mine, :]

    ring.wait(3, 4)
    ring.start("d1", "d2")
    across((1, 1)).start()
    across((3, 1)).start()
    weights[0].wait_recv()
    weights[1].wait_recv()
    weights[7].start()
    weights[8].start()
    ring.wait(5, 6, 7, 8)
    across((2, 0)).start()
    across((2, 1)).start()
    for p in range(PEERS):

        @pl.when(c != p)
        def _():
            to_peer(
                att.at[T * p : T * p + T], att_t.at[p], asend.at[p], arecv.at[p], p
            ).wait()

    ring.sent()
    keep.wait()
    for rel in PLACES:
        across(rel).wait()
    weights[0].wait_send()
    weights[1].wait_send()
    for copy in weights[2:]:
        copy.wait()
    for copy in early:
        copy.wait()


def attention(normed, wq, picks, up, qgain, kgain, cosine, sine, inner, outer):
    full = jax.ShapeDtypeStruct((S, W), BF)
    wide = jax.ShapeDtypeStruct((S, W), F32)
    return pl.pallas_call(
        attention_kernel,
        out_shape=(
            jax.ShapeDtypeStruct((PEERS, T, W), BF),
            full, full, full, full, wide, wide,
            jax.ShapeDtypeStruct((S, PAD), F32),
            jax.ShapeDtypeStruct((S, PAD), BF),
            jax.ShapeDtypeStruct((D, PAD), BF),
            jax.ShapeDtypeStruct((PEERS, 8, T, W), BF),
            jax.ShapeDtypeStruct((PEERS, 8, T, W), BF),
        )
        + (jax.ShapeDtypeStruct(inner[0].shape, BF),) * 4
        + (jax.ShapeDtypeStruct(outer[0].shape, BF),) * 3
        + (jax.ShapeDtypeStruct(inner[0].shape, BF),) * 4
        + (jax.ShapeDtypeStruct(outer[0].shape, BF),) * 5,
        in_specs=[ANY, ANY, VMEM, VMEM, VMEM, VMEM, VMEM, VMEM] + [ANY] * 9,
        out_specs=(VMEM,) * 10 + (ANY,) * 18,
        scratch_shapes=[
            pltpu.VMEM((16, T, 6 * W), BF),
            pltpu.SemaphoreType.DMA((7,)),
            pltpu.VMEM((8, S), F32),
            pltpu.VMEM((PEERS, 8, S), F32),
            pltpu.SemaphoreType.DMA((PEERS,)),
            pltpu.SemaphoreType.DMA((PEERS,)),
            pltpu.SemaphoreType.DMA((PEERS,)),
            pltpu.SemaphoreType.DMA((PEERS,)),
            pltpu.SemaphoreType.DMA((9,)),
            pltpu.SemaphoreType.DMA((9,)),
            pltpu.SemaphoreType.DMA((PEERS,)),
            pltpu.SemaphoreType.DMA((PEERS,)),
            pltpu.SemaphoreType.DMA((9,)),
            pltpu.SemaphoreType.DMA((9,)),
            pltpu.VMEM((S, D), BF),
            pltpu.SemaphoreType.DMA,
            pltpu.SemaphoreType.DMA((9,)),
            pltpu.SemaphoreType.DMA((9,)),
        ],
        compiler_params=params(2, 63),
        cost_estimate=pl.CostEstimate(flops=3 * 10**10, bytes_accessed=10**7, transcendentals=0),
        name="attention",
    )(normed, wq, picks, up, qgain, kgain, cosine, sine, *inner, *outer)


def load_out(mine, other, wo, sem):
    half = lax.rem(lax.axis_index("row"), 2)
    copies = []
    for index, (src, side) in enumerate(((mine, half), (other, 1 - half))):
        for p in range(PEERS):
            copies.append(
                pltpu.make_async_copy(
                    src.at[p],
                    wo.at[span(side * (D // 2), D // 2), W * p : W * p + W],
                    sem.at[index * PEERS + p],
                )
            )
    return copies


def member_of(routes, rows):
    lane = lanes(rows)
    found = lane == routes[:, 0:1] + 64
    for j in range(1, 8):
        found = found | (lane == routes[:, j : j + 1] + 64)
    return found


def state_kernel(
    att_t, mine, other, resid, extra, gain, bank, ru, routes,
    pay, state, prob_out, branch, lat_out,
    wo, sem,
):
    loads = load_out(mine, other, wo, sem)
    for load in loads:
        load.start()
    lane = lanes(T)
    lat = jnp.zeros((T, PAD), F32)
    for p in range(PEERS):
        lat += nt(att_t[p], extra[p])
    lat = jnp.where(lane < RANK, lat, 0.0)
    lat_out[...] = lat
    moved = pltpu.roll(lat, RANK, 1).astype(BF)
    x = jnp.concatenate([att_t[p] for p in range(PEERS)], axis=1)
    for load in loads:
        load.wait()
    total = jnp.zeros((T, 1), F32)
    for p in range(PEERS):
        feats = slice(W * p, W * p + W)
        part = nt(x, wo[feats, :]) + nn(moved, extra[p])
        branch[:, feats] = part.astype(BF)
        st = resid[p].astype(F32) + part
        state[:, feats] = st
        total += jnp.sum(st * st, axis=1, keepdims=True)
    r = lax.rsqrt(total / D + EPS)
    first = jnp.zeros((T, PAD), F32)
    for p in range(PEERS):
        feats = slice(W * p, W * p + W)
        m = (state[:, feats] * r * gain[:, feats]).astype(BF)
        pay[:, feats] = m
        first += nn(m, bank[feats, 0:PAD])
    code = jnp.where((lane >= 48) & (lane < 64), first, 0.0).astype(BF)
    valid = (lane >= 64) & (lane < 80)
    logits = jnp.where(valid, first + nn(code, ru[...]), -1e30)
    shifted = jnp.where(valid, jnp.exp(logits - jnp.max(logits, axis=1, keepdims=True)), 0.0)
    prob = shifted / jnp.sum(shifted, axis=1, keepdims=True)
    prob_out[...] = prob
    gate = jnp.where(member_of(routes, T), prob, 0.0)
    high = gate.astype(BF).astype(F32)
    low = pltpu.roll(gate - high, RANK, 1)
    pay[:, D:] = jnp.where(lane < 64, code.astype(F32), jnp.where(lane < 80, high, low)).astype(BF)


def to_state(att_t, mine, other, resid, extra, gain, bank, ru, routes):
    return pl.pallas_call(
        state_kernel,
        out_shape=(
            jax.ShapeDtypeStruct((T, D + PAD), BF),
            jax.ShapeDtypeStruct((T, D), F32),
            jax.ShapeDtypeStruct((T, PAD), F32),
            jax.ShapeDtypeStruct((T, D), BF),
            jax.ShapeDtypeStruct((T, PAD), F32),
        ),
        in_specs=[VMEM, ANY, ANY, VMEM, VMEM, VMEM, VMEM, VMEM, VMEM],
        out_specs=(VMEM,) * 5,
        scratch_shapes=[pltpu.VMEM((D, D), BF), pltpu.SemaphoreType.DMA((2 * PEERS,))],
        compiler_params=params(None, 63),
        cost_estimate=pl.CostEstimate(flops=10**10, bytes_accessed=10**7, transcendentals=0),
        name="state",
    )(att_t, mine, other, resid, extra, gain, bank, ru, routes)


EARLY_IN, LATE_IN = (0, 1, 2, 4), (3, 5, 6, 7)
EARLY_OUT, LATE_OUT = (0, 1, 2, 4, 6), (3, 5, 7)
SHIFTS = ((0, 0), (1, 0), (0, 3), (1, 3), (0, 1), (1, 1), (0, 2), (1, 2))
CHUNK = 256
TILE = 512
STEPS = (1, 2, 3)
LAST = 0


def expert_kernel(*refs):
    pay, branch, cot, ebank, upin, ad = refs[0:6]
    pin, pout, ein, eout = refs[6:14], refs[14:22], refs[22:26], refs[26:31]
    refs = refs[9:]
    mixed, summed, xout, gup, glow, glift, gdown = refs[22:29]
    (xfull, win, wd, cbuf, obuf, rbuf, a1, act, hid, vg, gg, ug, mix, xacc,
     aup, alow, alift, adown,
     lsem, csend, crecv, csem, send1, recv1, send2, recv2, xsem, mbank, bsend, brecv, esem) = refs[29:]
    c = lax.axis_index("col")
    r = lax.axis_index("row")
    half = lax.rem(r, 2)
    partner = r + 1 - 2 * half
    barrier = greet()

    def offset(shift, side):
        plane = lax.rem(r // 8 + shift[0], 2)
        place = lax.rem(lax.rem(r, 8) // 2 + shift[1], 4)
        return (plane * 8 + place * 2 + side) * T

    def inner(i, src, side):
        return (src, win.at[:, :, span(offset(SHIFTS[i], side), T), :], 2 * i)

    def outer(i, src, side):
        return (src, wd.at[:, :, span(offset(SHIFTS[i], side), T)], 2 * i + 1)

    def across(side, kind):
        late = [inner(i, pin[i], side) for i in LATE_IN] if kind == 0 else [
            outer(i, pout[i], side) for i in LATE_OUT
        ]
        return [
            pltpu.make_async_remote_copy(
                src_ref=src, dst_ref=dst, send_sem=csend.at[n], recv_sem=crecv.at[n],
                device_id={"row": partner}, device_id_type=MESH,
            )
            for src, dst, n in late
        ]

    def local(kind):
        made, pieces, early, others = (
            (inner, pin, EARLY_IN, ein), (outer, pout, EARLY_OUT, eout)
        )[kind]
        every = [made(i, pieces[i], half) for i in range(8)]
        copies = [pltpu.make_async_copy(src, dst, lsem.at[n]) for src, dst, n in every]
        every = [made(i, src, 1 - half) for i, src in zip(early, others)]
        copies += [pltpu.make_async_copy(src, dst, esem.at[n]) for src, dst, n in every]
        return copies

    sources = [place(rel) for rel in PLACES]

    def source(step, t):
        chosen = sources[2 * LAST + t]
        for j in range(3):
            chosen = jnp.where(step == j, sources[2 * STEPS[j] + t], chosen)
        return chosen

    def cot_copies(step, slot):
        return [
            pltpu.make_async_copy(
                cot.at[:, span(source(step, t) * T, T), :],
                cbuf.at[slot, :, T * t : T * t + T, :],
                csem.at[2 * slot + t],
            )
            for t in range(2)
        ]

    ring = Gather(
        lambda rel, lo, n: xfull.at[pl.ds(T * PLACES.index(rel) + lo, n)],
        lambda src, dst, lo, n: xfull.at[pl.ds(T * PLACES.index(dst) + lo, n)],
        T, send1, recv1,
    )
    for n in range(1, 16):
        pl.semaphore_signal(
            barrier, inc=1, device_id={"row": lax.rem(r + n, 16)}, device_id_type=MESH
        )

    def bank_copy(n):
        q = lax.rem(r + n, 16)
        return pltpu.make_async_remote_copy(
            src_ref=ebank.at[q], dst_ref=mbank.at[r], send_sem=bsend.at[n], recv_sem=brecv.at[n],
            device_id={"row": q}, device_id_type=MESH,
        )

    def bank_arrival(n):
        q = lax.rem(r + 16 - n, 16)
        return pltpu.make_async_remote_copy(
            src_ref=ebank.at[q], dst_ref=mbank.at[q], send_sem=bsend.at[n], recv_sem=brecv.at[n],
            device_id={"row": q}, device_id_type=MESH,
        )

    def bank(at):
        return mbank[at // T : (at + TILE) // T].reshape(TILE, PAD)

    def whole_bank():
        return mbank[...].reshape(D, PAD)

    xfull[0:T, :] = pay[...]
    mbank[r] = ebank[r]
    pl.semaphore_wait(barrier, PEERS + 14)
    ring.start("a0", "a1", "a2")
    for n in range(1, 16):
        bank_copy(n).start()
    for kind in range(2):
        for copy in across(half, kind):
            copy.start()
        for copy in local(kind):
            copy.start()
    for copy in cot_copies(0, 0):
        copy.start()
    aup[...] = jnp.zeros_like(aup)
    alow[...] = jnp.zeros_like(alow)
    alift[...] = jnp.zeros_like(alift)
    adown[...] = jnp.zeros_like(adown)
    lane = lanes(CHUNK)
    ring.wait(0)
    ring.start("b1", "b2")
    ring.wait(1, 2)
    ring.start("c1", "c2")
    for n in range(1, 16):
        bank_arrival(n).wait_recv()
    for n in range(1, 16):
        bank_copy(n).wait_send()
    def weights_here(kind):
        for copy in local(kind):
            copy.wait()
        for copy in across(half, kind):
            copy.wait_send()
        for copy in across(1 - half, kind):
            copy.wait_recv()

    weights_here(0)

    def chunk(j, carry):
        rows = span(lax.rem(j + STEPS[0], 4) * CHUNK, CHUNK)
        slot = lax.rem(j, 2)

        @pl.when(j == 1)
        def _():
            ring.wait(3, 4)
            ring.start("d1", "d2")

        @pl.when(j == 2)
        def _():
            ring.wait(5, 6, 7, 8)

        for copy in cot_copies(j, slot):
            copy.wait()

        @pl.when(j < 3)
        def _():
            for copy in cot_copies(j + 1, 1 - slot):
                copy.start()

        mix[...] = jnp.zeros_like(mix)

        @pl.when(j == 3)
        def _():
            mix[0:T, :] = branch[...].astype(F32)

        extras = xfull[rows, D : D + PAD].astype(F32)
        inlat = nn(xfull[rows, 0:D], whole_bank()).astype(BF)
        gate_grads = []
        ilg_total = jnp.zeros((CHUNK, PAD), F32)
        for e in range(2):
            spot = 64 + 2 * c + e
            gate = jnp.sum(
                jnp.where((lane == spot) | (lane == spot + RANK), extras, 0.0),
                axis=1, keepdims=True,
            )

            for f in range(FF // TILE):
                fs = slice(f * TILE, f * TILE + TILE)
                x = xfull[rows, 0:D]
                g = nn(x, win[e, 0, :, fs]) + nn(inlat, upin[2 * e, :, fs])
                u = nn(x, win[e, 1, :, fs]) + nn(inlat, upin[2 * e + 1, :, fs])
                sg = 1.0 / (1.0 + jnp.exp(-g))
                silu = g * sg
                act[:, fs] = silu
                a1[:, fs] = u * sg * (1.0 + g * (1.0 - sg))
                hid[:, fs] = (silu * u).astype(BF)

            if e == 0:

                @pl.when(j == 0)
                def _():
                    weights_here(1)

            dl = nn(hid[...], ad[e]).astype(BF)

            gsum = jnp.zeros((CHUNK, 1), F32)
            for d in range(D // TILE):
                ds = slice(d * TILE, d * TILE + TILE)
                ev = nn(hid[...], wd[e, :, ds]) + nt(dl, bank(d * TILE))
                halves = [cbuf[slot, 2 * d + m] for m in range(TILE // W)]
                ct = jnp.concatenate(halves, axis=1).astype(F32)
                vg[:, ds] = (ct * gate).astype(BF)
                total = mix[:, ds] + ev * gate
                if e == 0:
                    mix[:, ds] = total
                else:
                    for t in range(2):
                        for m in range(TILE // W):
                            mixed[2 * d + m, span(source(j, t) * T, T), :] = total[
                                T * t : T * t + T, W * m : W * m + W
                            ].astype(BF)
                gsum += jnp.sum(ev * ct, axis=1, keepdims=True)
            gate_grads.append(gsum)
            low = 80 + RANK * e
            dlg = jnp.where(
                (lane >= low) & (lane < low + RANK), nn(vg[...], whole_bank()), 0.0
            ).astype(BF)

            for f in range(FF // TILE):
                fs = slice(f * TILE, f * TILE + TILE)
                hg = nt(vg[...], wd[e, fs, :]) + nt(dlg, ad[e, fs, :])
                gg[:, fs] = (hg * a1[:, fs]).astype(BF)
                ug[:, fs] = (hg * act[:, fs]).astype(BF)

            ilg_total += nt(gg[...], upin[2 * e]) + nt(ug[...], upin[2 * e + 1])
            ilg = ilg_total.astype(BF)

            for d in range(D // TILE):
                ds = slice(d * TILE, d * TILE + TILE)
                t = nt(gg[...], win[e, 0, ds, :]) + nt(ug[...], win[e, 1, ds, :])
                if e == 0:
                    xacc[:, ds] = t
                else:
                    t += nt(ilg, bank(d * TILE))
                    obuf[rows, ds] = (xacc[:, ds] + t).astype(BF)

            for n, grad in ((2 * e, gg), (2 * e + 1, ug)):
                aup[n] += tn(inlat, grad[...])[RANK * n : RANK * n + RANK, :]
            alow[e] += tn(dlg, hid[...])[low : low + RANK, :]
            alift[e] += tn(dl, vg[...])[low : low + RANK, :]
        adown[...] += tn(ilg_total.astype(BF), xfull[rows, 0:D])[0 : 4 * RANK, :]
        obuf[rows, D : D + PAD] = jnp.where(
            lane == 64 + 2 * c, gate_grads[0], jnp.where(lane == 65 + 2 * c, gate_grads[1], 0.0)
        ).astype(BF)
        for step in range(4):

            @pl.when(j == step)
            def _():
                for t in range(2):
                    n = 2 * ((step + STEPS[0]) % 4) + t
                    if n:
                        back_to(n).start()

        return carry

    def back_to(n):
        rel = PLACES[n]
        seen = PLACES.index(((4 - rel[0]) % 4, rel[1]))
        return to_peer(
            obuf.at[pl.ds(T * n, T)], rbuf.at[seen], send2.at[n], recv2.at[seen], place(rel)
        )

    lax.fori_loop(0, 4, chunk, 0)
    keep = [
        pltpu.make_async_copy(
            xfull.at[pl.ds(T * n, T)], xout.at[span(sources[n] * T, T)], xsem.at[n]
        )
        for n in range(PEERS)
    ]
    for copy in keep:
        copy.start()
    gup[...] = aup[...].astype(BF)
    glow[...] = alow[...].astype(BF)
    glift[...] = alift[...].astype(BF)
    gdown[...] = adown[...].astype(BF)
    ring.sent()
    for n in range(1, PEERS):
        back_to(n).wait_send()
        to_peer(
            obuf.at[pl.ds(T * n, T)], rbuf.at[n], send2.at[n], recv2.at[n], place(PLACES[n])
        ).wait_recv()
    for copy in keep:
        copy.wait()

    @pl.loop(0, T // 32)
    def _(i):
        at = span(i * 32, 32)
        total = obuf[at, :].astype(F32)
        for n in range(1, PEERS):
            total += rbuf[n, at, :].astype(F32)
        summed[at, :] = total


def experts(pay, branch, cot, bank, upin, ad, pin, pout, ein, eout):
    sems = pltpu.SemaphoreType.DMA
    return pl.pallas_call(
        expert_kernel,
        out_shape=(
            jax.ShapeDtypeStruct((PEERS, S, W), BF),
            jax.ShapeDtypeStruct((T, D + PAD), F32),
            jax.ShapeDtypeStruct((S, D + PAD), BF),
            jax.ShapeDtypeStruct((4, RANK, FF), BF),
            jax.ShapeDtypeStruct((2, RANK, FF), BF),
            jax.ShapeDtypeStruct((2, RANK, D), BF),
            jax.ShapeDtypeStruct((4 * RANK, D), BF),
        ),
        in_specs=[VMEM, VMEM, ANY, VMEM, VMEM, VMEM] + [ANY] * 25,
        out_specs=(VMEM, VMEM, ANY, VMEM, VMEM, VMEM, VMEM),
        scratch_shapes=[
            pltpu.VMEM((S, D + PAD), BF),
            pltpu.VMEM((2, 2, D, FF), BF),
            pltpu.VMEM((2, FF, D), BF),
            pltpu.VMEM((2, PEERS, CHUNK, W), BF),
            pltpu.VMEM((S, D + PAD), BF),
            pltpu.VMEM((PEERS, T, D + PAD), BF),
            pltpu.VMEM((CHUNK, FF), F32),
            pltpu.VMEM((CHUNK, FF), F32),
            pltpu.VMEM((CHUNK, FF), BF),
            pltpu.VMEM((CHUNK, D), BF),
            pltpu.VMEM((CHUNK, FF), BF),
            pltpu.VMEM((CHUNK, FF), BF),
            pltpu.VMEM((CHUNK, D), F32),
            pltpu.VMEM((CHUNK, D), F32),
            pltpu.VMEM((4, RANK, FF), F32),
            pltpu.VMEM((2, RANK, FF), F32),
            pltpu.VMEM((2, RANK, D), F32),
            pltpu.VMEM((4 * RANK, D), F32),
            sems((16,)), sems((16,)), sems((16,)), sems((4,)),
            sems((9,)), sems((9,)), sems((PEERS,)), sems((PEERS,)), sems((PEERS,)),
            pltpu.VMEM((16, T, PAD), BF), sems((16,)), sems((16,)), sems((16,)),
        ],
        compiler_params=params(3, 63),
        cost_estimate=pl.CostEstimate(flops=10**11, bytes_accessed=10**7, transcendentals=0),
        name="experts",
    )(pay, branch, cot, bank, upin, ad, *pin, *pout, *ein, *eout)


HALVES = (slice(0, S // 2), slice(S // 2, S))


class Scatter:
    def __init__(self, parts, passing, near, last, send, recv):
        self.parts, self.passing, self.near, self.last = parts, passing, near, last
        self.send, self.recv = send, recv

    def piece(self, rel, half):
        return self.parts.at[PLACES.index(rel), HALVES[half]]

    def copy(self, kind, y, half):
        up, down = (1, 0), (3, 0)
        if kind == "far":
            to, src, dst = (up, down)[half], self.piece((2, y), half), self.passing.at[half, y]
        elif kind == "plain":
            to, rel = ((down, (3, y)), (up, (1, y)))[half]
            src, dst = self.piece(rel, half), self.near.at[0, half, y]
        elif kind == "summed":
            to, rel = ((up, (1, y)), (down, (3, y)))[half]
            src, dst = self.piece(rel, half), self.near.at[1, half, y]
        else:
            to, src, dst = (0, 1), self.piece((0, 1), half), self.last.at[half]
        n = ("far", "plain", "summed", "plane").index(kind) * 4 + 2 * y + half
        return to_peer(src, dst, self.send.at[n], self.recv.at[n], place(to))

    def ready(self, slot):
        rel = PLACES[slot]
        if rel[0] == 2:
            for half in range(2):
                self.copy("far", rel[1], half).start()
        elif rel[0]:
            self.copy("plain", rel[1], 1 if rel[0] == 1 else 0).start()

    def add(self, rel, half, others):
        slot, at = PLACES.index(rel), HALVES[half].start

        @pl.loop(0, S // 2 // 128)
        def _(i):
            rows, there = span(i * 128, 128), pl.ds(pl.multiple_of(at + i * 128, 128), 128)
            total = self.parts[slot, there, :].astype(F32)
            for other in others:
                total += other[rows, :].astype(F32)
            self.parts[slot, there, :] = total.astype(BF)

    def middle(self):
        for y in (1, 0):
            for half in range(2):
                self.copy("far", y, half).wait_recv()
                rel = ((1, y), (3, y))[half]
                self.add(rel, half, [self.passing.at[half, y]])
                self.copy("summed", y, half).start()

    def other_plane(self):
        for half in range(2):
            self.copy("plain", 1, half).wait_recv()
            self.copy("summed", 1, half).wait_recv()
            self.add((0, 1), half, [self.near.at[k, half, 1] for k in range(2)])
            self.copy("plane", 0, half).start()

    def end(self):
        for half in range(2):
            self.copy("plain", 0, half).wait_recv()
            self.copy("summed", 0, half).wait_recv()
            self.copy("plane", 0, half).wait_recv()

    def arrived(self, half, rows):
        kept = [self.near[k, half, 0, rows, :].astype(F32) for k in range(2)]
        return kept[0] + kept[1] + self.last[half, rows, :].astype(F32)

    def sent(self):
        for kind in ("far", "plain", "summed"):
            for y in range(2):
                for half in range(2):
                    self.copy(kind, y, half).wait_send()
        for half in range(2):
            self.copy("plane", 0, half).wait_send()


def back_kernel(
    summed, state, prob, routes, bank, ru, gain, cot, mine, other, extra, lat_o,
    q, k_, v, att, cols, qraw, kraw, qgain, kgain, cosine, sine, up, lat, xfull_in, normed_in, flat_in, mixture, tokens,
    pg, bgc, stat3, lcg, gqkvup, goutdown, goutup, grup, growdown, flat, mixed,
    wo, sem, bg, sbuf, abuf, dq, dk, dv, stat, inbox, ex,
    send1, recv1, send2, recv2, send3, recv3, xfull, normed, fsem, parts, passing, near, last, msem, send4, recv4, cot_t, *sems,
):
    c = lax.axis_index("col")
    barrier = greet()
    greet_row(barrier, PLANE, UP, DOWN)
    greet_partner(barrier)
    rows_in = RowGather(flat_in, flat, 6 * RANK, sems)
    loads = load_out(mine, other, wo, sem)
    for load in loads:
        load.start()
    fetches = [
        pltpu.make_async_copy(xfull_in, xfull, fsem.at[0]),
        pltpu.make_async_copy(normed_in, normed, fsem.at[1]),
    ]
    own = pltpu.make_async_copy(cot.at[:, span(c * T, T), :], cot_t, fsem.at[2])
    own.start()
    mix = Scatter(parts, passing, near, last, send4, recv4)
    fill = [
        pltpu.make_async_copy(mixture.at[place(rel)], parts.at[n], msem.at[n])
        for n, rel in enumerate(PLACES)
    ]
    for copy in fill:
        copy.start()
    for copy in fetches:
        copy.start()
    lane = lanes(T)
    p_ = prob[...]
    gg = jnp.where(member_of(routes, T), summed[:, D : D + PAD], 0.0)
    lgrad = (p_ * (gg - jnp.sum(p_ * gg, axis=1, keepdims=True))).astype(BF)
    rlg = nt(lgrad, ru[...]).astype(BF)
    both = jnp.where(lane < 64, rlg.astype(F32), lgrad.astype(F32)).astype(BF)
    total = jnp.zeros((T, 1), F32)
    for p in range(PEERS):
        feats = slice(W * p, W * p + W)
        st = state[:, feats]
        total += jnp.sum(st * st, axis=1, keepdims=True)
    r = lax.rsqrt(total / D + EPS)
    mean = jnp.zeros((T, 1), F32)
    for p in range(PEERS):
        feats = slice(W * p, W * p + W)
        m = (summed[:, feats] + nt(both, bank[feats, 0:PAD])) * gain[:, feats]
        mean += jnp.sum(state[:, feats] * m, axis=1, keepdims=True)
    mean = mean / D
    olg = jnp.zeros((T, PAD), F32)
    own.wait()
    for p in range(PEERS):
        feats = slice(W * p, W * p + W)
        m = (summed[:, feats] + nt(both, bank[feats, 0:PAD])) * gain[:, feats]
        st = state[:, feats]
        grad = (cot_t[p].astype(F32) + r * m - st * (r * r * r) * mean).astype(BF)
        bg[p] = grad
        olg += nt(grad, extra[p])
    olg = jnp.where((lane >= RANK) & (lane < 2 * RANK), olg, 0.0)
    moved = pltpu.roll(olg, PAD - RANK, 1).astype(BF)
    info = jnp.where(
        lane < RANK, lat_o[...], jnp.where(lane < 2 * RANK, olg, both.astype(F32))
    ).astype(BF)
    x = jnp.concatenate([bg[p] for p in range(PEERS)], axis=1)
    for load in loads:
        load.wait()
    pl.semaphore_wait(barrier, PEERS - 1 + 4)
    rows_in.start()
    for n in (4, 3, 5, 2, 6, 1, 7, 0):
        d = peer_of(n)
        part = nn(x, wo[:, span(d * W, W)]) + nn(moved, extra[d])
        sbuf[d, :, 0:W] = part.astype(BF)
        sbuf[d, :, W : W + PAD] = info
        if n:
            to_peer(sbuf.at[d], abuf.at[c], send1.at[n], recv1.at[n], d).start()
        else:
            abuf[c] = sbuf[c]
            bgc[c] = bg[c]
    for copy in fill:
        copy.wait()
    for n in ORDER:
        d = peer_of(n)
        to_peer(sbuf.at[d], abuf.at[source_of(n)], send1.at[n], recv1.at[n], d).wait()
    for slot in (7, 6, 4, 5, 2, 3):
        mix.ready(slot)
    for n in ORDER:
        d = peer_of(n)
        to_peer(bg.at[d], bgc.at[c], send2.at[n], recv2.at[n], d).start()
    rows_in.step(0)
    rows_in.step(1)
    for p in range(PEERS):
        ex[T * p : T * p + T, :] = abuf[p, :, W : W + PAD]

    blocks = 4
    size = S // blocks
    for h in range(2):
        feats = slice(HEAD * h, HEAD * h + HEAD)
        for i in reversed(range(blocks)):
            rows = slice(i * size, (i + 1) * size)
            seen = (i + 1) * size
            allowed = lax.broadcasted_iota(jnp.int32, (size, seen), 1) <= (
                lax.broadcasted_iota(jnp.int32, (size, seen), 0) + i * size
            )
            g = jnp.concatenate([abuf[2 * i, :, feats], abuf[2 * i + 1, :, feats]], axis=0)
            qb = q[rows, feats]
            kb = k_[0:seen, feats]
            score = nt(qb, kb) * FACTOR
            full = jnp.where(allowed, jnp.exp(score - cols[rows, 2 + h : 3 + h]), 0.0)
            wgrad = nt(g, v[0:seen, feats])
            center = jnp.sum(full * wgrad, axis=1, keepdims=True)
            sgrad = (full * (wgrad - center)).astype(BF)
            dq[rows, feats] = nn(sgrad, kb) * FACTOR
            dvp = tn(full.astype(BF), g)
            dkp = tn(sgrad, qb) * FACTOR
            if i == blocks - 1:
                dv[0:seen, feats] = dvp
                dk[0:seen, feats] = dkp
            else:
                dv[0:seen, feats] += dvp
                dk[0:seen, feats] += dkp
    for i in range(blocks):
        rows = slice(i * size, (i + 1) * size)
        dots = []
        for raw, gain_, grads in ((qraw, qgain, dq), (kraw, kgain, dk)):
            dot = jnp.zeros((size, 1), F32)
            for h in range(2):
                feats = slice(HEAD * h, HEAD * h + HEAD)
                y = grads[rows, feats]
                y = y * cosine[rows, :] - pltpu.roll(y, HEAD // 2, 1) * sine[rows, :]
                y = y * gain_[:, feats]
                grads[rows, feats] = y
                dot += jnp.sum(y * raw[rows, feats], axis=1, keepdims=True)
            dots.append(dot)
        stat[:, rows] = columns_to_rows(*dots)
    swap_start(stat, inbox, send3, recv3)
    mix.middle()
    rows_in.step(2)
    for copy in fetches:
        copy.wait()
    goutdown[...] = tn(ex[...], att[...])[RANK : 2 * RANK, :].astype(BF)
    grup[...] = tn(xfull[:, D : D + PAD], ex[...])[48:64, :].astype(BF)
    growdown[3 * RANK : 4 * RANK, :] = tn(ex[...], xfull[:, 0:D])[48:64, :].astype(BF)
    dots = swap_finish(stat, inbox, send3, recv3)
    wide = lanes(size)
    for i in range(blocks):
        rows = slice(i * size, (i + 1) * size)
        column = rows_to_columns(dots[:, rows])
        stat_sum = jnp.zeros((size, 1), F32)
        code = jnp.zeros((size, PAD), F32)
        for n, (raw, grads) in enumerate(((qraw, dq), (kraw, dk))):
            rs = cols[rows, n : n + 1]
            x = raw[rows, :]
            y = rs * grads[rows, :] - x * (rs * rs * rs * column[:, n : n + 1] / D)
            y = y.astype(BF)
            pg[rows, W * n : W * n + W] = y
            stat_sum += jnp.sum(y.astype(F32) * x, axis=1, keepdims=True)
            code += nt(y, up[:, W * n : W * n + W])
        y = dv[rows, :].astype(BF)
        pg[rows, 2 * W : 3 * W] = y
        stat_sum += jnp.sum(y.astype(F32) * v[rows, :].astype(F32), axis=1, keepdims=True)
        code += nt(y, up[:, 2 * W : 3 * W])
        lcg[rows, :] = jnp.where(wide < 3 * RANK, code, 0.0).astype(BF)
        stat3[:, rows] = columns_to_rows(stat_sum, stat_sum)
    mix.other_plane()
    for n in range(3):
        gqkvup[n] = tn(lat[...], pg[:, W * n : W * n + W])[RANK * n : RANK * n + RANK, :].astype(BF)
    growdown[0 : 3 * RANK, :] = tn(lcg[...], normed[...])[0 : 3 * RANK, :].astype(BF)
    for n in ORDER:
        d = peer_of(n)
        to_peer(bg.at[d], bgc.at[source_of(n)], send2.at[n], recv2.at[n], d).wait()
    acc = jnp.zeros((PAD, W), F32)
    for p in range(PEERS):
        acc += tn(ex[T * p : T * p + T, :], bgc[p])
    goutup[...] = acc[0:RANK, :].astype(BF)
    mix.end()
    rows_in.step(3)
    for half in range(2):

        @pl.loop(0, S // 2 // 64)
        def _(i):
            rows = span(i * 64, 64)
            there = pl.ds(pl.multiple_of(half * (S // 2) + i * 64, 64), 64)
            total = tokens[there, :].astype(F32) + parts[0, there, :].astype(F32)
            mixed[there, :] = (total + mix.arrived(half, rows)).astype(BF)

    mix.sent()
    rows_in.finish()


def back(*args):
    sems = pltpu.SemaphoreType.DMA((PEERS,))
    kinds = [VMEM] * len(args)
    kinds[8] = ANY
    kinds[9] = ANY
    kinds[25] = ANY
    kinds[26] = ANY
    kinds[27] = ANY
    kinds[28] = ANY
    kinds[7] = ANY
    return pl.pallas_call(
        back_kernel,
        out_shape=(
            jax.ShapeDtypeStruct((S, 3 * W), BF),
            jax.ShapeDtypeStruct((PEERS, T, W), BF),
            jax.ShapeDtypeStruct((8, S), F32),
            jax.ShapeDtypeStruct((S, PAD), BF),
            jax.ShapeDtypeStruct((3, RANK, W), BF),
            jax.ShapeDtypeStruct((RANK, W), BF),
            jax.ShapeDtypeStruct((RANK, W), BF),
            jax.ShapeDtypeStruct((RANK, PAD), BF),
            jax.ShapeDtypeStruct((4 * RANK, D), BF),
            jax.ShapeDtypeStruct((16, 6 * RANK, FF), BF),
            jax.ShapeDtypeStruct((S, W), BF),
        ),
        in_specs=kinds,
        out_specs=(VMEM,) * 9 + (ANY, VMEM),
        scratch_shapes=[
            pltpu.VMEM((D, D), BF),
            pltpu.SemaphoreType.DMA((2 * PEERS,)),
            pltpu.VMEM((PEERS, T, W), BF),
            pltpu.VMEM((PEERS, T, W + PAD), BF),
            pltpu.VMEM((PEERS, T, W + PAD), BF),
            pltpu.VMEM((S, W), F32),
            pltpu.VMEM((S, W), F32),
            pltpu.VMEM((S, W), F32),
            pltpu.VMEM((8, S), F32),
            pltpu.VMEM((PEERS, 8, S), F32),
            pltpu.VMEM((S, PAD), BF),
            sems, sems, sems, sems, sems, sems,
            pltpu.VMEM((S, D + PAD), BF),
            pltpu.VMEM((S, D), BF),
            pltpu.SemaphoreType.DMA((3,)),
            pltpu.VMEM((PEERS, S, W), BF),
            pltpu.VMEM((2, 2, S // 2, W), BF),
            pltpu.VMEM((2, 2, 2, S // 2, W), BF),
            pltpu.VMEM((2, S // 2, W), BF),
            sems,
            pltpu.SemaphoreType.DMA((16,)),
            pltpu.SemaphoreType.DMA((16,)),
            pltpu.VMEM((PEERS, T, W), BF),
            *row_sems(),
        ],
        compiler_params=params(4, 63),
        cost_estimate=pl.CostEstimate(flops=4 * 10**10, bytes_accessed=10**7, transcendentals=0),
        name="back",
    )(*args)


GROUPS = 10


def input_kernel(
    pg, lcg, wq, bank, stat3, bgc, tokens, rinv, gain,
    picked, gdown, glift, growdown, gqkvup, goutdown, goutup, grup,
    out, gin, glif, grout, gqkvdown, gqkvup_all, gout, goutup_all, grup_all,
    w, wsem, own, sbuf, passing, near, last, inbox,
    tall, thin, tallbuf, thinbuf, tallsum, thinsum, mine, theirs,
    send, recv, send3, recv3, send4, recv4, send5, recv5, send6, recv6,
):
    c = lax.axis_index("col")
    r = lax.axis_index("row")
    barrier = greet()
    for n in range(1, 16):
        pl.semaphore_signal(
            barrier, inc=1, device_id={"row": lax.rem(r + n, 16)}, device_id_type=MESH
        )
    loads = [
        pltpu.make_async_copy(
            wq.at[:, T * k : T * k + T, :], w.at[:, :, W * k : W * k + W], wsem.at[k]
        )
        for k in range(3)
    ]
    for load in loads:
        load.start()
    for p in range(16):
        at = slice(T * p, T * p + T)
        tall[p, 0 : 4 * RANK, :] = gdown[:, at]
        tall[p, 4 * RANK : 6 * RANK, :] = glift[:, at]
        tall[p, 6 * RANK : 10 * RANK, :] = growdown[:, at]
    thin[0 : 3 * RANK, :] = gqkvup[...]
    thin[3 * RANK : 4 * RANK, :] = goutdown[...]
    thin[4 * RANK : 5 * RANK, :] = goutup[...]
    thin[5 * RANK : 6 * RANK, 0:PAD] = grup[...]
    thin[5 * RANK : 6 * RANK, PAD:W] = jnp.zeros((RANK, PAD), BF)
    for load in loads:
        load.wait()
    pl.semaphore_wait(barrier, PEERS - 1 + 15)

    def row_copies(n):
        p = lax.rem(r + n, 16)
        where = {"row": p}
        return [
            pltpu.make_async_remote_copy(
                src_ref=tall.at[p], dst_ref=tallbuf.at[r],
                send_sem=send4.at[n], recv_sem=recv4.at[n],
                device_id=where, device_id_type=MESH,
            ),
            pltpu.make_async_remote_copy(
                src_ref=thin, dst_ref=thinbuf.at[r], send_sem=send5.at[n], recv_sem=recv5.at[n],
                device_id=where, device_id_type=MESH,
            ),
        ]

    def row_arrivals(n):
        p = lax.rem(r + 16 - n, 16)
        where = {"row": p}
        return [
            pltpu.make_async_remote_copy(
                src_ref=tallbuf.at[p], dst_ref=tallbuf.at[p],
                send_sem=send4.at[n], recv_sem=recv4.at[n],
                device_id=where, device_id_type=MESH,
            ),
            pltpu.make_async_remote_copy(
                src_ref=thin, dst_ref=thinbuf.at[p], send_sem=send5.at[n], recv_sem=recv5.at[n],
                device_id=where, device_id_type=MESH,
            ),
        ]

    for n in range(1, 16):
        for copy in row_copies(n):
            copy.start()
    tallbuf[r] = tall[r]
    thinbuf[r] = thin[...]
    swap_start(stat3, inbox, send3, recv3)
    ring = Scatter(sbuf, passing, near, last, send, recv)
    for slot in (7, 6, 4, 5, 2, 3, 1, 0):
        d = place(PLACES[slot])
        wide = span(d * W, W)
        for i in range(2):
            rows = slice(512 * i, 512 * i + 512)
            part = nt(lcg[rows, :], bank[wide, 0:PAD])
            part += nt(pg[rows, :], w[pl.ds(2 * d, 2)].reshape(W, 3 * W))
            if slot:
                sbuf[slot, rows, :] = part.astype(BF)
            else:
                own[rows, :] = part
        ring.ready(slot)
    for n in range(1, 16):
        for copy in row_arrivals(n):
            copy.wait_recv()
    ring.middle()

    def summed(s, shape, read):
        return lax.fori_loop(
            0, 16, lambda q, acc: acc + picked[s, q] * read(q).astype(F32), jnp.zeros(shape, F32)
        )

    @pl.loop(0, SETS)
    def _(s):
        at = span(s * RANK, RANK)
        total = summed(s, (GROUPS * RANK, T), lambda q: tallbuf[q])
        for g in range(GROUPS):
            tallsum[g, at, :] = total[RANK * g : RANK * g + RANK, :]

    mine[...] = tallsum[6:9].astype(BF)
    theirs[c] = mine[...]
    for k in ORDER:
        to_peer(mine, theirs.at[c], send6.at[k], recv6.at[k], peer_of(k)).start()
    ring.other_plane()

    @pl.loop(0, SETS)
    def _(s):
        at = span(s * RANK, RANK)
        total = summed(s, (6 * RANK, W), lambda q: thinbuf[q])
        for g in range(6):
            thinsum[g, at, :] = total[RANK * g : RANK * g + RANK, :]

    for g in range(4):
        gin[g] = jnp.transpose(tallsum[g])
    for g in range(2):
        glif[g] = tallsum[4 + g]
    grout[...] = jnp.transpose(tallsum[9])
    for k in range(3):
        gqkvup_all[k] = thinsum[k]
    for m in range(2):
        gout[PAD * m : PAD * m + PAD, :] = jnp.transpose(thinsum[3, :, PAD * m : PAD * m + PAD])
    goutup_all[...] = thinsum[4]
    grup_all[...] = thinsum[5, :, 0:PAD]
    for k in ORDER:
        to_peer(mine, theirs.at[source_of(k)], send6.at[k], recv6.at[k], peer_of(k)).wait()
    for k in range(3):
        total = theirs[0, k].astype(F32)
        for p in range(1, PEERS):
            total += theirs[p, k].astype(F32)
        gqkvdown[k] = jnp.transpose(total)
    for n in range(1, 16):
        for copy in row_copies(n):
            copy.wait_send()
    dots = swap_finish(stat3, inbox, send3, recv3)
    ring.end()
    ring.sent()
    for i in range(4):
        rows = slice(256 * i, 256 * i + 256)
        column = rows_to_columns(dots[:, rows])[:, 0:1]
        total = own[rows, :] + ring.arrived(i // 2, slice(256 * (i % 2), 256 * (i % 2) + 256))
        q = rinv[rows, 0:1]
        grad = bgc[rows, :].astype(F32) + q * (total * gain[...])
        out[rows, :] = grad - tokens[rows, :].astype(F32) * (q * q * column / D)


def to_input(*args):
    sems = pltpu.SemaphoreType.DMA((PEERS,))
    more = pltpu.SemaphoreType.DMA((16,))
    kinds = [VMEM] * len(args)
    kinds[2] = ANY
    kinds[9] = pl.BlockSpec(memory_space=pltpu.SMEM)
    square = (PAD, PAD)
    return pl.pallas_call(
        input_kernel,
        out_shape=tuple(
            jax.ShapeDtypeStruct(shape, F32)
            for shape in (
                (S, W), (4, *square), (2, *square), square, (3, *square), (3, PAD, W), (W, PAD),
                (PAD, W), square,
            )
        ),
        in_specs=kinds,
        out_specs=(VMEM,) * 9,
        scratch_shapes=[
            pltpu.VMEM((16, T, 3 * W), BF),
            pltpu.SemaphoreType.DMA((3,)),
            pltpu.VMEM((S, W), F32),
            pltpu.VMEM((PEERS, S, W), BF),
            pltpu.VMEM((2, 2, S // 2, W), BF),
            pltpu.VMEM((2, 2, 2, S // 2, W), BF),
            pltpu.VMEM((2, S // 2, W), BF),
            pltpu.VMEM((PEERS, 8, S), F32),
            pltpu.VMEM((16, GROUPS * RANK, T), BF),
            pltpu.VMEM((6 * RANK, W), BF),
            pltpu.VMEM((16, GROUPS * RANK, T), BF),
            pltpu.VMEM((16, 6 * RANK, W), BF),
            pltpu.VMEM((GROUPS, *square), F32),
            pltpu.VMEM((6, PAD, W), F32),
            pltpu.VMEM((3, *square), BF),
            pltpu.VMEM((PEERS, 3, *square), BF),
            more, more, sems, sems, more, more, more, more, sems, sems,
        ],
        compiler_params=params(5, 63),
        cost_estimate=pl.CostEstimate(flops=5 * 10**10, bytes_accessed=10**7, transcendentals=0),
        name="input",
    )(*args)


def sums_kernel(sets, flat, ginup, glower, low):
    ginup[...] = jnp.zeros_like(ginup)
    low[...] = jnp.zeros_like(low)

    @pl.loop(0, 16)
    def _(q):
        at = span(sets[q] * RANK, RANK)
        for g in range(4):
            ginup[g, at, :] += flat[q, RANK * g : RANK * g + RANK, :].astype(F32)
        for g in range(2):
            low[g, at, :] += flat[q, RANK * (4 + g) : RANK * (5 + g), :].astype(F32)

    for g in range(2):
        for m in range(FF // PAD):
            glower[g, PAD * m : PAD * m + PAD, :] = jnp.transpose(low[g, :, PAD * m : PAD * m + PAD])


def sums(sets, flat):
    return pl.pallas_call(
        sums_kernel,
        out_shape=(
            jax.ShapeDtypeStruct((4, PAD, FF), F32), jax.ShapeDtypeStruct((2, FF, PAD), F32),
        ),
        in_specs=[pl.BlockSpec(memory_space=pltpu.SMEM), VMEM],
        out_specs=(VMEM, VMEM),
        scratch_shapes=[pltpu.VMEM((2, PAD, FF), F32)],
        compiler_params=params(None, 63),
        cost_estimate=pl.CostEstimate(flops=10**9, bytes_accessed=10**7, transcendentals=0),
        name="sums",
    )(sets, flat)


def rope_tables():
    half = HEAD // 2
    frequency = (10000.0 ** (-(np.arange(half, dtype=np.float32) * 2.0) / HEAD)).astype(np.float32)
    angle = np.arange(S, dtype=np.float32)[:, None] * frequency[None, :]
    cosine, sine = np.cos(angle), np.sin(angle)
    return (
        np.concatenate([cosine, cosine], axis=1).astype(np.float32),
        np.concatenate([-sine, sine], axis=1).astype(np.float32),
    )


def body(
    tokens, cotangent, routes, adapter_set, attn_gain, mixer_gain, query_gain, key_gain,
    qkv_weight, qkv_down, qkv_up, out_weight, out_down, out_up,
    router_weight, router_down, router_up,
    expert_in, expert_in_down, expert_in_up, expert_out, expert_out_down, expert_out_up,
):
    c = lax.axis_index("col")
    start = adapter_set[0] * RANK

    out_up_pick = lax.dynamic_slice_in_dim(out_up, start, RANK, 0)
    out_down_pick = lax.dynamic_slice_in_dim(out_down, start, RANK, 1)
    pay0 = jnp.concatenate([tokens, out_down_pick.T, out_up_pick], axis=0)

    flag = jnp.broadcast_to(adapter_set.astype(BF)[:, None], (T, PAD))
    shard = jnp.concatenate(
        [
            qkv_weight.reshape(3 * T, W),
            jnp.concatenate([qkv_down[0], qkv_down[1]], axis=1),
            jnp.concatenate([qkv_down[2], router_down], axis=1),
            jnp.concatenate([jnp.pad(router_weight, ((0, 0), (64, 48))), flag], axis=1),
            out_weight.T,
        ],
        axis=0,
    )
    normed, rinv, resid, extra, cot, po, pl0, pr0, xl, xr, xf, xo, wq = gather_tokens(
        pay0, attn_gain[None], cotangent, expert_in, expert_out, shard
    )
    sets = wq[:, 5 * T, PAD].astype(F32)
    picked = (sets[None, :] == jnp.arange(SETS, dtype=F32)[:, None]).astype(F32)
    spot = jnp.arange(PAD, dtype=jnp.int32)
    rank = spot[None, :, None] - start
    picks = (
        (rank >= 0) & (rank < RANK)
        & (rank + RANK * jnp.arange(4, dtype=jnp.int32)[:, None, None] == spot[None, None, :])
    ).astype(BF)

    down = jnp.concatenate(
        [
            jnp.moveaxis(expert_out_up, 2, 0),
            jnp.moveaxis(expert_in_down.reshape(4, T, PAD), 0, 1),
        ],
        axis=1,
    ).reshape(T, 6, SETS, RANK)
    down = jnp.einsum(
        "dnsj,sr->rdnj", down, picked.astype(BF), preferred_element_type=F32
    ).astype(BF).reshape(16, T, 6 * RANK)
    ebank = jnp.concatenate(
        [
            down[:, :, 2 * RANK :], jnp.zeros((16, T, 16), BF), down[:, :, : 2 * RANK],
            jnp.zeros((16, T, 16), BF),
        ],
        axis=2,
    )

    qkv_up_pick = lax.dynamic_slice_in_dim(qkv_up, start, RANK, 1)
    up = jnp.concatenate(
        [jnp.pad(qkv_up_pick[k], ((RANK * k, PAD - RANK * k - RANK), (0, 0))) for k in range(3)],
        axis=1,
    )
    in_up_pick = lax.dynamic_slice_in_dim(expert_in_up, start, RANK, 2).reshape(4, RANK, FF)
    upin = jnp.stack(
        [jnp.pad(in_up_pick[n], ((RANK * n, PAD - RANK * n - RANK), (0, 0))) for n in range(4)]
    )
    lower_pick = lax.dynamic_slice_in_dim(expert_out_down, start, RANK, 2)
    ad = jnp.stack(
        [jnp.pad(lower_pick[e], ((0, 0), (80 + RANK * e, 32 - RANK * e))) for e in range(2)]
    )
    ru = jnp.pad(lax.dynamic_slice_in_dim(router_up, start, RANK, 0), ((48, 64), (64, 48)))
    routes_t = lax.dynamic_slice_in_dim(routes, c * T, T, 0)
    cosine, sine = rope_tables()

    qg, kg = query_gain[None], key_gain[None]
    (
        att_t, att, q, k, v, qraw, kraw, cols, lat, bank, half, other,
        pl1, pr1, pf0, pf1, yl, yr, yf, *swapped,
    ) = attention(
        normed, wq, picks, up, qg, kg, cosine, sine,
        (expert_in, po, pl0, pr0), (expert_out, xo, xl, xr, xf),
    )
    pin = [expert_in, po, pl0, pl1, pr0, pr1, pf0, pf1]
    pout = [expert_out, xo, xl, yl, xr, yr, xf, yf]
    half, other = half.reshape(PEERS, S, W), other.reshape(PEERS, S, W)
    pay, state, prob, branch, lat_o = to_state(
        att_t, half, other, resid, extra, mixer_gain[None], bank, ru, routes_t
    )
    mixture, summed, xfull, gup, glow, glift, gdown = experts(
        pay, branch, cot, ebank, upin, ad, pin, pout, swapped[:4], swapped[4:]
    )
    flat = jnp.concatenate([gup.reshape(4 * RANK, FF), glow.reshape(2 * RANK, FF)], axis=0)

    pg, bgc, stat3, lcg, gqkvup, goutdown, goutup, grup, gtall, flat, mixed = back(
        summed, state, prob, routes_t, bank, ru, mixer_gain[None], cot, half, other, extra,
        lat_o, q, k, v, att, cols, qraw, kraw, qg, kg, cosine, sine, up, lat, xfull, normed,
        flat, mixture, tokens,
    )
    gain_mine = lax.dynamic_slice_in_dim(attn_gain, c * W, W, 0)[None]
    (
        tokens_grad, in_down_grad, lift_grad, router_down_grad, qkv_down_grad, qkv_up_grad,
        out_down_grad, out_up_grad, router_up_grad,
    ) = to_input(
        pg, lcg, wq, bank, stat3, bgc.reshape(S, W), tokens, rinv, gain_mine,
        picked, gdown, glift.reshape(2 * RANK, D), gtall, gqkvup.reshape(3 * RANK, W),
        goutdown, goutup, grup,
    )
    in_up_grad, lower_grad = sums(sets.astype(jnp.int32), flat)
    in_down_grad = in_down_grad.reshape(2, 2, T, PAD)
    in_up_grad = in_up_grad.reshape(2, 2, PAD, FF)
    router_up_grad = router_up_grad[:, 64:80]
    return (
        mixed, tokens_grad, qkv_down_grad, qkv_up_grad, out_down_grad, out_up_grad,
        router_down_grad, router_up_grad, in_down_grad, in_up_grad, lower_grad, lift_grad,
    )


def solution(mesh):
    in_specs = (
        P("row", "col"), P("row", "col"), P("row", None), P("row"), P(), P(), P("col"), P("col"),
        P(None, "row", "col"), P(None, "row", None), P(None, None, "col"),
        P("col", "row"), P("col", None), P(None, "col"),
        P("row", None), P("row", None), P(),
        P("col", None, "row", None), P("col", None, "row", None), P("col", None, None, None),
        P("col", None, "row"), P("col", None, None), P("col", None, "row"),
    )
    out_specs = (
        P("row", "col"), P("row", "col"), P(None, "row", None), P(None, None, "col"),
        P("col", None), P(None, "col"), P("row", None), P(),
        P("col", None, "row", None), P("col", None, None, None), P("col", None, None),
        P("col", None, "row"),
    )
    return jax.shard_map(body, mesh=mesh, in_specs=in_specs, out_specs=out_specs, check_vma=False)
```

```python
import functools

import jax
import jax.numpy as jnp
import numpy as np
from jax import lax
from jax.experimental import pallas as pl
from jax.experimental.pallas import tpu as pltpu
from jax.sharding import PartitionSpec as P

D = 2048
HEAD = 128
FF = 1024
RANK = 16
SETS = 8
S = 1024
W = 256
T = 128
PEERS = 8
PAD = 128
EPS = 1e-05
FACTOR = HEAD ** (-0.5)
F32 = jnp.float32
BF = jnp.bfloat16
MESH = pl.DeviceIdType.MESH
VMEM = pl.BlockSpec(memory_space=pltpu.VMEM)
ANY = pl.BlockSpec(memory_space=pl.ANY)

NN = (((1,), (0,)), ((), ()))
NT = (((1,), (1,)), ((), ()))
TN = (((0,), (0,)), ((), ()))


def nn(a, b):
    return lax.dot_general(a, b, NN, preferred_element_type=F32)


def nt(a, b):
    return lax.dot_general(a, b, NT, preferred_element_type=F32)


def tn(a, b):
    return lax.dot_general(a, b, TN, preferred_element_type=F32)


def lanes(rows):
    return lax.broadcasted_iota(jnp.int32, (rows, PAD), 1)


def span(start, size):
    return pl.ds(pl.multiple_of(start, size), size)


def params(collective=None, limit=62):
    return pltpu.CompilerParams(
        collective_id=collective,
        has_side_effects=collective is not None,
        vmem_limit_bytes=limit * 2**20,
    )


def greet():
    c = lax.axis_index("col")
    barrier = pltpu.get_barrier_semaphore()
    for k in range(1, PEERS):
        pl.semaphore_signal(
            barrier, inc=1, device_id={"col": lax.rem(c + k, PEERS)}, device_id_type=MESH
        )
    return barrier


def to_peer(src, dst, send, recv, peer):
    return pltpu.make_async_remote_copy(
        src_ref=src,
        dst_ref=dst,
        send_sem=send,
        recv_sem=recv,
        device_id={"col": peer},
        device_id_type=MESH,
    )


def peer_of(k):
    return lax.rem(lax.axis_index("col") + k, PEERS)


def source_of(k):
    return lax.rem(lax.axis_index("col") + PEERS - k, PEERS)


ORDER = (4, 1, 7, 5, 3, 2, 6)


PLACES = ((0, 0), (0, 1), (1, 0), (3, 0), (1, 1), (3, 1), (2, 0), (2, 1))
NEAR = ((0, 1), (1, 0), (3, 0))


def place(rel):
    c = lax.axis_index("col")
    return lax.rem(c // 4 + rel[1], 2) * 4 + lax.rem(lax.rem(c, 4) + rel[0], 4)


def greet_near():
    barrier = pltpu.get_barrier_semaphore()
    for rel in NEAR:
        pl.semaphore_signal(barrier, inc=1, device_id={"col": place(rel)}, device_id_type=MESH)
    return barrier


class Gather:
    MOVES = {
        "a0": ((0, 0), (0, 1), 0, (0, 1), 0),
        "a1": ((0, 0), (3, 0), 0, (1, 0), 2),
        "a2": ((0, 0), (1, 0), 0, (3, 0), 1),
        "b1": ((0, 1), (3, 1), 0, (1, 0), 4),
        "b2": ((0, 1), (1, 1), 0, (3, 0), 3),
        "c1": ((3, 0), (2, 0), 1, (1, 0), 5),
        "c2": ((1, 0), (2, 0), 2, (3, 0), 6),
        "d1": ((3, 1), (2, 1), 1, (1, 0), 7),
        "d2": ((1, 1), (2, 1), 2, (3, 0), 8),
    }
    FROM = (
        ((0, 1), 0), ((1, 0), 0), ((3, 0), 0), ((1, 1), 0), ((3, 1), 0),
        ((2, 0), 1), ((2, 0), 2), ((2, 1), 1), ((2, 1), 2),
    )

    def __init__(self, here, there, rows, send, recv, axis="col"):
        self.here, self.there, self.rows, self.send, self.recv = here, there, rows, send, recv
        self.axis = axis

    def copy(self, src, dst, send, recv, to):
        to = place(to) if self.axis == "col" else row_place((to[1], to[0]))
        return pltpu.make_async_remote_copy(
            src_ref=src, dst_ref=dst, send_sem=send, recv_sem=recv,
            device_id={self.axis: to}, device_id_type=MESH,
        )

    def part(self, which):
        half = self.rows // 2
        return ((0, self.rows), (0, half), (half, half))[which]

    def move(self, name):
        src, dst, which, to, arrives = self.MOVES[name]
        lo, n = self.part(which)
        return self.copy(
            self.here(src, lo, n), self.there(src, dst, lo, n),
            self.send.at[list(self.MOVES).index(name)], self.recv.at[arrives], to,
        )

    def start(self, *names):
        for name in names:
            self.move(name).start()

    def wait(self, *arrivals):
        for i in arrivals:
            rel, which = self.FROM[i]
            lo, n = self.part(which)
            ref = self.here(rel, lo, n)
            self.copy(ref, ref, self.send.at[0], self.recv.at[i], (0, 1)).wait_recv()

    def sent(self):
        for name in self.MOVES:
            self.move(name).wait_send()


def row_place(shift):
    r = lax.axis_index("row")
    plane = lax.rem(r // 8 + shift[0], 2)
    spot = lax.rem(lax.rem(r, 8) // 2 + shift[1], 4)
    return plane * 8 + spot * 2 + lax.rem(r, 2)


PLANE, UP, DOWN, FAR = (1, 0), (0, 1), (0, 3), (0, 2)


def greet_row(barrier, *shifts):
    for shift in shifts:
        pl.semaphore_signal(
            barrier, inc=1, device_id={"row": row_place(shift)}, device_id_type=MESH
        )


def along(src, dst, send, recv, shift):
    return pltpu.make_async_remote_copy(
        src_ref=src, dst_ref=dst, send_sem=send, recv_sem=recv,
        device_id={"row": row_place(shift)}, device_id_type=MESH,
    )


class RowGather:
    def __init__(self, shard, out, rows, sems):
        self.send, self.recv, self.xsend, self.xrecv, self.sem = sems
        self.shard, self.out, self.rows = shard, out, rows
        self.ring = Gather(
            self.part, lambda src, dst, lo, n: out.at[self.at(src), lo : lo + n],
            rows, self.send, self.recv, "row",
        )
        self.keep = pltpu.make_async_copy(shard, out.at[lax.axis_index("row")], self.sem)

    def at(self, rel):
        return row_place((rel[1], rel[0]))

    def part(self, rel, lo, n):
        if rel == (0, 0):
            return self.shard.at[lo : lo + n]
        return self.out.at[self.at(rel), lo : lo + n]

    def across(self, rel):
        r = lax.axis_index("row")
        n = PLACES.index(rel)
        return pltpu.make_async_remote_copy(
            src_ref=self.part(rel, 0, self.rows), dst_ref=self.out.at[self.at(rel)],
            send_sem=self.xsend.at[n], recv_sem=self.xrecv.at[n],
            device_id={"row": r + 1 - 2 * lax.rem(r, 2)}, device_id_type=MESH,
        )

    def start(self):
        self.ring.start("a0", "a1", "a2")
        self.keep.start()
        self.across((0, 0)).start()

    def step(self, i):
        waits, sends = (
            ((0,), ("b1", "b2")), ((1, 2), ("c1", "c2")), ((3, 4), ("d1", "d2")), ((5, 6, 7, 8), ())
        )[i]
        places = (((0, 1),), ((1, 0), (3, 0)), ((1, 1), (3, 1)), ((2, 0), (2, 1)))[i]
        self.ring.wait(*waits)
        self.ring.start(*sends)
        for rel in places:
            self.across(rel).start()

    def finish(self):
        self.ring.sent()
        self.keep.wait()
        r = lax.axis_index("row")
        for rel in PLACES:
            self.across(rel).wait_send()
        for rel in PLACES:
            n = PLACES.index(rel)
            q = self.at(rel) + 1 - 2 * lax.rem(r, 2)
            pltpu.make_async_remote_copy(
                src_ref=self.part(rel, 0, self.rows), dst_ref=self.out.at[q],
                send_sem=self.xsend.at[n], recv_sem=self.xrecv.at[n],
                device_id={"row": r + 1 - 2 * lax.rem(r, 2)}, device_id_type=MESH,
            ).wait_recv()


def row_sems():
    sems = pltpu.SemaphoreType.DMA
    return [sems((9,)), sems((9,)), sems((PEERS,)), sems((PEERS,)), sems]


def greet_partner(barrier):
    r = lax.axis_index("row")
    pl.semaphore_signal(
        barrier, inc=1, device_id={"row": r + 1 - 2 * lax.rem(r, 2)}, device_id_type=MESH
    )


def tokens_kernel(
    pay, gain, cot, win, wout, shard,
    normed, rinv, resid, extra, cots, wo, wl, wr, ql, qr, qf, qo, wq,
    buf, send, recv, send2, recv2, sem, send3, recv3, *sems,
):
    c = lax.axis_index("col")
    barrier = greet_near()
    greet_row(barrier, PLANE, UP, DOWN, FAR)
    greet_partner(barrier)
    rows_in = RowGather(shard, wq, shard.shape[0], sems)
    weights = [
        along(src, dst, send3.at[n], recv3.at[n], shift)
        for n, (src, dst, shift) in enumerate(
            (
                (win, wo, PLANE), (wout, qo, PLANE), (win, wl, UP), (win, wr, DOWN),
                (wout, ql, UP), (wout, qr, DOWN), (wout, qf, FAR),
            )
        )
    ]
    keep = pltpu.make_async_copy(cot, cots.at[c], sem)
    keep.start()
    buf[c] = pay[...]
    pl.semaphore_wait(barrier, 8)
    ring = Gather(
        lambda rel, lo, n: buf.at[place(rel), lo : lo + n],
        lambda src, dst, lo, n: buf.at[place(src), lo : lo + n],
        pay.shape[0], send, recv,
    )

    def cot_part(rel, lo, n):
        if rel == (0, 0):
            return cot.at[lo : lo + n]
        return cots.at[place(rel), lo : lo + n]

    second = Gather(
        cot_part, lambda src, dst, lo, n: cots.at[place(src), lo : lo + n], S, send2, recv2
    )
    ring.start("a0", "a1", "a2")
    rows_in.start()
    ring.wait(0)
    ring.start("b1", "b2")
    rows_in.step(0)
    ring.wait(1, 2)
    ring.start("c1", "c2")
    rows_in.step(1)
    for copy in weights:
        copy.start()
    ring.wait(3, 4)
    ring.start("d1", "d2")
    second.start("a0", "a1", "a2")
    rows_in.step(2)
    ring.wait(5, 6, 7, 8)
    extra[...] = jnp.zeros_like(extra)
    for p in range(PEERS):
        resid[p] = buf[p, span(c * T, T), :]
        extra[p, 0 : 2 * RANK, :] = buf[p, S : S + 2 * RANK, :]

    @pl.loop(0, S // 64)
    def _(i):
        rows = span(i * 64, 64)
        total = jnp.zeros((64, 1), F32)
        for p in range(PEERS):
            x = buf[p, rows, :].astype(F32)
            total += jnp.sum(x * x, axis=1, keepdims=True)
        r = lax.rsqrt(total / D + EPS)
        for p in range(PEERS):
            x = buf[p, rows, :].astype(F32)
            normed[rows, W * p : W * p + W] = (x * r * gain[:, W * p : W * p + W]).astype(BF)
        rinv[rows, :] = jnp.broadcast_to(r, (64, PAD))

    second.wait(0)
    second.start("b1", "b2")
    second.wait(1, 2)
    second.start("c1", "c2")
    second.wait(3, 4)
    second.start("d1", "d2")
    rows_in.step(3)
    second.wait(5, 6, 7, 8)
    ring.sent()
    second.sent()
    keep.wait()
    rows_in.finish()
    for copy in weights:
        copy.wait()


def gather_tokens(pay, gain, cot, win, wout, shard):
    rows = pay.shape[0]
    return pl.pallas_call(
        tokens_kernel,
        out_shape=(
            jax.ShapeDtypeStruct((S, D), BF),
            jax.ShapeDtypeStruct((S, PAD), F32),
            jax.ShapeDtypeStruct((PEERS, T, W), BF),
            jax.ShapeDtypeStruct((PEERS, PAD, W), BF),
            jax.ShapeDtypeStruct((PEERS, S, W), BF),
        )
        + (jax.ShapeDtypeStruct(win.shape, BF),) * 3
        + (jax.ShapeDtypeStruct(wout.shape, BF),) * 4
        + (jax.ShapeDtypeStruct((16, *shard.shape), BF),),
        in_specs=[VMEM, VMEM, ANY, ANY, ANY, ANY],
        out_specs=(VMEM, VMEM, VMEM, VMEM) + (ANY,) * 9,
        scratch_shapes=[
            pltpu.VMEM((PEERS, rows, W), BF),
            pltpu.SemaphoreType.DMA((9,)),
            pltpu.SemaphoreType.DMA((9,)),
            pltpu.SemaphoreType.DMA((9,)),
            pltpu.SemaphoreType.DMA((9,)),
            pltpu.SemaphoreType.DMA,
            pltpu.SemaphoreType.DMA((7,)),
            pltpu.SemaphoreType.DMA((7,)),
            *row_sems(),
        ],
        compiler_params=params(1, 63),
        cost_estimate=pl.CostEstimate(flops=5 * 10**10, bytes_accessed=10**7, transcendentals=0),
        name="tokens",
    )(pay, gain, cot, win, wout, shard)


def columns_to_rows(first, second):
    lane = lanes(first.shape[0])
    tile = jnp.where(lane == 0, first, jnp.where(lane == 1, second, 0.0))
    return jnp.transpose(tile)[0:8, :]


def rows_to_columns(rows):
    padded = jnp.concatenate([rows, jnp.zeros((PAD - 8, rows.shape[1]), F32)], axis=0)
    return jnp.transpose(padded)


def swap_start(stat, inbox, send, recv):
    c = lax.axis_index("col")
    for k in ORDER:
        to_peer(stat, inbox.at[c], send.at[k], recv.at[k], peer_of(k)).start()


def swap_finish(stat, inbox, send, recv):
    for k in ORDER:
        to_peer(stat, inbox.at[source_of(k)], send.at[k], recv.at[k], peer_of(k)).wait()
    total = stat[...]
    for k in range(1, PEERS):
        total += inbox[source_of(k)]
    return total


def attention_kernel(
    normed_in, wq, picks, up, qgain, kgain, cosine, sine,
    p0, po, pl0, pr0, x0, xo, xl, xr, xf,
    att_t, att, qo, ko, vo, qraw, kraw, cols, lat, bank, wmine, wother,
    pl1, pr1, pf0, pf1, yl, yr, yf, *rest,
):
    swapped, rest = rest[0:9], rest[9:]
    (
        w, wsem, stat, inbox, ssem, rsem, asend, arecv, osend, orecv, xsend, xrecv, psend, precv,
        normed, nsem, esend, erecv,
    ) = rest
    c = lax.axis_index("col")
    side = lax.rem(lax.axis_index("row"), 2)
    partner = lax.axis_index("row") + 1 - 2 * side
    barrier = greet()
    pl.semaphore_signal(barrier, inc=1, device_id={"row": partner}, device_id_type=MESH)
    greet_row(barrier, PLANE, UP, DOWN)
    first, last = pl.ds(0, 1), pl.ds(1, 1)
    weights = [
        along(src, dst, psend.at[n], precv.at[n], shift)
        for n, (src, dst, shift) in enumerate(
            (
                (po, pl1, UP), (po, pr1, DOWN),
                (pl0.at[first], pf0.at[first], UP), (pr0.at[last], pf0.at[last], DOWN),
                (xl, yl, PLANE), (xr, yr, PLANE), (xf, yf, PLANE),
                (pl1.at[first], pf1.at[first], UP), (pr1.at[last], pf1.at[last], DOWN),
            )
        )
    ]

    early = [
        pltpu.make_async_remote_copy(
            src_ref=src, dst_ref=dst, send_sem=esend.at[n], recv_sem=erecv.at[n],
            device_id={"row": partner}, device_id_type=MESH,
        )
        for n, (src, dst) in enumerate(zip((p0, po, pl0, pr0, x0, xo, xl, xr, xf), swapped))
    ]
    fetch = pltpu.make_async_copy(normed_in, normed, nsem)
    fetch.start()

    def out_part(rel, lo, n):
        if rel == (0, 0):
            return wq.at[pl.ds(8 * side + lo, n), 6 * T : 7 * T, :]
        return wmine.at[place(rel), lo : lo + n]

    ring = Gather(
        out_part, lambda src, dst, lo, n: wmine.at[place(src), lo : lo + n], 8, osend, orecv
    )

    def across(rel):
        n = PLACES.index(rel)
        return pltpu.make_async_remote_copy(
            src_ref=out_part(rel, 0, 8), dst_ref=wother.at[place(rel)],
            send_sem=xsend.at[n], recv_sem=xrecv.at[n],
            device_id={"row": partner}, device_id_type=MESH,
        )

    keep = pltpu.make_async_copy(out_part((0, 0), 0, 8), wmine.at[c], wsem.at[6])
    keep.start()
    loads = [
        pltpu.make_async_copy(
            wq.at[:, T * k : T * k + T, :], w.at[:, :, W * k : W * k + W], wsem.at[k]
        )
        for k in range(6)
    ]
    for load in loads:
        load.start()
    pl.semaphore_wait(barrier, PEERS + 3)
    ring.start("a0", "a1", "a2")
    for copy in weights[:4]:
        copy.start()
    for copy in early:
        copy.start()
    across((0, 0)).start()
    for load in loads:
        load.wait()
    fetch.wait()

    for i in range(4):
        tile = w[4 * i : 4 * i + 4, :, 3 * W :].reshape(4 * T, 3 * W)
        chosen = tile[:, 2 * W : 2 * W + PAD].astype(F32)
        for n in range(4):
            chosen += nn(tile[:, PAD * n : PAD * n + PAD], picks[n])
        bank[4 * T * i : 4 * T * i + 4 * T, :] = chosen.astype(BF)

    blocks = 4
    rows_of = S // blocks
    lane = lanes(rows_of)
    for i in range(blocks):
        rows = slice(i * rows_of, (i + 1) * rows_of)
        x = normed[rows, :]
        code = jnp.where(lane < 3 * RANK, nn(x, bank[...]), 0.0).astype(BF)
        lat[rows, :] = code
        parts = nn(x, w[:, :, 0 : 3 * W].reshape(D, 3 * W)) + nn(code, up[...])
        first_part, second_part = parts[:, 0:W], parts[:, W : 2 * W]
        qraw[rows, :] = first_part
        kraw[rows, :] = second_part
        vo[rows, :] = parts[:, 2 * W :].astype(BF)
        stat[:, rows] = columns_to_rows(
            jnp.sum(first_part * first_part, axis=1, keepdims=True),
            jnp.sum(second_part * second_part, axis=1, keepdims=True),
        )
    swap_start(stat, inbox, ssem, rsem)
    ring.wait(0)
    ring.start("b1", "b2")
    for copy in weights[4:7]:
        copy.start()
    ring.wait(1, 2)
    ring.start("c1", "c2")
    for rel in NEAR:
        across(rel).start()
    total = swap_finish(stat, inbox, ssem, rsem)
    scale = lax.rsqrt(total / D + EPS)
    for i in range(blocks):
        rows = slice(i * rows_of, (i + 1) * rows_of)
        column = rows_to_columns(scale[:, rows])
        cols[rows, :] = column
        for index, (raw, gain, out) in enumerate(((qraw, qgain, qo), (kraw, kgain, ko))):
            for h in range(2):
                feats = slice(HEAD * h, HEAD * h + HEAD)
                x = raw[rows, feats] * column[:, index : index + 1] * gain[:, feats]
                y = x * cosine[rows, :] + pltpu.roll(x, HEAD // 2, 1) * sine[rows, :]
                out[rows, feats] = y.astype(BF)
    for i in range(blocks):
        rows = slice(i * rows_of, (i + 1) * rows_of)
        seen = (i + 1) * rows_of
        allowed = lax.broadcasted_iota(jnp.int32, (rows_of, seen), 1) <= (
            lax.broadcasted_iota(jnp.int32, (rows_of, seen), 0) + i * rows_of
        )
        logs = []
        for h in range(2):
            feats = slice(HEAD * h, HEAD * h + HEAD)
            score = nt(qo[rows, feats], ko[0:seen, feats]) * FACTOR
            score = jnp.where(allowed, score, -1e30)
            top = jnp.max(score, axis=1, keepdims=True)
            weight = jnp.exp(score - top)
            norm = jnp.sum(weight, axis=1, keepdims=True)
            attend = (weight * (1.0 / norm)).astype(BF)
            att[rows, feats] = nn(attend, vo[0:seen, feats]).astype(BF)
            logs.append(top + jnp.log(norm))
        cols[rows, :] = jnp.where(
            lane == 2, logs[0], jnp.where(lane == 3, logs[1], cols[rows, :])
        )
        for p in (2 * i, 2 * i + 1):
            mine = slice(T * p, T * p + T)

            @pl.when(c != p)
            def _():
                to_peer(att.at[mine], att_t.at[c], asend.at[p], arecv.at[c], p).start()

            @pl.when(c == p)
            def _():
                att_t[p] = att[mine, :]

    ring.wait(3, 4)
    ring.start("d1", "d2")
    across((1, 1)).start()
    across((3, 1)).start()
    weights[0].wait_recv()
    weights[1].wait_recv()
    weights[7].start()
    weights[8].start()
    ring.wait(5, 6, 7, 8)
    across((2, 0)).start()
    across((2, 1)).start()
    for p in range(PEERS):

        @pl.when(c != p)
        def _():
            to_peer(
                att.at[T * p : T * p + T], att_t.at[p], asend.at[p], arecv.at[p], p
            ).wait()

    ring.sent()
    keep.wait()
    for rel in PLACES:
        across(rel).wait()
    weights[0].wait_send()
    weights[1].wait_send()
    for copy in weights[2:]:
        copy.wait()
    for copy in early:
        copy.wait()


def attention(normed, wq, picks, up, qgain, kgain, cosine, sine, inner, outer):
    full = jax.ShapeDtypeStruct((S, W), BF)
    wide = jax.ShapeDtypeStruct((S, W), F32)
    return pl.pallas_call(
        attention_kernel,
        out_shape=(
            jax.ShapeDtypeStruct((PEERS, T, W), BF),
            full, full, full, full, wide, wide,
            jax.ShapeDtypeStruct((S, PAD), F32),
            jax.ShapeDtypeStruct((S, PAD), BF),
            jax.ShapeDtypeStruct((D, PAD), BF),
            jax.ShapeDtypeStruct((PEERS, 8, T, W), BF),
            jax.ShapeDtypeStruct((PEERS, 8, T, W), BF),
        )
        + (jax.ShapeDtypeStruct(inner[0].shape, BF),) * 4
        + (jax.ShapeDtypeStruct(outer[0].shape, BF),) * 3
        + (jax.ShapeDtypeStruct(inner[0].shape, BF),) * 4
        + (jax.ShapeDtypeStruct(outer[0].shape, BF),) * 5,
        in_specs=[ANY, ANY, VMEM, VMEM, VMEM, VMEM, VMEM, VMEM] + [ANY] * 9,
        out_specs=(VMEM,) * 10 + (ANY,) * 18,
        scratch_shapes=[
            pltpu.VMEM((16, T, 6 * W), BF),
            pltpu.SemaphoreType.DMA((7,)),
            pltpu.VMEM((8, S), F32),
            pltpu.VMEM((PEERS, 8, S), F32),
            pltpu.SemaphoreType.DMA((PEERS,)),
            pltpu.SemaphoreType.DMA((PEERS,)),
            pltpu.SemaphoreType.DMA((PEERS,)),
            pltpu.SemaphoreType.DMA((PEERS,)),
            pltpu.SemaphoreType.DMA((9,)),
            pltpu.SemaphoreType.DMA((9,)),
            pltpu.SemaphoreType.DMA((PEERS,)),
            pltpu.SemaphoreType.DMA((PEERS,)),
            pltpu.SemaphoreType.DMA((9,)),
            pltpu.SemaphoreType.DMA((9,)),
            pltpu.VMEM((S, D), BF),
            pltpu.SemaphoreType.DMA,
            pltpu.SemaphoreType.DMA((9,)),
            pltpu.SemaphoreType.DMA((9,)),
        ],
        compiler_params=params(2, 63),
        cost_estimate=pl.CostEstimate(flops=3 * 10**10, bytes_accessed=10**7, transcendentals=0),
        name="attention",
    )(normed, wq, picks, up, qgain, kgain, cosine, sine, *inner, *outer)


def load_out(mine, other, wo, sem):
    half = lax.rem(lax.axis_index("row"), 2)
    copies = []
    for index, (src, side) in enumerate(((mine, half), (other, 1 - half))):
        for p in range(PEERS):
            copies.append(
                pltpu.make_async_copy(
                    src.at[p],
                    wo.at[span(side * (D // 2), D // 2), W * p : W * p + W],
                    sem.at[index * PEERS + p],
                )
            )
    return copies


def member_of(routes, rows):
    lane = lanes(rows)
    found = lane == routes[:, 0:1] + 64
    for j in range(1, 8):
        found = found | (lane == routes[:, j : j + 1] + 64)
    return found


def state_kernel(
    att_t, mine, other, resid, extra, gain, bank, ru, routes,
    pay, state, prob_out, branch, lat_out,
    wo, sem,
):
    loads = load_out(mine, other, wo, sem)
    for load in loads:
        load.start()
    lane = lanes(T)
    lat = jnp.zeros((T, PAD), F32)
    for p in range(PEERS):
        lat += nt(att_t[p], extra[p])
    lat = jnp.where(lane < RANK, lat, 0.0)
    lat_out[...] = lat
    moved = pltpu.roll(lat, RANK, 1).astype(BF)
    x = jnp.concatenate([att_t[p] for p in range(PEERS)], axis=1)
    for load in loads:
        load.wait()
    total = jnp.zeros((T, 1), F32)
    for p in range(PEERS):
        feats = slice(W * p, W * p + W)
        part = nt(x, wo[feats, :]) + nn(moved, extra[p])
        branch[:, feats] = part.astype(BF)
        st = resid[p].astype(F32) + part
        state[:, feats] = st
        total += jnp.sum(st * st, axis=1, keepdims=True)
    r = lax.rsqrt(total / D + EPS)
    first = jnp.zeros((T, PAD), F32)
    for p in range(PEERS):
        feats = slice(W * p, W * p + W)
        m = (state[:, feats] * r * gain[:, feats]).astype(BF)
        pay[:, feats] = m
        first += nn(m, bank[feats, 0:PAD])
    code = jnp.where((lane >= 48) & (lane < 64), first, 0.0).astype(BF)
    valid = (lane >= 64) & (lane < 80)
    logits = jnp.where(valid, first + nn(code, ru[...]), -1e30)
    shifted = jnp.where(valid, jnp.exp(logits - jnp.max(logits, axis=1, keepdims=True)), 0.0)
    prob = shifted / jnp.sum(shifted, axis=1, keepdims=True)
    prob_out[...] = prob
    gate = jnp.where(member_of(routes, T), prob, 0.0)
    high = gate.astype(BF).astype(F32)
    low = pltpu.roll(gate - high, RANK, 1)
    pay[:, D:] = jnp.where(lane < 64, code.astype(F32), jnp.where(lane < 80, high, low)).astype(BF)


def to_state(att_t, mine, other, resid, extra, gain, bank, ru, routes):
    return pl.pallas_call(
        state_kernel,
        out_shape=(
            jax.ShapeDtypeStruct((T, D + PAD), BF),
            jax.ShapeDtypeStruct((T, D), F32),
            jax.ShapeDtypeStruct((T, PAD), F32),
            jax.ShapeDtypeStruct((T, D), BF),
            jax.ShapeDtypeStruct((T, PAD), F32),
        ),
        in_specs=[VMEM, ANY, ANY, VMEM, VMEM, VMEM, VMEM, VMEM, VMEM],
        out_specs=(VMEM,) * 5,
        scratch_shapes=[pltpu.VMEM((D, D), BF), pltpu.SemaphoreType.DMA((2 * PEERS,))],
        compiler_params=params(None, 63),
        cost_estimate=pl.CostEstimate(flops=10**10, bytes_accessed=10**7, transcendentals=0),
        name="state",
    )(att_t, mine, other, resid, extra, gain, bank, ru, routes)


EARLY_IN, LATE_IN = (0, 1, 2, 4), (3, 5, 6, 7)
EARLY_OUT, LATE_OUT = (0, 1, 2, 4, 6), (3, 5, 7)
SHIFTS = ((0, 0), (1, 0), (0, 3), (1, 3), (0, 1), (1, 1), (0, 2), (1, 2))
CHUNK = 256
TILE = 512
STEPS = (1, 2, 3)
LAST = 0


def expert_kernel(*refs):
    pay, branch, cot, ebank, upin, ad = refs[0:6]
    pin, pout, ein, eout = refs[6:14], refs[14:22], refs[22:26], refs[26:31]
    refs = refs[9:]
    mixed, summed, xout, gup, glow, glift, gdown = refs[22:29]
    (xfull, win, wd, cbuf, obuf, rbuf, a1, act, hid, vg, gg, ug, mix, xacc,
     aup, alow, alift, adown,
     lsem, csend, crecv, csem, send1, recv1, send2, recv2, xsem, mbank, bsend, brecv, esem) = refs[29:]
    c = lax.axis_index("col")
    r = lax.axis_index("row")
    half = lax.rem(r, 2)
    partner = r + 1 - 2 * half
    barrier = greet()

    def offset(shift, side):
        plane = lax.rem(r // 8 + shift[0], 2)
        place = lax.rem(lax.rem(r, 8) // 2 + shift[1], 4)
        return (plane * 8 + place * 2 + side) * T

    def inner(i, src, side):
        return (src, win.at[:, :, span(offset(SHIFTS[i], side), T), :], 2 * i)

    def outer(i, src, side):
        return (src, wd.at[:, :, span(offset(SHIFTS[i], side), T)], 2 * i + 1)

    def across(side, kind):
        late = [inner(i, pin[i], side) for i in LATE_IN] if kind == 0 else [
            outer(i, pout[i], side) for i in LATE_OUT
        ]
        return [
            pltpu.make_async_remote_copy(
                src_ref=src, dst_ref=dst, send_sem=csend.at[n], recv_sem=crecv.at[n],
                device_id={"row": partner}, device_id_type=MESH,
            )
            for src, dst, n in late
        ]

    def local(kind):
        made, pieces, early, others = (
            (inner, pin, EARLY_IN, ein), (outer, pout, EARLY_OUT, eout)
        )[kind]
        every = [made(i, pieces[i], half) for i in range(8)]
        copies = [pltpu.make_async_copy(src, dst, lsem.at[n]) for src, dst, n in every]
        every = [made(i, src, 1 - half) for i, src in zip(early, others)]
        copies += [pltpu.make_async_copy(src, dst, esem.at[n]) for src, dst, n in every]
        return copies

    sources = [place(rel) for rel in PLACES]

    def source(step, t):
        chosen = sources[2 * LAST + t]
        for j in range(3):
            chosen = jnp.where(step == j, sources[2 * STEPS[j] + t], chosen)
        return chosen

    def cot_copies(step, slot):
        return [
            pltpu.make_async_copy(
                cot.at[:, span(source(step, t) * T, T), :],
                cbuf.at[slot, :, T * t : T * t + T, :],
                csem.at[2 * slot + t],
            )
            for t in range(2)
        ]

    ring = Gather(
        lambda rel, lo, n: xfull.at[pl.ds(T * PLACES.index(rel) + lo, n)],
        lambda src, dst, lo, n: xfull.at[pl.ds(T * PLACES.index(dst) + lo, n)],
        T, send1, recv1,
    )
    for n in range(1, 16):
        pl.semaphore_signal(
            barrier, inc=1, device_id={"row": lax.rem(r + n, 16)}, device_id_type=MESH
        )

    def bank_copy(n):
        q = lax.rem(r + n, 16)
        return pltpu.make_async_remote_copy(
            src_ref=ebank.at[q], dst_ref=mbank.at[r], send_sem=bsend.at[n], recv_sem=brecv.at[n],
            device_id={"row": q}, device_id_type=MESH,
        )

    def bank_arrival(n):
        q = lax.rem(r + 16 - n, 16)
        return pltpu.make_async_remote_copy(
            src_ref=ebank.at[q], dst_ref=mbank.at[q], send_sem=bsend.at[n], recv_sem=brecv.at[n],
            device_id={"row": q}, device_id_type=MESH,
        )

    def bank(at):
        return mbank[at // T : (at + TILE) // T].reshape(TILE, PAD)

    def whole_bank():
        return mbank[...].reshape(D, PAD)

    xfull[0:T, :] = pay[...]
    mbank[r] = ebank[r]
    pl.semaphore_wait(barrier, PEERS + 14)
    ring.start("a0", "a1", "a2")
    for n in range(1, 16):
        bank_copy(n).start()
    for kind in range(2):
        for copy in across(half, kind):
            copy.start()
        for copy in local(kind):
            copy.start()
    for copy in cot_copies(0, 0):
        copy.start()
    aup[...] = jnp.zeros_like(aup)
    alow[...] = jnp.zeros_like(alow)
    alift[...] = jnp.zeros_like(alift)
    adown[...] = jnp.zeros_like(adown)
    lane = lanes(CHUNK)
    ring.wait(0)
    ring.start("b1", "b2")
    ring.wait(1, 2)
    ring.start("c1", "c2")
    for n in range(1, 16):
        bank_arrival(n).wait_recv()
    for n in range(1, 16):
        bank_copy(n).wait_send()
    def weights_here(kind):
        for copy in local(kind):
            copy.wait()
        for copy in across(half, kind):
            copy.wait_send()
        for copy in across(1 - half, kind):
            copy.wait_recv()

    weights_here(0)

    def chunk(j, carry):
        rows = span(lax.rem(j + STEPS[0], 4) * CHUNK, CHUNK)
        slot = lax.rem(j, 2)

        @pl.when(j == 1)
        def _():
            ring.wait(3, 4)
            ring.start("d1", "d2")

        @pl.when(j == 2)
        def _():
            ring.wait(5, 6, 7, 8)

        for copy in cot_copies(j, slot):
            copy.wait()

        @pl.when(j < 3)
        def _():
            for copy in cot_copies(j + 1, 1 - slot):
                copy.start()

        mix[...] = jnp.zeros_like(mix)

        @pl.when(j == 3)
        def _():
            mix[0:T, :] = branch[...].astype(F32)

        extras = xfull[rows, D : D + PAD].astype(F32)
        inlat = nn(xfull[rows, 0:D], whole_bank()).astype(BF)
        gate_grads = []
        ilg_total = jnp.zeros((CHUNK, PAD), F32)
        for e in range(2):
            spot = 64 + 2 * c + e
            gate = jnp.sum(
                jnp.where((lane == spot) | (lane == spot + RANK), extras, 0.0),
                axis=1, keepdims=True,
            )

            for f in range(FF // TILE):
                fs = slice(f * TILE, f * TILE + TILE)
                x = xfull[rows, 0:D]
                g = nn(x, win[e, 0, :, fs]) + nn(inlat, upin[2 * e, :, fs])
                u = nn(x, win[e, 1, :, fs]) + nn(inlat, upin[2 * e + 1, :, fs])
                sg = 1.0 / (1.0 + jnp.exp(-g))
                silu = g * sg
                act[:, fs] = silu
                a1[:, fs] = u * sg * (1.0 + g * (1.0 - sg))
                hid[:, fs] = (silu * u).astype(BF)

            if e == 0:

                @pl.when(j == 0)
                def _():
                    weights_here(1)

            dl = nn(hid[...], ad[e]).astype(BF)

            gsum = jnp.zeros((CHUNK, 1), F32)
            for d in range(D // TILE):
                ds = slice(d * TILE, d * TILE + TILE)
                ev = nn(hid[...], wd[e, :, ds]) + nt(dl, bank(d * TILE))
                halves = [cbuf[slot, 2 * d + m] for m in range(TILE // W)]
                ct = jnp.concatenate(halves, axis=1).astype(F32)
                vg[:, ds] = (ct * gate).astype(BF)
                total = mix[:, ds] + ev * gate
                if e == 0:
                    mix[:, ds] = total
                else:
                    for t in range(2):
                        for m in range(TILE // W):
                            mixed[2 * d + m, span(source(j, t) * T, T), :] = total[
                                T * t : T * t + T, W * m : W * m + W
                            ].astype(BF)
                gsum += jnp.sum(ev * ct, axis=1, keepdims=True)
            gate_grads.append(gsum)
            low = 80 + RANK * e
            dlg = jnp.where(
                (lane >= low) & (lane < low + RANK), nn(vg[...], whole_bank()), 0.0
            ).astype(BF)

            for f in range(FF // TILE):
                fs = slice(f * TILE, f * TILE + TILE)
                hg = nt(vg[...], wd[e, fs, :]) + nt(dlg, ad[e, fs, :])
                gg[:, fs] = (hg * a1[:, fs]).astype(BF)
                ug[:, fs] = (hg * act[:, fs]).astype(BF)

            ilg_total += nt(gg[...], upin[2 * e]) + nt(ug[...], upin[2 * e + 1])
            ilg = ilg_total.astype(BF)

            for d in range(D // TILE):
                ds = slice(d * TILE, d * TILE + TILE)
                t = nt(gg[...], win[e, 0, ds, :]) + nt(ug[...], win[e, 1, ds, :])
                if e == 0:
                    xacc[:, ds] = t
                else:
                    t += nt(ilg, bank(d * TILE))
                    obuf[rows, ds] = (xacc[:, ds] + t).astype(BF)

            for n, grad in ((2 * e, gg), (2 * e + 1, ug)):
                aup[n] += tn(inlat, grad[...])[RANK * n : RANK * n + RANK, :]
            alow[e] += tn(dlg, hid[...])[low : low + RANK, :]
            alift[e] += tn(dl, vg[...])[low : low + RANK, :]
        adown[...] += tn(ilg_total.astype(BF), xfull[rows, 0:D])[0 : 4 * RANK, :]
        obuf[rows, D : D + PAD] = jnp.where(
            lane == 64 + 2 * c, gate_grads[0], jnp.where(lane == 65 + 2 * c, gate_grads[1], 0.0)
        ).astype(BF)
        for step in range(4):

            @pl.when(j == step)
            def _():
                for t in range(2):
                    n = 2 * ((step + STEPS[0]) % 4) + t
                    if n:
                        back_to(n).start()

        return carry

    def back_to(n):
        rel = PLACES[n]
        seen = PLACES.index(((4 - rel[0]) % 4, rel[1]))
        return to_peer(
            obuf.at[pl.ds(T * n, T)], rbuf.at[seen], send2.at[n], recv2.at[seen], place(rel)
        )

    lax.fori_loop(0, 4, chunk, 0)
    keep = [
        pltpu.make_async_copy(
            xfull.at[pl.ds(T * n, T)], xout.at[span(sources[n] * T, T)], xsem.at[n]
        )
        for n in range(PEERS)
    ]
    for copy in keep:
        copy.start()
    gup[...] = aup[...].astype(BF)
    glow[...] = alow[...].astype(BF)
    glift[...] = alift[...].astype(BF)
    gdown[...] = adown[...].astype(BF)
    ring.sent()
    for n in range(1, PEERS):
        back_to(n).wait_send()
        to_peer(
            obuf.at[pl.ds(T * n, T)], rbuf.at[n], send2.at[n], recv2.at[n], place(PLACES[n])
        ).wait_recv()
    for copy in keep:
        copy.wait()

    @pl.loop(0, T // 32)
    def _(i):
        at = span(i * 32, 32)
        total = obuf[at, :].astype(F32)
        for n in range(1, PEERS):
            total += rbuf[n, at, :].astype(F32)
        summed[at, :] = total


def experts(pay, branch, cot, bank, upin, ad, pin, pout, ein, eout):
    sems = pltpu.SemaphoreType.DMA
    return pl.pallas_call(
        expert_kernel,
        out_shape=(
            jax.ShapeDtypeStruct((PEERS, S, W), BF),
            jax.ShapeDtypeStruct((T, D + PAD), F32),
            jax.ShapeDtypeStruct((S, D + PAD), BF),
            jax.ShapeDtypeStruct((4, RANK, FF), BF),
            jax.ShapeDtypeStruct((2, RANK, FF), BF),
            jax.ShapeDtypeStruct((2, RANK, D), BF),
            jax.ShapeDtypeStruct((4 * RANK, D), BF),
        ),
        in_specs=[VMEM, VMEM, ANY, VMEM, VMEM, VMEM] + [ANY] * 25,
        out_specs=(VMEM, VMEM, ANY, VMEM, VMEM, VMEM, VMEM),
        scratch_shapes=[
            pltpu.VMEM((S, D + PAD), BF),
            pltpu.VMEM((2, 2, D, FF), BF),
            pltpu.VMEM((2, FF, D), BF),
            pltpu.VMEM((2, PEERS, CHUNK, W), BF),
            pltpu.VMEM((S, D + PAD), BF),
            pltpu.VMEM((PEERS, T, D + PAD), BF),
            pltpu.VMEM((CHUNK, FF), F32),
            pltpu.VMEM((CHUNK, FF), F32),
            pltpu.VMEM((CHUNK, FF), BF),
            pltpu.VMEM((CHUNK, D), BF),
            pltpu.VMEM((CHUNK, FF), BF),
            pltpu.VMEM((CHUNK, FF), BF),
            pltpu.VMEM((CHUNK, D), F32),
            pltpu.VMEM((CHUNK, D), F32),
            pltpu.VMEM((4, RANK, FF), F32),
            pltpu.VMEM((2, RANK, FF), F32),
            pltpu.VMEM((2, RANK, D), F32),
            pltpu.VMEM((4 * RANK, D), F32),
            sems((16,)), sems((16,)), sems((16,)), sems((4,)),
            sems((9,)), sems((9,)), sems((PEERS,)), sems((PEERS,)), sems((PEERS,)),
            pltpu.VMEM((16, T, PAD), BF), sems((16,)), sems((16,)), sems((16,)),
        ],
        compiler_params=params(3, 63),
        cost_estimate=pl.CostEstimate(flops=10**11, bytes_accessed=10**7, transcendentals=0),
        name="experts",
    )(pay, branch, cot, bank, upin, ad, *pin, *pout, *ein, *eout)


HALVES = (slice(0, S // 2), slice(S // 2, S))


class Scatter:
    def __init__(self, parts, passing, near, last, send, recv):
        self.parts, self.passing, self.near, self.last = parts, passing, near, last
        self.send, self.recv = send, recv

    def piece(self, rel, half):
        return self.parts.at[PLACES.index(rel), HALVES[half]]

    def copy(self, kind, y, half):
        up, down = (1, 0), (3, 0)
        if kind == "far":
            to, src, dst = (up, down)[half], self.piece((2, y), half), self.passing.at[half, y]
        elif kind == "plain":
            to, rel = ((down, (3, y)), (up, (1, y)))[half]
            src, dst = self.piece(rel, half), self.near.at[0, half, y]
        elif kind == "summed":
            to, rel = ((up, (1, y)), (down, (3, y)))[half]
            src, dst = self.piece(rel, half), self.near.at[1, half, y]
        else:
            to, src, dst = (0, 1), self.piece((0, 1), half), self.last.at[half]
        n = ("far", "plain", "summed", "plane").index(kind) * 4 + 2 * y + half
        return to_peer(src, dst, self.send.at[n], self.recv.at[n], place(to))

    def ready(self, slot):
        rel = PLACES[slot]
        if rel[0] == 2:
            for half in range(2):
                self.copy("far", rel[1], half).start()
        elif rel[0]:
            self.copy("plain", rel[1], 1 if rel[0] == 1 else 0).start()

    def add(self, rel, half, others):
        slot, at = PLACES.index(rel), HALVES[half].start

        @pl.loop(0, S // 2 // 128)
        def _(i):
            rows, there = span(i * 128, 128), pl.ds(pl.multiple_of(at + i * 128, 128), 128)
            total = self.parts[slot, there, :].astype(F32)
            for other in others:
                total += other[rows, :].astype(F32)
            self.parts[slot, there, :] = total.astype(BF)

    def middle(self):
        for y in (1, 0):
            for half in range(2):
                self.copy("far", y, half).wait_recv()
                rel = ((1, y), (3, y))[half]
                self.add(rel, half, [self.passing.at[half, y]])
                self.copy("summed", y, half).start()

    def other_plane(self):
        for half in range(2):
            self.copy("plain", 1, half).wait_recv()
            self.copy("summed", 1, half).wait_recv()
            self.add((0, 1), half, [self.near.at[k, half, 1] for k in range(2)])
            self.copy("plane", 0, half).start()

    def end(self):
        for half in range(2):
            self.copy("plain", 0, half).wait_recv()
            self.copy("summed", 0, half).wait_recv()
            self.copy("plane", 0, half).wait_recv()

    def arrived(self, half, rows):
        kept = [self.near[k, half, 0, rows, :].astype(F32) for k in range(2)]
        return kept[0] + kept[1] + self.last[half, rows, :].astype(F32)

    def sent(self):
        for kind in ("far", "plain", "summed"):
            for y in range(2):
                for half in range(2):
                    self.copy(kind, y, half).wait_send()
        for half in range(2):
            self.copy("plane", 0, half).wait_send()


def back_kernel(
    summed, state, prob, routes, bank, ru, gain, cot, mine, other, extra, lat_o,
    q, k_, v, att, cols, qraw, kraw, qgain, kgain, cosine, sine, up, lat, xfull_in, normed_in, flat_in,
    pg, bgc, stat3, lcg, gqkvup, goutdown, goutup, grup, growdown, flat,
    wo, sem, bg, sbuf, abuf, dq, dk, dv, stat, inbox, ex,
    send1, recv1, send2, recv2, send3, recv3, xfull, normed, fsem, cot_t, *sems,
):
    c = lax.axis_index("col")
    barrier = greet()
    greet_row(barrier, PLANE, UP, DOWN)
    greet_partner(barrier)
    rows_in = RowGather(flat_in, flat, 6 * RANK, sems)
    loads = load_out(mine, other, wo, sem)
    for load in loads:
        load.start()
    fetches = [
        pltpu.make_async_copy(xfull_in, xfull, fsem.at[0]),
        pltpu.make_async_copy(normed_in, normed, fsem.at[1]),
    ]
    own = pltpu.make_async_copy(cot.at[:, span(c * T, T), :], cot_t, fsem.at[2])
    own.start()
    for copy in fetches:
        copy.start()
    lane = lanes(T)
    p_ = prob[...]
    gg = jnp.where(member_of(routes, T), summed[:, D : D + PAD], 0.0)
    lgrad = (p_ * (gg - jnp.sum(p_ * gg, axis=1, keepdims=True))).astype(BF)
    rlg = nt(lgrad, ru[...]).astype(BF)
    both = jnp.where(lane < 64, rlg.astype(F32), lgrad.astype(F32)).astype(BF)
    total = jnp.zeros((T, 1), F32)
    for p in range(PEERS):
        feats = slice(W * p, W * p + W)
        st = state[:, feats]
        total += jnp.sum(st * st, axis=1, keepdims=True)
    r = lax.rsqrt(total / D + EPS)
    mean = jnp.zeros((T, 1), F32)
    for p in range(PEERS):
        feats = slice(W * p, W * p + W)
        m = (summed[:, feats] + nt(both, bank[feats, 0:PAD])) * gain[:, feats]
        mean += jnp.sum(state[:, feats] * m, axis=1, keepdims=True)
    mean = mean / D
    olg = jnp.zeros((T, PAD), F32)
    own.wait()
    for p in range(PEERS):
        feats = slice(W * p, W * p + W)
        m = (summed[:, feats] + nt(both, bank[feats, 0:PAD])) * gain[:, feats]
        st = state[:, feats]
        grad = (cot_t[p].astype(F32) + r * m - st * (r * r * r) * mean).astype(BF)
        bg[p] = grad
        olg += nt(grad, extra[p])
    olg = jnp.where((lane >= RANK) & (lane < 2 * RANK), olg, 0.0)
    moved = pltpu.roll(olg, PAD - RANK, 1).astype(BF)
    info = jnp.where(
        lane < RANK, lat_o[...], jnp.where(lane < 2 * RANK, olg, both.astype(F32))
    ).astype(BF)
    x = jnp.concatenate([bg[p] for p in range(PEERS)], axis=1)
    for load in loads:
        load.wait()
    pl.semaphore_wait(barrier, PEERS - 1 + 4)
    rows_in.start()
    for n in (4, 3, 5, 2, 6, 1, 7, 0):
        d = peer_of(n)
        part = nn(x, wo[:, span(d * W, W)]) + nn(moved, extra[d])
        sbuf[d, :, 0:W] = part.astype(BF)
        sbuf[d, :, W : W + PAD] = info
        if n:
            to_peer(sbuf.at[d], abuf.at[c], send1.at[n], recv1.at[n], d).start()
        else:
            abuf[c] = sbuf[c]
            bgc[c] = bg[c]
    for n in ORDER:
        d = peer_of(n)
        to_peer(sbuf.at[d], abuf.at[source_of(n)], send1.at[n], recv1.at[n], d).wait()
    for n in ORDER:
        d = peer_of(n)
        to_peer(bg.at[d], bgc.at[c], send2.at[n], recv2.at[n], d).start()
    rows_in.step(0)
    rows_in.step(1)
    for p in range(PEERS):
        ex[T * p : T * p + T, :] = abuf[p, :, W : W + PAD]

    blocks = 4
    size = S // blocks
    for h in range(2):
        feats = slice(HEAD * h, HEAD * h + HEAD)
        for i in reversed(range(blocks)):
            rows = slice(i * size, (i + 1) * size)
            seen = (i + 1) * size
            allowed = lax.broadcasted_iota(jnp.int32, (size, seen), 1) <= (
                lax.broadcasted_iota(jnp.int32, (size, seen), 0) + i * size
            )
            g = jnp.concatenate([abuf[2 * i, :, feats], abuf[2 * i + 1, :, feats]], axis=0)
            qb = q[rows, feats]
            kb = k_[0:seen, feats]
            score = nt(qb, kb) * FACTOR
            full = jnp.where(allowed, jnp.exp(score - cols[rows, 2 + h : 3 + h]), 0.0)
            wgrad = nt(g, v[0:seen, feats])
            center = jnp.sum(full * wgrad, axis=1, keepdims=True)
            sgrad = (full * (wgrad - center)).astype(BF)
            dq[rows, feats] = nn(sgrad, kb) * FACTOR
            dvp = tn(full.astype(BF), g)
            dkp = tn(sgrad, qb) * FACTOR
            if i == blocks - 1:
                dv[0:seen, feats] = dvp
                dk[0:seen, feats] = dkp
            else:
                dv[0:seen, feats] += dvp
                dk[0:seen, feats] += dkp
    for i in range(blocks):
        rows = slice(i * size, (i + 1) * size)
        dots = []
        for raw, gain_, grads in ((qraw, qgain, dq), (kraw, kgain, dk)):
            dot = jnp.zeros((size, 1), F32)
            for h in range(2):
                feats = slice(HEAD * h, HEAD * h + HEAD)
                y = grads[rows, feats]
                y = y * cosine[rows, :] - pltpu.roll(y, HEAD // 2, 1) * sine[rows, :]
                y = y * gain_[:, feats]
                grads[rows, feats] = y
                dot += jnp.sum(y * raw[rows, feats], axis=1, keepdims=True)
            dots.append(dot)
        stat[:, rows] = columns_to_rows(*dots)
    swap_start(stat, inbox, send3, recv3)
    rows_in.step(2)
    for copy in fetches:
        copy.wait()
    goutdown[...] = tn(ex[...], att[...])[RANK : 2 * RANK, :].astype(BF)
    grup[...] = tn(xfull[:, D : D + PAD], ex[...])[48:64, :].astype(BF)
    growdown[3 * RANK : 4 * RANK, :] = tn(ex[...], xfull[:, 0:D])[48:64, :].astype(BF)
    dots = swap_finish(stat, inbox, send3, recv3)
    wide = lanes(size)
    for i in range(blocks):
        rows = slice(i * size, (i + 1) * size)
        column = rows_to_columns(dots[:, rows])
        stat_sum = jnp.zeros((size, 1), F32)
        code = jnp.zeros((size, PAD), F32)
        for n, (raw, grads) in enumerate(((qraw, dq), (kraw, dk))):
            rs = cols[rows, n : n + 1]
            x = raw[rows, :]
            y = rs * grads[rows, :] - x * (rs * rs * rs * column[:, n : n + 1] / D)
            y = y.astype(BF)
            pg[rows, W * n : W * n + W] = y
            stat_sum += jnp.sum(y.astype(F32) * x, axis=1, keepdims=True)
            code += nt(y, up[:, W * n : W * n + W])
        y = dv[rows, :].astype(BF)
        pg[rows, 2 * W : 3 * W] = y
        stat_sum += jnp.sum(y.astype(F32) * v[rows, :].astype(F32), axis=1, keepdims=True)
        code += nt(y, up[:, 2 * W : 3 * W])
        lcg[rows, :] = jnp.where(wide < 3 * RANK, code, 0.0).astype(BF)
        stat3[:, rows] = columns_to_rows(stat_sum, stat_sum)
    for n in range(3):
        gqkvup[n] = tn(lat[...], pg[:, W * n : W * n + W])[RANK * n : RANK * n + RANK, :].astype(BF)
    growdown[0 : 3 * RANK, :] = tn(lcg[...], normed[...])[0 : 3 * RANK, :].astype(BF)
    for n in ORDER:
        d = peer_of(n)
        to_peer(bg.at[d], bgc.at[source_of(n)], send2.at[n], recv2.at[n], d).wait()
    acc = jnp.zeros((PAD, W), F32)
    for p in range(PEERS):
        acc += tn(ex[T * p : T * p + T, :], bgc[p])
    goutup[...] = acc[0:RANK, :].astype(BF)
    rows_in.step(3)
    rows_in.finish()


def back(*args):
    sems = pltpu.SemaphoreType.DMA((PEERS,))
    kinds = [VMEM] * len(args)
    kinds[8] = ANY
    kinds[9] = ANY
    kinds[25] = ANY
    kinds[26] = ANY
    kinds[27] = ANY
    kinds[7] = ANY
    return pl.pallas_call(
        back_kernel,
        out_shape=(
            jax.ShapeDtypeStruct((S, 3 * W), BF),
            jax.ShapeDtypeStruct((PEERS, T, W), BF),
            jax.ShapeDtypeStruct((8, S), F32),
            jax.ShapeDtypeStruct((S, PAD), BF),
            jax.ShapeDtypeStruct((3, RANK, W), BF),
            jax.ShapeDtypeStruct((RANK, W), BF),
            jax.ShapeDtypeStruct((RANK, W), BF),
            jax.ShapeDtypeStruct((RANK, PAD), BF),
            jax.ShapeDtypeStruct((4 * RANK, D), BF),
            jax.ShapeDtypeStruct((16, 6 * RANK, FF), BF),
        ),
        in_specs=kinds,
        out_specs=(VMEM,) * 9 + (ANY,),
        scratch_shapes=[
            pltpu.VMEM((D, D), BF),
            pltpu.SemaphoreType.DMA((2 * PEERS,)),
            pltpu.VMEM((PEERS, T, W), BF),
            pltpu.VMEM((PEERS, T, W + PAD), BF),
            pltpu.VMEM((PEERS, T, W + PAD), BF),
            pltpu.VMEM((S, W), F32),
            pltpu.VMEM((S, W), F32),
            pltpu.VMEM((S, W), F32),
            pltpu.VMEM((8, S), F32),
            pltpu.VMEM((PEERS, 8, S), F32),
            pltpu.VMEM((S, PAD), BF),
            sems, sems, sems, sems, sems, sems,
            pltpu.VMEM((S, D + PAD), BF),
            pltpu.VMEM((S, D), BF),
            pltpu.SemaphoreType.DMA((3,)),
            pltpu.VMEM((PEERS, T, W), BF),
            *row_sems(),
        ],
        compiler_params=params(4, 63),
        cost_estimate=pl.CostEstimate(flops=4 * 10**10, bytes_accessed=10**7, transcendentals=0),
        name="back",
    )(*args)


GROUPS = 10


def input_kernel(
    pg, lcg, wq, bank, stat3, bgc, tokens, rinv, gain,
    picked, gdown, glift, growdown, gqkvup, goutdown, goutup, grup,
    out, gin, glif, grout, gqkvdown, gqkvup_all, gout, goutup_all, grup_all,
    w, wsem, own, sbuf, passing, near, last, inbox,
    tall, thin, tallbuf, thinbuf, tallsum, thinsum, mine, theirs,
    send, recv, send3, recv3, send4, recv4, send5, recv5, send6, recv6,
):
    c = lax.axis_index("col")
    r = lax.axis_index("row")
    barrier = greet()
    for n in range(1, 16):
        pl.semaphore_signal(
            barrier, inc=1, device_id={"row": lax.rem(r + n, 16)}, device_id_type=MESH
        )
    loads = [
        pltpu.make_async_copy(
            wq.at[:, T * k : T * k + T, :], w.at[:, :, W * k : W * k + W], wsem.at[k]
        )
        for k in range(3)
    ]
    for load in loads:
        load.start()
    for p in range(16):
        at = slice(T * p, T * p + T)
        tall[p, 0 : 4 * RANK, :] = gdown[:, at]
        tall[p, 4 * RANK : 6 * RANK, :] = glift[:, at]
        tall[p, 6 * RANK : 10 * RANK, :] = growdown[:, at]
    thin[0 : 3 * RANK, :] = gqkvup[...]
    thin[3 * RANK : 4 * RANK, :] = goutdown[...]
    thin[4 * RANK : 5 * RANK, :] = goutup[...]
    thin[5 * RANK : 6 * RANK, 0:PAD] = grup[...]
    thin[5 * RANK : 6 * RANK, PAD:W] = jnp.zeros((RANK, PAD), BF)
    for load in loads:
        load.wait()
    pl.semaphore_wait(barrier, PEERS - 1 + 15)

    def row_copies(n):
        p = lax.rem(r + n, 16)
        where = {"row": p}
        return [
            pltpu.make_async_remote_copy(
                src_ref=tall.at[p], dst_ref=tallbuf.at[r],
                send_sem=send4.at[n], recv_sem=recv4.at[n],
                device_id=where, device_id_type=MESH,
            ),
            pltpu.make_async_remote_copy(
                src_ref=thin, dst_ref=thinbuf.at[r], send_sem=send5.at[n], recv_sem=recv5.at[n],
                device_id=where, device_id_type=MESH,
            ),
        ]

    def row_arrivals(n):
        p = lax.rem(r + 16 - n, 16)
        where = {"row": p}
        return [
            pltpu.make_async_remote_copy(
                src_ref=tallbuf.at[p], dst_ref=tallbuf.at[p],
                send_sem=send4.at[n], recv_sem=recv4.at[n],
                device_id=where, device_id_type=MESH,
            ),
            pltpu.make_async_remote_copy(
                src_ref=thin, dst_ref=thinbuf.at[p], send_sem=send5.at[n], recv_sem=recv5.at[n],
                device_id=where, device_id_type=MESH,
            ),
        ]

    for n in range(1, 16):
        for copy in row_copies(n):
            copy.start()
    tallbuf[r] = tall[r]
    thinbuf[r] = thin[...]
    swap_start(stat3, inbox, send3, recv3)
    ring = Scatter(sbuf, passing, near, last, send, recv)
    for slot in (7, 6, 4, 5, 2, 3, 1, 0):
        d = place(PLACES[slot])
        wide = span(d * W, W)
        for i in range(2):
            rows = slice(512 * i, 512 * i + 512)
            part = nt(lcg[rows, :], bank[wide, 0:PAD])
            part += nt(pg[rows, :], w[pl.ds(2 * d, 2)].reshape(W, 3 * W))
            if slot:
                sbuf[slot, rows, :] = part.astype(BF)
            else:
                own[rows, :] = part
        ring.ready(slot)
    for n in range(1, 16):
        for copy in row_arrivals(n):
            copy.wait_recv()
    ring.middle()

    def summed(s, shape, read):
        return lax.fori_loop(
            0, 16, lambda q, acc: acc + picked[s, q] * read(q).astype(F32), jnp.zeros(shape, F32)
        )

    @pl.loop(0, SETS)
    def _(s):
        at = span(s * RANK, RANK)
        total = summed(s, (GROUPS * RANK, T), lambda q: tallbuf[q])
        for g in range(GROUPS):
            tallsum[g, at, :] = total[RANK * g : RANK * g + RANK, :]

    mine[...] = tallsum[6:9].astype(BF)
    theirs[c] = mine[...]
    for k in ORDER:
        to_peer(mine, theirs.at[c], send6.at[k], recv6.at[k], peer_of(k)).start()
    ring.other_plane()

    @pl.loop(0, SETS)
    def _(s):
        at = span(s * RANK, RANK)
        total = summed(s, (6 * RANK, W), lambda q: thinbuf[q])
        for g in range(6):
            thinsum[g, at, :] = total[RANK * g : RANK * g + RANK, :]

    for g in range(4):
        gin[g] = jnp.transpose(tallsum[g])
    for g in range(2):
        glif[g] = tallsum[4 + g]
    grout[...] = jnp.transpose(tallsum[9])
    for k in range(3):
        gqkvup_all[k] = thinsum[k]
    for m in range(2):
        gout[PAD * m : PAD * m + PAD, :] = jnp.transpose(thinsum[3, :, PAD * m : PAD * m + PAD])
    goutup_all[...] = thinsum[4]
    grup_all[...] = thinsum[5, :, 0:PAD]
    for k in ORDER:
        to_peer(mine, theirs.at[source_of(k)], send6.at[k], recv6.at[k], peer_of(k)).wait()
    for k in range(3):
        total = theirs[0, k].astype(F32)
        for p in range(1, PEERS):
            total += theirs[p, k].astype(F32)
        gqkvdown[k] = jnp.transpose(total)
    for n in range(1, 16):
        for copy in row_copies(n):
            copy.wait_send()
    dots = swap_finish(stat3, inbox, send3, recv3)
    ring.end()
    ring.sent()
    for i in range(4):
        rows = slice(256 * i, 256 * i + 256)
        column = rows_to_columns(dots[:, rows])[:, 0:1]
        total = own[rows, :] + ring.arrived(i // 2, slice(256 * (i % 2), 256 * (i % 2) + 256))
        q = rinv[rows, 0:1]
        grad = bgc[rows, :].astype(F32) + q * (total * gain[...])
        out[rows, :] = grad - tokens[rows, :].astype(F32) * (q * q * column / D)


def to_input(*args):
    sems = pltpu.SemaphoreType.DMA((PEERS,))
    more = pltpu.SemaphoreType.DMA((16,))
    kinds = [VMEM] * len(args)
    kinds[2] = ANY
    kinds[9] = pl.BlockSpec(memory_space=pltpu.SMEM)
    square = (PAD, PAD)
    return pl.pallas_call(
        input_kernel,
        out_shape=tuple(
            jax.ShapeDtypeStruct(shape, F32)
            for shape in (
                (S, W), (4, *square), (2, *square), square, (3, *square), (3, PAD, W), (W, PAD),
                (PAD, W), square,
            )
        ),
        in_specs=kinds,
        out_specs=(VMEM,) * 9,
        scratch_shapes=[
            pltpu.VMEM((16, T, 3 * W), BF),
            pltpu.SemaphoreType.DMA((3,)),
            pltpu.VMEM((S, W), F32),
            pltpu.VMEM((PEERS, S, W), BF),
            pltpu.VMEM((2, 2, S // 2, W), BF),
            pltpu.VMEM((2, 2, 2, S // 2, W), BF),
            pltpu.VMEM((2, S // 2, W), BF),
            pltpu.VMEM((PEERS, 8, S), F32),
            pltpu.VMEM((16, GROUPS * RANK, T), BF),
            pltpu.VMEM((6 * RANK, W), BF),
            pltpu.VMEM((16, GROUPS * RANK, T), BF),
            pltpu.VMEM((16, 6 * RANK, W), BF),
            pltpu.VMEM((GROUPS, *square), F32),
            pltpu.VMEM((6, PAD, W), F32),
            pltpu.VMEM((3, *square), BF),
            pltpu.VMEM((PEERS, 3, *square), BF),
            more, more, sems, sems, more, more, more, more, sems, sems,
        ],
        compiler_params=params(5, 63),
        cost_estimate=pl.CostEstimate(flops=5 * 10**10, bytes_accessed=10**7, transcendentals=0),
        name="input",
    )(*args)


def sums_kernel(sets, flat, ginup, glower, low):
    ginup[...] = jnp.zeros_like(ginup)
    low[...] = jnp.zeros_like(low)

    @pl.loop(0, 16)
    def _(q):
        at = span(sets[q] * RANK, RANK)
        for g in range(4):
            ginup[g, at, :] += flat[q, RANK * g : RANK * g + RANK, :].astype(F32)
        for g in range(2):
            low[g, at, :] += flat[q, RANK * (4 + g) : RANK * (5 + g), :].astype(F32)

    for g in range(2):
        for m in range(FF // PAD):
            glower[g, PAD * m : PAD * m + PAD, :] = jnp.transpose(low[g, :, PAD * m : PAD * m + PAD])


def sums(sets, flat):
    return pl.pallas_call(
        sums_kernel,
        out_shape=(
            jax.ShapeDtypeStruct((4, PAD, FF), F32), jax.ShapeDtypeStruct((2, FF, PAD), F32),
        ),
        in_specs=[pl.BlockSpec(memory_space=pltpu.SMEM), VMEM],
        out_specs=(VMEM, VMEM),
        scratch_shapes=[pltpu.VMEM((2, PAD, FF), F32)],
        compiler_params=params(None, 63),
        cost_estimate=pl.CostEstimate(flops=10**9, bytes_accessed=10**7, transcendentals=0),
        name="sums",
    )(sets, flat)


def rope_tables():
    half = HEAD // 2
    frequency = (10000.0 ** (-(np.arange(half, dtype=np.float32) * 2.0) / HEAD)).astype(np.float32)
    angle = np.arange(S, dtype=np.float32)[:, None] * frequency[None, :]
    cosine, sine = np.cos(angle), np.sin(angle)
    return (
        np.concatenate([cosine, cosine], axis=1).astype(np.float32),
        np.concatenate([-sine, sine], axis=1).astype(np.float32),
    )


def body(
    tokens, cotangent, routes, adapter_set, attn_gain, mixer_gain, query_gain, key_gain,
    qkv_weight, qkv_down, qkv_up, out_weight, out_down, out_up,
    router_weight, router_down, router_up,
    expert_in, expert_in_down, expert_in_up, expert_out, expert_out_down, expert_out_up,
):
    c = lax.axis_index("col")
    start = adapter_set[0] * RANK

    out_up_pick = lax.dynamic_slice_in_dim(out_up, start, RANK, 0)
    out_down_pick = lax.dynamic_slice_in_dim(out_down, start, RANK, 1)
    pay0 = jnp.concatenate([tokens, out_down_pick.T, out_up_pick], axis=0)

    flag = jnp.broadcast_to(adapter_set.astype(BF)[:, None], (T, PAD))
    shard = jnp.concatenate(
        [
            qkv_weight.reshape(3 * T, W),
            jnp.concatenate([qkv_down[0], qkv_down[1]], axis=1),
            jnp.concatenate([qkv_down[2], router_down], axis=1),
            jnp.concatenate([jnp.pad(router_weight, ((0, 0), (64, 48))), flag], axis=1),
            out_weight.T,
        ],
        axis=0,
    )
    normed, rinv, resid, extra, cot, po, pl0, pr0, xl, xr, xf, xo, wq = gather_tokens(
        pay0, attn_gain[None], cotangent, expert_in, expert_out, shard
    )
    sets = wq[:, 5 * T, PAD].astype(F32)
    picked = (sets[None, :] == jnp.arange(SETS, dtype=F32)[:, None]).astype(F32)
    spot = jnp.arange(PAD, dtype=jnp.int32)
    rank = spot[None, :, None] - start
    picks = (
        (rank >= 0) & (rank < RANK)
        & (rank + RANK * jnp.arange(4, dtype=jnp.int32)[:, None, None] == spot[None, None, :])
    ).astype(BF)

    down = jnp.concatenate(
        [
            jnp.moveaxis(expert_out_up, 2, 0),
            jnp.moveaxis(expert_in_down.reshape(4, T, PAD), 0, 1),
        ],
        axis=1,
    ).reshape(T, 6, SETS, RANK)
    down = jnp.einsum(
        "dnsj,sr->rdnj", down, picked.astype(BF), preferred_element_type=F32
    ).astype(BF).reshape(16, T, 6 * RANK)
    ebank = jnp.concatenate(
        [
            down[:, :, 2 * RANK :], jnp.zeros((16, T, 16), BF), down[:, :, : 2 * RANK],
            jnp.zeros((16, T, 16), BF),
        ],
        axis=2,
    )

    qkv_up_pick = lax.dynamic_slice_in_dim(qkv_up, start, RANK, 1)
    up = jnp.concatenate(
        [jnp.pad(qkv_up_pick[k], ((RANK * k, PAD - RANK * k - RANK), (0, 0))) for k in range(3)],
        axis=1,
    )
    in_up_pick = lax.dynamic_slice_in_dim(expert_in_up, start, RANK, 2).reshape(4, RANK, FF)
    upin = jnp.stack(
        [jnp.pad(in_up_pick[n], ((RANK * n, PAD - RANK * n - RANK), (0, 0))) for n in range(4)]
    )
    lower_pick = lax.dynamic_slice_in_dim(expert_out_down, start, RANK, 2)
    ad = jnp.stack(
        [jnp.pad(lower_pick[e], ((0, 0), (80 + RANK * e, 32 - RANK * e))) for e in range(2)]
    )
    ru = jnp.pad(lax.dynamic_slice_in_dim(router_up, start, RANK, 0), ((48, 64), (64, 48)))
    routes_t = lax.dynamic_slice_in_dim(routes, c * T, T, 0)
    cosine, sine = rope_tables()

    qg, kg = query_gain[None], key_gain[None]
    (
        att_t, att, q, k, v, qraw, kraw, cols, lat, bank, half, other,
        pl1, pr1, pf0, pf1, yl, yr, yf, *swapped,
    ) = attention(
        normed, wq, picks, up, qg, kg, cosine, sine,
        (expert_in, po, pl0, pr0), (expert_out, xo, xl, xr, xf),
    )
    pin = [expert_in, po, pl0, pl1, pr0, pr1, pf0, pf1]
    pout = [expert_out, xo, xl, yl, xr, yr, xf, yf]
    half, other = half.reshape(PEERS, S, W), other.reshape(PEERS, S, W)
    pay, state, prob, branch, lat_o = to_state(
        att_t, half, other, resid, extra, mixer_gain[None], bank, ru, routes_t
    )
    mixture, summed, xfull, gup, glow, glift, gdown = experts(
        pay, branch, cot, ebank, upin, ad, pin, pout, swapped[:4], swapped[4:]
    )
    mixture = lax.psum_scatter(mixture.reshape(PEERS * S, W), "col", scatter_dimension=0, tiled=True)
    flat = jnp.concatenate([gup.reshape(4 * RANK, FF), glow.reshape(2 * RANK, FF)], axis=0)

    pg, bgc, stat3, lcg, gqkvup, goutdown, goutup, grup, gtall, flat = back(
        summed, state, prob, routes_t, bank, ru, mixer_gain[None], cot, half, other, extra,
        lat_o, q, k, v, att, cols, qraw, kraw, qg, kg, cosine, sine, up, lat, xfull, normed,
        flat,
    )
    pg, mixture = lax.optimization_barrier((pg, mixture))
    mixed = (tokens.astype(F32) + mixture.astype(F32)).astype(BF)
    gain_mine = lax.dynamic_slice_in_dim(attn_gain, c * W, W, 0)[None]
    (
        tokens_grad, in_down_grad, lift_grad, router_down_grad, qkv_down_grad, qkv_up_grad,
        out_down_grad, out_up_grad, router_up_grad,
    ) = to_input(
        pg, lcg, wq, bank, stat3, bgc.reshape(S, W), tokens, rinv, gain_mine,
        picked, gdown, glift.reshape(2 * RANK, D), gtall, gqkvup.reshape(3 * RANK, W),
        goutdown, goutup, grup,
    )
    in_up_grad, lower_grad = sums(sets.astype(jnp.int32), flat)
    in_down_grad = in_down_grad.reshape(2, 2, T, PAD)
    in_up_grad = in_up_grad.reshape(2, 2, PAD, FF)
    router_up_grad = router_up_grad[:, 64:80]
    return (
        mixed, tokens_grad, qkv_down_grad, qkv_up_grad, out_down_grad, out_up_grad,
        router_down_grad, router_up_grad, in_down_grad, in_up_grad, lower_grad, lift_grad,
    )


def solution(mesh):
    in_specs = (
        P("row", "col"), P("row", "col"), P("row", None), P("row"), P(), P(), P("col"), P("col"),
        P(None, "row", "col"), P(None, "row", None), P(None, None, "col"),
        P("col", "row"), P("col", None), P(None, "col"),
        P("row", None), P("row", None), P(),
        P("col", None, "row", None), P("col", None, "row", None), P("col", None, None, None),
        P("col", None, "row"), P("col", None, None), P("col", None, "row"),
    )
    out_specs = (
        P("row", "col"), P("row", "col"), P(None, "row", None), P(None, None, "col"),
        P("col", None), P(None, "col"), P("row", None), P(),
        P("col", None, "row", None), P("col", None, None, None), P("col", None, None),
        P("col", None, "row"),
    )
    return jax.shard_map(body, mesh=mesh, in_specs=in_specs, out_specs=out_specs, check_vma=False)
```
